32 devices in a mesh: dp: 4 (over y, x), wide: 2 (over core), narrow: 4 (over z).
Axes of the slice: x: 2, y: 2, z: 4, core: 2. Of those that a mesh axis runs over, the one named last changes fastest.
Arguments:
- numeric: bfloat16 [32768, 256], P(('dp', 'wide', 'narrow')), may hold values from -180 to 180
- cat_index: int32 [32768, 16], P(('dp', 'wide', 'narrow')), may hold values from 0 to 63, as said below
- cardinality: int32 [16], replicated, may hold values from 16 to 64
- emb_table: bfloat16 [1024, 16], replicated, may hold values from -6 to 6
- input_norm_gain: float32 [512], replicated, may hold values from 0.5 to 1.5
- input_norm_bias: float32 [512], replicated, may hold values from -3 to 3
- mask_logit: float32 [6, 512], replicated, may hold values from -6 to 6
- w_feat: bfloat16 [6, 3, 512, 512], P(None, None, 'narrow', 'wide'), may hold values from -0.25 to 0.25
- w_state: bfloat16 [6, 3, 512, 512], P(None, None, 'narrow', 'wide'), may hold values from -0.25 to 0.25
- gate_bias: float32 [6, 3, 512], replicated, may hold values from -3 to 3
- head_w1: bfloat16 [512, 256], replicated, may hold values from -0.25 to 0.25
- head_b1: float32 [256], replicated, may hold values from -3 to 3
- head_w2: bfloat16 [256, 10], replicated, may hold values from -0.75 to 0.75
- head_b2: float32 [10], replicated, may hold values from -3 to 3
- cotangent: bfloat16 [32768, 10], P(('dp', 'wide', 'narrow')), may hold values from -6 to 6
Outputs:
- logits: float32 [32768, 10], P(('dp', 'wide', 'narrow'))
- grad_numeric: float32 [32768, 256], P(('dp', 'wide', 'narrow'))
- grad_emb_table: float32 [1024, 16], replicated
- grad_bn_gain: float32 [512], replicated
- grad_bn_bias: float32 [512], replicated
- grad_mask_logit: float32 [6, 512], replicated
- grad_w_feat: float32 [6, 3, 512, 512], P(None, None, 'narrow', 'wide')
- grad_w_state: float32 [6, 3, 512, 512], P(None, None, 'narrow', 'wide')
- grad_gate_bias: float32 [6, 3, 512], replicated
- grad_head_w1: float32 [512, 256], replicated
- grad_head_b1: float32 [256], replicated
- grad_head_w2: float32 [256, 10], replicated
- grad_head_b2: float32 [10], replicated
The draws below stay inside these ranges and needn't reach their ends.
Inputs may be any that keep to these rules, and one draw needn't show every extreme that they name: `cat_index`: each index is below its column's cardinality.
All inputs are finite; a program needn't handle non-finite values.
Results may differ from the reference program's by a relative error of at most 0.015.
Values may be sent and summed in bfloat16 or wider, within the bound.
No kernel may reach another device: no remote copies, remote signals or barrier semaphores. Data moves between devices by JAX's collectives and lax.ppermute only.
A program may use at most 192 MiB of HBM per device.

```python
import math
from functools import partial
import jax
import jax.numpy as jnp
from jax import lax

NUM = 256
CAT = 16
EMB = 16
VOCAB = 64
HEAD_WIDTH = 256
CLASSES = 10
SECTIONS = 6
FEAT = 512
TABLE_ROWS = 1024
ROWS = 32768


def column_limits(key):
    key = jax.random.fold_in(key, 11)
    first, second = jax.random.split(key, 2)
    values = jax.random.randint(first, (CAT,), VOCAB // 4, VOCAB + 1)
    order = jax.random.permutation(second, CAT)
    values = jnp.where(order == 0, VOCAB, values)
    values = jnp.where(order == 1, VOCAB // 4, values)
    return values.astype(jnp.int32)


def draw_cardinality(key, part):
    return column_limits(key)


def draw_cat_index(key, part):
    limits = column_limits(key)
    key = jax.random.fold_in(key, 5)
    raw_values = jax.random.randint(key, (ROWS, CAT), 0, 1048576)
    return (raw_values % limits[None, :]).astype(jnp.int32)


def draw_numeric(key, part):
    key = jax.random.fold_in(key, 7)
    first, second = jax.random.split(key, 2)
    position = jnp.arange(ROWS, dtype=jnp.float32) / ROWS
    column_scale = jnp.exp(jax.random.uniform(second, (1, NUM), minval=0.0, maxval=math.log(10.0)))
    base = jnp.clip(jax.random.normal(first, (ROWS, NUM)), -6.0, 6.0)
    row_scale = jnp.exp(position * math.log(3.0))
    values = base * row_scale[:, None] * column_scale
    return values.astype(jnp.float32).astype(jnp.bfloat16)


def block_levels(stream_key, shape, cuts, least, largest):
    factor_of, own = 1.0, jax.random.fold_in(stream_key, 6)
    for dim, parts in cuts:
        steps = jnp.exp(jax.random.uniform(jax.random.fold_in(own, dim), (parts,), jnp.float32, least / len(cuts), largest / len(cuts)))
        factor_of = factor_of * jnp.repeat(steps, shape[dim] // parts).reshape([-1 if axis == dim else 1 for axis in range(len(shape))])
    return factor_of


def noise(key, extent, deviation, bound, pieces=(), kind=jnp.bfloat16):
    loudness = block_levels(key, extent, pieces, -0.22, 0.18) if pieces else 1.0
    drawn = jax.random.normal(key, extent, jnp.float32) * deviation * loudness
    return jnp.minimum(jnp.maximum(drawn, -bound), bound).astype(kind)


def setup_inputs(seed: int = 0) -> dict:
    arg_keys = jax.random.split(jax.random.key(seed), 16)
    numeric = draw_numeric(jax.random.fold_in(arg_keys[15], 71), 0)
    cat_index = draw_cat_index(jax.random.fold_in(arg_keys[15], 71), 0)
    cardinality = draw_cardinality(jax.random.fold_in(arg_keys[15], 71), 0)
    emb_table = noise(arg_keys[3], (TABLE_ROWS, EMB), 1.0, 6.0)
    input_norm_gain = jnp.clip(1.0 + 0.1 * jax.random.normal(arg_keys[4], (FEAT,), jnp.float32), 0.5, 1.5)
    input_norm_bias = noise(arg_keys[5], (FEAT,), 0.5, 3.0, (), jnp.float32)
    mask_logit = noise(arg_keys[6], (SECTIONS, FEAT), 1.5, 6.0, (), jnp.float32)
    w_feat = noise(arg_keys[7], (SECTIONS, 3, FEAT, FEAT), FEAT ** -0.5, 0.25, ((2, 4), (3, 2)))
    w_state = noise(arg_keys[8], (SECTIONS, 3, FEAT, FEAT), FEAT ** -0.5, 0.25, ((2, 4), (3, 2)))
    gate_bias = noise(arg_keys[9], (SECTIONS, 3, FEAT), 0.5, 3.0, (), jnp.float32)
    head_w1 = noise(arg_keys[10], (FEAT, HEAD_WIDTH), FEAT ** -0.5, 0.25)
    head_b1 = noise(arg_keys[11], (HEAD_WIDTH,), 0.5, 3.0, (), jnp.float32)
    head_w2 = noise(arg_keys[12], (HEAD_WIDTH, CLASSES), (HEAD_WIDTH // 4) ** -0.5, 0.75)
    head_b2 = noise(arg_keys[13], (CLASSES,), 0.5, 3.0, (), jnp.float32)
    cotangent = noise(arg_keys[14], (ROWS, CLASSES), 1.0, 6.0, ((0, 32),))
    return dict(numeric=numeric, cat_index=cat_index, cardinality=cardinality, emb_table=emb_table, input_norm_gain=input_norm_gain, input_norm_bias=input_norm_bias, mask_logit=mask_logit, w_feat=w_feat, w_state=w_state, gate_bias=gate_bias, head_w1=head_w1, head_b1=head_b1, head_w2=head_w2, head_b2=head_b2, cotangent=cotangent)


@jax.custom_vjp
def low(v):
    return lax.optimization_barrier(v.astype(jnp.bfloat16)).astype(jnp.float32)

@jax.custom_vjp
def low_back(v):
    return v

def low_keep(v):
    return (low(v), None)

def low_pass(kept, grad):
    return (grad,)

def back_keep(v):
    return (v, None)

def back_low(kept, grad):
    return (low(grad),)
low.defvjp(low_keep, low_pass)
low_back.defvjp(back_keep, back_low)
EPSILON = 1e-05

def matmul(left, right):
    return jnp.dot(left, right, precision=lax.Precision.HIGHEST)

def forward(table_row, numeric, table, input_norm_gain, input_norm_bias, mask_logit, w_feat, w_state, gate_bias, head_w1, head_b1, head_w2, head_b2):
    count_rows = numeric.shape[0]
    looked = jnp.take(table, table_row, axis=0).reshape(count_rows, -1)
    raw = jnp.concatenate([numeric, looked], axis=1)
    mean = lax.optimization_barrier(jnp.mean(raw, axis=0))
    mean_removed = raw - mean
    var = lax.optimization_barrier(jnp.mean(mean_removed * mean_removed, axis=0))
    normalized_rows = mean_removed * lax.rsqrt(var + EPSILON) * input_norm_gain + input_norm_bias
    state = normalized_rows
    for section in range(SECTIONS):
        gate_mask = jax.nn.sigmoid(mask_logit[section])
        feat_low = low(normalized_rows * gate_mask)
        state_low = low(state)
        wf = w_feat[section]
        ws = w_state[section]
        bias = gate_bias[section]
        update_pre = low_back(matmul(feat_low, wf[0]) + matmul(state_low, ws[0]) + bias[0])
        reset_pre = low_back(matmul(feat_low, wf[1]) + matmul(state_low, ws[1]) + bias[1])
        update = jax.nn.sigmoid(update_pre)
        reset = jax.nn.sigmoid(reset_pre)
        reset_low = low(reset * state)
        cand_pre = low_back(matmul(feat_low, wf[2]) + matmul(reset_low, ws[2]) + bias[2])
        candidate = jnp.tanh(cand_pre)
        state = (1.0 - update) * state + update * candidate
    head_in = low(state)
    head_pre = low_back(matmul(head_in, head_w1) + head_b1)
    act = low(jax.nn.gelu(head_pre, approximate=False))
    return matmul(act, head_w2) + head_b2

def reference(numeric, cat_index, cardinality, emb_table, input_norm_gain, input_norm_bias, mask_logit, w_feat, w_state, gate_bias, head_w1, head_b1, head_w2, head_b2, cotangent):
    offsets = (jnp.cumsum(cardinality) - cardinality).astype(jnp.int32)
    table_row = (cat_index + offsets[None, :]).astype(jnp.int32)
    logits, pullback = jax.vjp(partial(forward, table_row), numeric.astype(jnp.float32), emb_table.astype(jnp.float32), input_norm_gain, input_norm_bias, mask_logit, w_feat.astype(jnp.float32), w_state.astype(jnp.float32), gate_bias, head_w1.astype(jnp.float32), head_b1, head_w2.astype(jnp.float32), head_b2)
    grads = pullback(cotangent.astype(jnp.float32))
    return (logits, grads[0], grads[1], grads[2], grads[3], grads[4], grads[5], grads[6], grads[7], grads[8], grads[9], grads[10], grads[11])
```

```python
import functools
import jax
import jax.numpy as jnp
from jax import lax
from jax.experimental import pallas as pl
from jax.experimental.pallas import tpu as pltpu
from jax.sharding import PartitionSpec as P

EPSILON = 1e-05
BF = jnp.bfloat16
F32 = jnp.float32


def mdot(left, right):
    return lax.dot_general(left, right, (((1,), (0,)), ((), ())), preferred_element_type=F32)


def tdot(left, right):
    return lax.dot_general(left, right, (((0,), (0,)), ((), ())), preferred_element_type=F32)


def ndot(left, right):
    return lax.dot_general(left, right, (((1,), (1,)), ((), ())), preferred_element_type=F32)


def sigm(v):
    return 0.5 * jnp.tanh(0.5 * v) + 0.5


def forward_kernel(copies, n, first, place, raw, *refs):
    refs = list(refs)
    h_in = None if first else refs.pop(0)
    norm, mask, bias = refs[:3]
    pieces = refs[3 : 3 + copies.count]
    outs = refs[3 + copies.count : 3 + copies.count + 4 * n + 1]
    wbuf, sems = refs[3 + copies.count + 4 * n + 1 :]

    @pl.when(pl.program_id(0) == 0)
    def _():
        copies.run(place, pieces, wbuf, sems)

    normed = (raw[...].astype(F32) - norm[0:1, :]) * norm[1:2, :] + norm[2:3, :]
    h = normed if first else h_in[...]
    for k in range(n):
        u_out, r_out, c_out, h_out = outs[4 * k : 4 * k + 4]
        feat = (normed * sigm(mask[k : k + 1, :])).astype(BF)
        low = h.astype(BF)
        h_out[...] = low
        rpre = mdot(feat, wbuf[k, 0, 1]) + mdot(low, wbuf[k, 1, 1]) + bias[k, 1:2, :]
        r = sigm(rpre)
        upre = mdot(feat, wbuf[k, 0, 0]) + mdot(low, wbuf[k, 1, 0]) + bias[k, 0:1, :]
        u = sigm(upre)
        reset = (r * h).astype(BF)
        cpre = mdot(feat, wbuf[k, 0, 2]) + mdot(reset, wbuf[k, 1, 2]) + bias[k, 2:3, :]
        c = jnp.tanh(cpre)
        h = h + u * (c - h)
        u_out[...] = u.astype(BF)
        r_out[...] = r.astype(BF)
        c_out[...] = c.astype(BF)
    outs[4 * n][...] = h


def forward_sections(copies, n, place, raw, h, norm, mask, bias, pieces, rb):
    rows, feat = raw.shape
    first = h is None
    row = lambda dt: pl.BlockSpec((rb, feat), lambda i, s: (i, 0))
    whole = lambda a: pl.BlockSpec(a.shape, lambda i, s: (0,) * a.ndim)
    ins = [raw] + ([] if first else [h]) + [norm, mask, bias] + list(pieces)
    specs = [row(BF)] + ([] if first else [row(F32)]) + [whole(norm), whole(mask), whole(bias)]
    specs += [pl.BlockSpec(memory_space=pl.ANY)] * len(pieces)
    out_shape = [jax.ShapeDtypeStruct((rows, feat), BF)] * (4 * n) + [jax.ShapeDtypeStruct((rows, feat), F32)]
    return pl.pallas_call(
        functools.partial(forward_kernel, copies, n, first),
        grid_spec=pltpu.PrefetchScalarGridSpec(
            num_scalar_prefetch=1,
            grid=(rows // rb,),
            in_specs=specs,
            out_specs=[row(BF)] * (4 * n) + [row(F32)],
            scratch_shapes=[
                pltpu.VMEM((n, 2, 3, feat, feat), BF),
                pltpu.SemaphoreType.DMA((copies.total,)),
            ],
        ),
        out_shape=out_shape,
        compiler_params=pltpu.CompilerParams(vmem_limit_bytes=56 * 2**20),
        cost_estimate=pl.CostEstimate(
            flops=n * rows * feat * feat * 12, bytes_accessed=n * rows * feat * 14, transcendentals=n * rows * feat * 3
        ),
        name="forward_sections",
    )(place, *ins)


def backward_kernel(copies, nb, rb, first, place, raw, u_in, r_in, c_in, h_in, dh_in, *refs):
    refs = list(refs)
    dn_in = None if first else refs.pop(0)
    norm, mask = refs[:2]
    pieces = refs[2 : 2 + copies.count]
    dh_out, dn_out, mine, other, small = refs[2 + copies.count : 7 + copies.count]
    wbuf, dbuf, lhs, sems = refs[7 + copies.count :]
    step = pl.program_id(0)

    @pl.when(step == 0)
    def _():
        copies.run(place, pieces, wbuf, sems)
        small[...] = jnp.zeros_like(small)

    @pl.when(step < nb)
    def _():
        rows = pl.ds(pl.multiple_of(step * rb, rb), rb)
        normed = (raw[...].astype(F32) - norm[0:1, :]) * norm[1:2, :] + norm[2:3, :]
        gate_mask = sigm(mask[0:1, :])
        feat = (normed * gate_mask).astype(BF)
        u = u_in[...].astype(F32)
        c = c_in[...].astype(F32)
        dh = dh_in[...]
        h = h_in[...].astype(F32)
        t = dh * u
        dc = (t * (1.0 - c * c)).astype(BF)
        dreset = ndot(dc, wbuf[0, 1, 2])
        du = (t * (c - h) * (1.0 - u)).astype(BF)
        r = r_in[...].astype(F32)
        rh = r * h
        dr = (dreset * rh * (1.0 - r)).astype(BF)
        dbuf[0, rows, :] = du
        dbuf[1, rows, :] = dr
        dbuf[2, rows, :] = dc
        lhs[0, :, rows] = feat.T
        lhs[1, :, rows] = h_in[...].T
        lhs[2, :, rows] = rh.astype(BF).T
        dfeat = ndot(dc, wbuf[0, 0, 2]) + ndot(du, wbuf[0, 0, 0]) + ndot(dr, wbuf[0, 0, 1])
        dh_out[...] = (dh - t) + dreset * r + ndot(du, wbuf[0, 1, 0]) + ndot(dr, wbuf[0, 1, 1])
        if first:
            dn_out[...] = dfeat * gate_mask
        else:
            dn_out[...] = dn_in[...] + dfeat * gate_mask
        small[0:1, :] += jnp.sum(du.astype(F32), 0, keepdims=True)
        small[1:2, :] += jnp.sum(dr.astype(F32), 0, keepdims=True)
        small[2:3, :] += jnp.sum(dc.astype(F32), 0, keepdims=True)
        small[3:4, :] += jnp.sum(dfeat * normed, 0, keepdims=True) * (gate_mask * (1.0 - gate_mask))

    @pl.when(step >= nb)
    def _():
        m = step - nb
        which = jnp.where(m < 3, 0, jnp.where(m < 5, 1, 2))
        j = lax.rem(m, 3)
        half = mine.shape[2]
        cols = pl.multiple_of(place[1] * half, half)
        others = pl.multiple_of((1 - place[1]) * half, half)
        left = lhs[which]
        other[0] = mdot(left, dbuf[j, :, pl.ds(others, half)]).astype(BF)
        mine[0] = mdot(left, dbuf[j, :, pl.ds(cols, half)]).astype(BF)


def backward_section(copies, place, raw, saved, dh, dn, norm, mask, pieces, rb, half):
    rows, feat = raw.shape
    first = dn is None
    nb = rows // rb
    block = lambda i, s: (jnp.minimum(i, nb - 1), 0)
    row = pl.BlockSpec((rb, feat), block)
    whole = lambda a: pl.BlockSpec(a.shape, lambda i, s: (0,) * a.ndim)
    u, r, c, h = saved
    ins = [raw, u, r, c, h, dh] + ([] if first else [dn]) + [norm, mask] + list(pieces)
    specs = [row] * (6 if first else 7) + [whole(norm), whole(mask)]
    specs += [pl.BlockSpec(memory_space=pl.ANY)] * len(pieces)
    grad = pl.BlockSpec((1, feat, half), lambda i, s: (jnp.maximum(i - nb, 0), 0, 0))
    return pl.pallas_call(
        functools.partial(backward_kernel, copies, nb, rb, first),
        grid_spec=pltpu.PrefetchScalarGridSpec(
            num_scalar_prefetch=1,
            grid=(nb + 6,),
            in_specs=specs,
            out_specs=[row, row, grad, grad, pl.BlockSpec((8, feat), lambda i, s: (0, 0))],
            scratch_shapes=[
                pltpu.VMEM((1, 2, 3, feat, feat), BF),
                pltpu.VMEM((3, rows, feat), BF),
                pltpu.VMEM((3, feat, rows), BF),
                pltpu.SemaphoreType.DMA((copies.total,)),
            ],
        ),
        out_shape=[
            jax.ShapeDtypeStruct((rows, feat), F32),
            jax.ShapeDtypeStruct((rows, feat), F32),
            jax.ShapeDtypeStruct((6, feat, half), BF),
            jax.ShapeDtypeStruct((6, feat, half), BF),
            jax.ShapeDtypeStruct((8, feat), F32),
        ],
        compiler_params=pltpu.CompilerParams(vmem_limit_bytes=56 * 2**20),
        cost_estimate=pl.CostEstimate(
            flops=rows * feat * feat * 24, bytes_accessed=rows * feat * 30, transcendentals=0
        ),
        name="backward_section",
    )(place, *ins)


class Whole:
    count = 2

    def __init__(self, n):
        self.total = 2

    def run(self, place, pieces, wbuf, sems):
        copies = [
            pltpu.make_async_copy(pieces[a], wbuf.at[:, a], sems.at[a]) for a in range(2)
        ]
        for copy in copies:
            copy.start()
        for copy in copies:
            copy.wait()


def spread(table_rows, vocab, offsets, columns):
    row = lax.broadcasted_iota(jnp.int32, (vocab, table_rows), 0)
    lane = lax.broadcasted_iota(jnp.int32, (vocab, table_rows), 1)
    return jnp.concatenate([(lane == row + offsets[c]).astype(BF) for c in range(columns)], axis=0)


def column_offsets(cardinality, columns):
    offsets, total = [], 0
    for c in range(columns):
        offsets.append(total)
        total = total + cardinality[c]
    return offsets


def onehot(cat, vocab):
    columns = cat.shape[1]
    width = columns * vocab
    lane = lax.broadcasted_iota(jnp.int32, (columns, width), 1)
    owner = lax.broadcasted_iota(jnp.int32, (columns, width), 0)
    repeat = (lane // vocab == owner).astype(BF)
    values = mdot(cat.astype(F32).astype(BF), repeat)
    wanted = (lax.broadcasted_iota(jnp.int32, (1, width), 1) % vocab).astype(F32)
    return (values == wanted).astype(BF)


def prepare_kernel(vocab, rb, cardinality, numeric, cat, table, raw, stats, counts):
    rows, num = numeric.shape
    columns, emb = cat.shape[1], table.shape[1]
    table_rows = table.shape[0]
    width = columns * emb
    offsets = column_offsets(cardinality, columns)
    chosen = spread(table_rows, vocab, offsets, columns)
    tile = (
        lax.broadcasted_iota(jnp.int32, (emb, width), 1) % emb
        == lax.broadcasted_iota(jnp.int32, (emb, width), 0)
    ).astype(BF)
    tiled = mdot(table[...], tile).astype(BF)
    placed = mdot(chosen, tiled)
    own = (
        lax.broadcasted_iota(jnp.int32, placed.shape, 1) // emb
        == lax.broadcasted_iota(jnp.int32, placed.shape, 0) // vocab
    )
    blocks = jnp.where(own, placed, 0.0).astype(BF)
    total = jnp.zeros((1, num + width), F32)
    counted = jnp.zeros((1, columns * vocab), F32)
    for b in range(rows // rb):
        part = pl.ds(b * rb, rb)
        hot = onehot(cat[part, :], vocab)
        looked = mdot(hot, blocks)
        raw[part, :num] = numeric[part, :]
        raw[part, num:] = looked.astype(BF)
        total = total + jnp.concatenate(
            [jnp.sum(numeric[part, :].astype(F32), 0, keepdims=True), jnp.sum(looked, 0, keepdims=True)], axis=1
        )
        counted = counted + mdot(jnp.ones((8, rb), BF), hot)[0:1, :]
    mean = total / rows
    squares = jnp.zeros_like(total)
    for b in range(rows // rb):
        part = pl.ds(b * rb, rb)
        away = raw[part, :].astype(F32) - mean
        squares = squares + jnp.sum(away * away, 0, keepdims=True)
    stats[0:1, :] = mean
    stats[1:2, :] = squares
    counts[...] = counted


def prepare(numeric, cat_index, cardinality, emb_table, vocab):
    rows, num = numeric.shape
    feat = num + cat_index.shape[1] * emb_table.shape[1]
    vmem = pl.BlockSpec(memory_space=pltpu.VMEM)
    return pl.pallas_call(
        functools.partial(prepare_kernel, vocab, 256),
        in_specs=[pl.BlockSpec(memory_space=pltpu.SMEM), vmem, vmem, vmem],
        out_specs=[vmem, vmem, vmem],
        out_shape=[
            jax.ShapeDtypeStruct((rows, feat), BF),
            jax.ShapeDtypeStruct((2, feat), F32),
            jax.ShapeDtypeStruct((1, cat_index.shape[1] * vocab), F32),
        ],
        compiler_params=pltpu.CompilerParams(vmem_limit_bytes=56 * 2**20),
        cost_estimate=pl.CostEstimate(flops=10**9, bytes_accessed=3 * 10**6, transcendentals=0),
        name="prepare",
    )(cardinality, numeric, cat_index, emb_table)


def head_kernel(h, w1, b1, w2, b2, g, logits, dh, grad_w1, grad_w2, grad_b):
    step = pl.program_id(0)
    head_in = h[...].astype(BF)
    x = mdot(head_in, w1[...]) + b1[...]
    phi = 0.5 * (1.0 + lax.erf(x * 0.7071067811865476))
    act = (x * phi).astype(BF)
    logits[...] = mdot(act, w2[...]) + b2[...]
    dact = ndot(g[...], w2[...])
    slope = phi + x * (jnp.exp(-0.5 * x * x) * 0.3989422804014327)
    dx = (dact * slope).astype(BF)
    dh[...] = ndot(dx, w1[...])
    one = tdot(head_in, dx)
    two = tdot(g[...], act)
    sums = jnp.sum(dx.astype(F32), 0, keepdims=True)
    wide = jnp.concatenate(
        [jnp.sum(g[...].astype(F32), 0, keepdims=True), jnp.zeros((1, sums.shape[1] - g.shape[1]), F32)], axis=1
    )

    @pl.when(step == 0)
    def _():
        grad_w1[...] = jnp.zeros_like(grad_w1)
        grad_w2[...] = jnp.zeros_like(grad_w2)
        grad_b[...] = jnp.zeros_like(grad_b)

    grad_w1[...] += one
    grad_w2[...] += two
    grad_b[0:1, :] += sums
    grad_b[1:2, :] += wide


def head(h, w1, b1, w2, b2, g, rb):
    rows, feat = h.shape
    hidden, classes = w2.shape
    row = lambda width: pl.BlockSpec((rb, width), lambda i: (i, 0))
    whole = lambda *shape: pl.BlockSpec(shape, lambda i: (0, 0))
    return pl.pallas_call(
        head_kernel,
        grid=(rows // rb,),
        in_specs=[
            row(feat),
            whole(feat, hidden),
            whole(1, hidden),
            whole(hidden, classes),
            whole(1, classes),
            row(classes),
        ],
        out_specs=[row(classes), row(feat), whole(feat, hidden), whole(classes, hidden), whole(2, hidden)],
        out_shape=[
            jax.ShapeDtypeStruct((rows, classes), F32),
            jax.ShapeDtypeStruct((rows, feat), F32),
            jax.ShapeDtypeStruct((feat, hidden), F32),
            jax.ShapeDtypeStruct((classes, hidden), F32),
            jax.ShapeDtypeStruct((2, hidden), F32),
        ],
        compiler_params=pltpu.CompilerParams(vmem_limit_bytes=56 * 2**20),
        cost_estimate=pl.CostEstimate(
            flops=rows * feat * hidden * 6, bytes_accessed=rows * feat * 8, transcendentals=rows * hidden
        ),
        name="head",
    )(h, w1, b1.reshape(1, -1), w2, b2.reshape(1, -1), g)


def sums_kernel(vocab, rb, raw, cat, dh, dn, norm, both, sums, table):
    rows, feat = raw.shape
    columns = cat.shape[1]
    width = columns * vocab
    emb_all = columns * (table.shape[0])
    num = feat - emb_all
    plain = jnp.zeros((1, feat), F32)
    scaled = jnp.zeros((1, feat), F32)
    crossed = jnp.zeros((emb_all, width), F32)
    for b in range(rows // rb):
        part = pl.ds(b * rb, rb)
        grad = dh[part, :] + dn[part, :]
        both[part, :] = grad
        away = raw[part, :].astype(F32) - norm[0:1, :]
        plain = plain + jnp.sum(grad, 0, keepdims=True)
        scaled = scaled + jnp.sum(grad * away, 0, keepdims=True)
        hot = onehot(cat[part, :], vocab)
        pieces = grad[:, num:]
        high = pieces.astype(BF)
        rest = (pieces - high.astype(F32)).astype(BF)
        crossed = crossed + tdot(high, hot) + tdot(rest, hot)
    sums[0:1, :] = plain
    sums[1:2, :] = scaled * norm[3:4, :]
    emb = table.shape[0]
    own = (
        lax.broadcasted_iota(jnp.int32, crossed.shape, 0) // emb
        == lax.broadcasted_iota(jnp.int32, crossed.shape, 1) // vocab
    )
    crossed = jnp.where(own, crossed, 0.0)
    out = crossed[:emb]
    for c in range(1, columns):
        out = out + crossed[c * emb : (c + 1) * emb]
    table[...] = out


def local_sums(raw, cat_index, dh, dn, norm, vocab, emb):
    rows, feat = raw.shape
    columns = cat_index.shape[1]
    vmem = pl.BlockSpec(memory_space=pltpu.VMEM)
    return pl.pallas_call(
        functools.partial(sums_kernel, vocab, 256),
        in_specs=[vmem] * 5,
        out_specs=[vmem] * 3,
        out_shape=[
            jax.ShapeDtypeStruct((rows, feat), F32),
            jax.ShapeDtypeStruct((2, feat), F32),
            jax.ShapeDtypeStruct((emb, columns * vocab), F32),
        ],
        compiler_params=pltpu.CompilerParams(vmem_limit_bytes=56 * 2**20),
        cost_estimate=pl.CostEstimate(flops=10**9, bytes_accessed=8 * 10**6, transcendentals=0),
        name="local_sums",
    )(raw, cat_index, dh, dn, norm)


def exact_dot(left, right):
    high = left.astype(BF)
    left = left - high.astype(F32)
    middle = left.astype(BF)
    low = (left - middle.astype(F32)).astype(BF)
    return mdot(high, right) + mdot(middle, right) + mdot(low, right)


def finish_kernel(vocab, count, cardinality, both, raw, norm, sums, table_sums, counts, table, grad, grad_table):
    rows, num = grad.shape
    emb, width = table_sums.shape
    columns = width // vocab
    mean, inverse, gain = norm[0:1, :], norm[3:4, :], norm[4:5, :]
    plain = sums[0:1, :] / count
    scaled = sums[1:2, :] / count
    factor = gain * inverse
    away = (raw[:, :num].astype(F32) - mean[:, :num]) * inverse[:, :num]
    grad[...] = factor[:, :num] * (both[:, :num] - plain[:, :num] - away * scaled[:, :num])

    @pl.when(pl.program_id(0) == 0)
    def _():
        finish_table(vocab, cardinality, norm, plain, scaled, factor, table_sums, counts, table, grad_table, num)


def finish_table(vocab, cardinality, norm, plain, scaled, factor, table_sums, counts, table, grad_table, num):
    emb, width = table_sums.shape
    columns = width // vocab
    mean, inverse = norm[0:1, :], norm[3:4, :]
    flat = columns * emb
    rows_of = lax.broadcasted_iota(jnp.int32, (emb, flat), 0)
    lanes_of = lax.broadcasted_iota(jnp.int32, (emb, flat), 1)
    mine = lanes_of % emb == rows_of
    expand = (
        lax.broadcasted_iota(jnp.int32, (flat, width), 0) // emb
        == lax.broadcasted_iota(jnp.int32, (flat, width), 1) // vocab
    ).astype(BF)
    vectors = [jnp.where(mine, v[:, num:], 0.0) for v in (mean, inverse, plain, scaled, factor)]
    wide = exact_dot(jnp.concatenate(vectors, axis=0), expand)
    mean_w, inverse_w, plain_w, scaled_w, factor_w = [wide[i * emb : (i + 1) * emb] for i in range(5)]
    offsets = column_offsets(cardinality, columns)
    chosen = spread(table.shape[1], vocab, offsets, columns)
    values = ndot(table[...], chosen)
    away = (values - mean_w) * inverse_w
    found = factor_w * (table_sums[...] - counts[...] * (plain_w + away * scaled_w))
    grad_table[...] = exact_dot(found, chosen)


def finish(cardinality, both, raw, norm, sums, table_sums, counts, table, num, count, vocab, rb):
    rows, feat = raw.shape
    row = lambda width: pl.BlockSpec((rb, width), lambda i, s: (i, 0))
    whole = lambda a: pl.BlockSpec(a.shape, lambda i, s: (0, 0))
    return pl.pallas_call(
        functools.partial(finish_kernel, vocab, count),
        grid_spec=pltpu.PrefetchScalarGridSpec(
            num_scalar_prefetch=1,
            grid=(rows // rb,),
            in_specs=[row(feat), row(feat)] + [whole(a) for a in (norm, sums, table_sums, counts, table)],
            out_specs=[row(num), whole(table)],
        ),
        out_shape=[
            jax.ShapeDtypeStruct((rows, num), F32),
            jax.ShapeDtypeStruct(table.shape, F32),
        ],
        compiler_params=pltpu.CompilerParams(vmem_limit_bytes=56 * 2**20),
        cost_estimate=pl.CostEstimate(flops=10**8, bytes_accessed=6 * 10**6, transcendentals=0),
        name="finish",
    )(cardinality, both, raw, norm, sums, table_sums, counts, table)


class Parts:
    count = 28

    def __init__(self, start, n, offset):
        self.start, self.n, self.offset = start, n, offset
        self.total = 28

    def run(self, place, pieces, wbuf, sems):
        depth, width = pieces[0].shape[2:]
        z, c = place[0], place[1]
        copies = []
        for a in range(2):
            half = place[2 + a]
            for core in range(2):
                column = (c if core == 0 else 1 - c) * width
                for s in range(7):
                    piece = pieces[a * 14 + core * 7 + s]
                    if s == 0:
                        row, tall, first = z * depth, depth, self.start
                    else:
                        hop = (s - 1) % 3 + 1
                        own = half if s < 4 else 1 - half
                        row = lax.rem(z + 4 - hop, 4) * depth + own * (depth // 2)
                        tall, first = depth // 2, self.offset
                    copies.append(
                        pltpu.make_async_copy(
                            piece.at[pl.ds(first, self.n)],
                            wbuf.at[
                                :,
                                a,
                                :,
                                pl.ds(pl.multiple_of(row, tall), tall),
                                pl.ds(pl.multiple_of(column, width), width),
                            ],
                            sems.at[len(copies)],
                        )
                    )
        for copy in copies:
            copy.start()
        for copy in copies:
            copy.wait()


SWAP = [(0, 1), (1, 0)]
ACROSS_X = [(0, 1), (1, 0), (2, 3), (3, 2)]
ACROSS_Y = [(0, 2), (2, 0), (1, 3), (3, 1)]
ROUND = [(0, 1), (1, 2), (2, 3), (3, 0)]
ACROSS = (ACROSS_X, ACROSS_Y)


def other_core(v):
    return lax.ppermute(v, "wide", SWAP)


def gather_parts(arrays, mine, across, place, start, n):
    parts = []
    for a in range(2):
        block = arrays[a]
        depth = block.shape[2]
        piece = lax.dynamic_slice(
            block,
            (start, 0, place[2 + a] * (depth // 2), 0),
            (n, block.shape[1], depth // 2, block.shape[3]),
        )
        hops = []
        for _ in range(3):
            piece = lax.ppermute(piece, "narrow", ROUND)
            hops.append(piece)
        hops += [lax.ppermute(v, "dp", ACROSS[a]) for v in hops]
        parts += [block] + hops + [across[a]] + [other_core(v) for v in hops]
    return parts


def total_of(v):
    v = v + other_core(v)
    for way in ACROSS:
        v = v + lax.ppermute(v, "dp", way)
    v = v + lax.ppermute(v, "narrow", [(0, 1), (1, 0), (2, 3), (3, 2)])
    return v + lax.ppermute(v, "narrow", [(0, 2), (1, 3), (2, 0), (3, 1)])


def merge(one, two, count):
    apart = one[0] - two[0]
    mean = 0.5 * (one[0] + two[0])
    return jnp.stack([mean, one[1] + two[1] + apart * apart * (0.5 * count)])


def whole_statistics(stats, rows):
    steps = [("wide", SWAP), ("dp", ACROSS_X), ("dp", ACROSS_Y)]
    steps += [("narrow", [(0, 1), (1, 0), (2, 3), (3, 2)]), ("narrow", [(0, 2), (1, 3), (2, 0), (3, 1)])]
    for axis, way in steps:
        stats = merge(stats, lax.ppermute(stats, axis, way), float(rows))
        rows = rows * 2
    return stats[0], stats[1] / rows


def half_of(block, index, which):
    tall = block.shape[2] // 2
    return lax.dynamic_slice_in_dim(block, jnp.where(which, index, 1 - index) * tall, tall, 2)


def reduce_section(mine, other, place):
    came = other_core(other)
    results = []
    z = place[0]
    for a in range(2):
        shape = (3, 4, mine.shape[1] // 4, mine.shape[2])
        kept = mine[3 * a : 3 * a + 3].reshape(shape).astype(F32)
        added = came[3 * a : 3 * a + 3].reshape(shape).astype(F32)
        index = place[2 + a]
        send = (half_of(kept, index, False) + half_of(added, index, False)).astype(BF)
        got = lax.ppermute(send, "dp", ACROSS[a])
        part = half_of(kept, index, True) + half_of(added, index, True) + got.astype(F32)
        part = part.astype(BF)
        block = lambda hop: lax.dynamic_index_in_dim(part, lax.rem(z + 4 - hop, 4), 1, keepdims=False).astype(F32)
        moving = block(1).astype(BF)
        for hop in (2, 3, 4):
            moving = lax.ppermute(moving, "narrow", ROUND)
            moving = block(hop) + moving.astype(F32)
            if hop < 4:
                moving = moving.astype(BF)
        results.append(moving.astype(BF))
    return results


def complete(halves, place):
    outs = []
    for a in range(2):
        half = jnp.stack(halves[a])
        half = half.astype(F32) + lax.ppermute(half, "dp", ACROSS[1 - a]).astype(F32)
        away = lax.ppermute(half.astype(BF), "dp", ACROSS[a]).astype(F32)
        low = place[2 + a] == 0
        outs.append(
            jnp.concatenate([jnp.where(low, half, away), jnp.where(low, away, half)], axis=2)
        )
    return outs


CHUNKS = ((0, 1), (1, 2), (3, 3))
VOCAB = 64


def body(
    numeric,
    cat_index,
    cardinality,
    emb_table,
    input_norm_gain,
    input_norm_bias,
    mask_logit,
    w_feat,
    w_state,
    gate_bias,
    head_w1,
    head_b1,
    head_w2,
    head_b2,
    cotangent,
):
    axes = ("dp", "wide", "narrow")
    rows, num = numeric.shape
    sections = w_feat.shape[0]
    feat = w_feat.shape[2] * lax.axis_size("narrow")
    emb = emb_table.shape[1]
    count = float(rows * lax.axis_size(axes))
    fast = tuple(lax.axis_size(a) for a in axes) == (4, 2, 4)
    d = lax.axis_index("dp")
    c = lax.axis_index("wide")
    z = lax.axis_index("narrow")
    half = feat // 2

    raw, stats, counts = prepare(numeric, cat_index, cardinality, emb_table, VOCAB)
    if fast:
        place = jnp.stack([z, c, lax.rem(d, 2), d // 2]).astype(jnp.int32)
        mean, var = whole_statistics(stats, rows)
        across = (other_core(w_feat), other_core(w_state))
        gathered = [gather_parts((w_feat, w_state), None, across, place, s, n) for s, n in CHUNKS]
        chunks = [(s, n, Parts(s, n, 0), g) for (s, n), g in zip(CHUNKS, gathered)]
    else:
        place = jnp.zeros((4,), jnp.int32)
        means = lax.all_gather(stats, axes)
        mean = jnp.mean(means[:, 0], 0)
        away = means[:, 0] - mean
        var = (jnp.sum(means[:, 1], 0) + rows * jnp.sum(away * away, 0)) / count
        whole = [
            lax.all_gather(lax.all_gather(w, "narrow", axis=2, tiled=True), "wide", axis=3, tiled=True)
            for w in (w_feat, w_state)
        ]
        chunks = [(s, n, Whole(n), [w[s : s + n] for w in whole]) for s, n in CHUNKS]
    inverse = lax.rsqrt(var + EPSILON)
    norm = jnp.stack([mean, inverse * input_norm_gain, input_norm_bias, inverse, input_norm_gain])

    saved = []
    h = None
    for s, n, copies, pieces in chunks:
        outs = forward_sections(
            copies, n, place, raw, h, norm, mask_logit[s : s + n], gate_bias[s : s + n], pieces, min(512, rows)
        )
        for k in range(n):
            one = Parts(s + k, 1, k) if fast else Whole(1)
            given = pieces if fast else [w[k : k + 1] for w in pieces]
            saved.append((outs[4 * k : 4 * k + 4], one, given))
        h = outs[4 * n]

    logits, dh, grad_w1, grad_w2, grad_hb = head(h, head_w1, head_b1, head_w2, head_b2, cotangent, 256)

    dn = None
    halves = ([None] * sections, [None] * sections)
    small = [None] * sections
    for k in reversed(range(sections)):
        kept, one, pieces = saved[k]
        dh, dn, mine, other, small[k] = backward_section(
            one, place, raw, kept, dh, dn, norm, mask_logit[k : k + 1], pieces, 256, half
        )
        if fast:
            halves[0][k], halves[1][k] = reduce_section(mine, other, place)
        else:
            local = jnp.concatenate([mine, other], axis=2)
            for a in range(2):
                part = lax.psum_scatter(local[3 * a : 3 * a + 3], "wide", scatter_dimension=2, tiled=True)
                part = lax.psum_scatter(part, "narrow", scatter_dimension=1, tiled=True)
                halves[a][k] = lax.psum(part, "dp").astype(F32)

    both, sums, table_sums = local_sums(raw, cat_index, dh, dn, norm, VOCAB, emb)
    pack = jnp.concatenate(
        [
            sums,
            table_sums.reshape(-1, feat),
            counts.reshape(-1, feat),
            jnp.stack(small)[:, :4].reshape(-1, feat),
            grad_w2.reshape(-1, feat),
            grad_hb.reshape(-1, feat),
        ]
    )
    early = lax.psum(grad_w1, axes)
    pack = total_of(pack) if fast else lax.psum(pack, axes)
    bounds = [2, table_sums.size // feat, counts.size // feat, 4 * sections, grad_w2.size // feat, 1]
    places = [sum(bounds[:i]) for i in range(len(bounds) + 1)]
    sums, table_sums, counts, small, grad_w2, grad_hb = [
        pack[places[i] : places[i + 1]] for i in range(len(bounds))
    ]
    grad_numeric, grad_table = finish(
        cardinality,
        both,
        raw,
        norm,
        sums,
        table_sums.reshape(emb, -1),
        counts.reshape(1, -1),
        emb_table.T,
        num,
        count,
        VOCAB,
        256,
    )
    if fast:
        grad_feat, grad_state = complete(halves, place)
    else:
        grad_feat, grad_state = (jnp.stack(v) for v in halves)
    small = small.reshape(sections, 4, feat)
    grad_hb = grad_hb.reshape(2, -1)
    classes = head_w2.shape[1]
    return (
        logits,
        grad_numeric,
        grad_table.T,
        sums[1],
        sums[0],
        small[:, 3],
        grad_feat,
        grad_state,
        small[:, :3],
        early,
        grad_hb[0],
        grad_w2.reshape(classes, -1).T,
        grad_hb[1, :classes],
    )


def solution(mesh):
    spread_rows = P(("dp", "wide", "narrow"), None)
    blocks = P(None, None, "narrow", "wide")
    in_specs = (spread_rows, spread_rows) + (P(),) * 5 + (blocks, blocks) + (P(),) * 5 + (spread_rows,)
    out_specs = (spread_rows, spread_rows) + (P(),) * 4 + (blocks, blocks) + (P(),) * 5
    return jax.shard_map(body, mesh=mesh, in_specs=in_specs, out_specs=out_specs, check_vma=False)
```

```python
import functools
import jax
import jax.numpy as jnp
from jax import lax
from jax.experimental import pallas as pl
from jax.experimental.pallas import tpu as pltpu
from jax.sharding import PartitionSpec as P

EPSILON = 1e-05
BF = jnp.bfloat16
F32 = jnp.float32
VMEM = pl.BlockSpec(memory_space=pltpu.VMEM)
SMEM = pl.BlockSpec(memory_space=pltpu.SMEM)
ANY = pl.BlockSpec(memory_space=pl.ANY)
MIB = 2**20
WORK = 4 * 10**11


def mdot(left, right):
    return lax.dot_general(left, right, (((1,), (0,)), ((), ())), preferred_element_type=F32)


def tdot(left, right):
    return lax.dot_general(left, right, (((0,), (0,)), ((), ())), preferred_element_type=F32)


def ndot(left, right):
    return lax.dot_general(left, right, (((1,), (1,)), ((), ())), preferred_element_type=F32)


def sigm(v):
    return 0.5 * jnp.tanh(0.5 * v) + 0.5


def call(kernel, turn, ins, outs, name, scratch=(), aliases=None, limit=4, work=0, awaited=()):
    specs = {"v": VMEM, "p": VMEM, "h": ANY, "a": ANY, "s": SMEM}
    memory = {"v": pltpu.VMEM, "h": pltpu.HBM}
    ins = [("v", turn)] + list(ins)
    used = len(ins)
    ins += [("a", x) for x in awaited]
    outs = [("v", turn.shape, turn.dtype)] + list(outs)
    given = [pltpu.with_memory_space_constraint(x, memory[kind]) if kind in memory else x for kind, x in ins]
    fast = is_fast()

    def shape(kind, dims, dtype):
        return memory[kind](dims, dtype) if kind in memory else jax.ShapeDtypeStruct(dims, dtype)

    def run(*refs):
        place = [lax.axis_index(a) if fast else 0 for a in ("narrow", "wide", "dp")]
        kernel(place, refs[1:used], refs[len(ins) + 1 : len(ins) + len(outs)], *refs[len(ins) + len(outs) :])

    turn, *results = pl.pallas_call(
        run,
        in_specs=[specs[kind] for kind, _ in ins],
        out_specs=[specs[o[0]] for o in outs],
        out_shape=[shape(*o) for o in outs],
        scratch_shapes=list(scratch),
        input_output_aliases={0: 0, **{i + 1: o + 1 for i, o in (aliases or {}).items()}},
        compiler_params=pltpu.CompilerParams(vmem_limit_bytes=limit * MIB),
        cost_estimate=pl.CostEstimate(flops=work, bytes_accessed=0, transcendentals=0),
        name=name,
    )(*given)
    return (*results, turn)


def is_fast():
    return tuple(lax.axis_size(a) for a in ("dp", "wide", "narrow")) == (4, 2, 4)


def forward_kernel(copies, s, n, first, last, rb, place, ins, outs, *scratch):
    raw, norm, mask, bias = ins[:4]
    pieces = ins[4:] if first else ins[5:]
    h_out = outs[0]
    if last:
        weights, saved = outs[1:]
        sems = scratch[0]
    else:
        stored, kept = outs[1:]
        weights, saved, sems, outsem = scratch
    loads = copies.start(place, pieces, weights, sems)
    for copy in loads:
        copy.wait()
    stores = []
    if not last:
        stores.append(pltpu.make_async_copy(weights, stored, outsem.at[0, 0]))
        stores[-1].start()
    for b in range(raw.shape[0] // rb):
        part = pl.ds(b * rb, rb)
        normed = (raw[part, :].astype(F32) - norm[0:1, :]) * norm[1:2, :] + norm[2:3, :]
        h = normed if first else ins[4][part, :]
        for k in range(n):
            feat = (normed * sigm(mask[s + k : s + k + 1, :])).astype(BF)
            low = h.astype(BF)
            saved[k, 3, part, :] = low
            rpre = mdot(feat, weights[k, 0, 1]) + mdot(low, weights[k, 1, 1]) + bias[s + k, 1:2, :]
            r = sigm(rpre)
            upre = mdot(feat, weights[k, 0, 0]) + mdot(low, weights[k, 1, 0]) + bias[s + k, 0:1, :]
            u = sigm(upre)
            reset = (r * h).astype(BF)
            cpre = mdot(feat, weights[k, 0, 2]) + mdot(reset, weights[k, 1, 2]) + bias[s + k, 2:3, :]
            c = jnp.tanh(cpre)
            h = h + u * (c - h)
            saved[k, 0, part, :] = u.astype(BF)
            saved[k, 1, part, :] = r.astype(BF)
            saved[k, 2, part, :] = c.astype(BF)
            if not last:
                stores.append(pltpu.make_async_copy(saved.at[k, :, part], kept.at[k, :, part], outsem.at[1 + b, k]))
                stores[-1].start()
        h_out[part, :] = h
    for copy in stores:
        copy.wait()


def forward_sections(copies, s, n, last, turn, raw, h, norm, mask, bias, pieces, rb=512):
    rows, feat = raw.shape
    first = h is None
    ins = [("v", raw), ("v", norm), ("v", mask), ("v", bias)] + ([] if first else [("v", h)]) + pieces
    whole = (n, 2, 3, feat, feat)
    kept = (n, 4, rows, feat)
    kind = "v" if last else "h"
    scratch = [] if last else [pltpu.VMEM(whole, BF), pltpu.VMEM(kept, BF)]
    scratch += [pltpu.SemaphoreType.DMA((copies.total,))]
    scratch += [] if last else [pltpu.SemaphoreType.DMA((1 + rows // rb, n))]
    return call(
        functools.partial(forward_kernel, copies, s, n, first, last, rb),
        turn,
        ins,
        [("v", (rows, feat), F32), (kind, whole, BF), (kind, kept, BF)],
        "forward_sections",
        work=WORK,
        scratch=scratch,
        aliases={} if first else {4: 0},
        limit=12 if last else 12 + 8 * n,
    )


def backward_kernel(s, rb, first, coming, place, ins, outs, sems):
    raw, saved, norm, mask, weights, dh_in = ins[:6]
    dn_in = None if first else ins[6]
    dh_out, dn_out, dbuf, lhs, small = outs[:5]
    loads = []
    if coming is not None:
        for i in range(2):
            loads.append(pltpu.make_async_copy(ins[-2 + i].at[pl.ds(coming, 1)], outs[5 + i], sems.at[i]))
            loads[-1].start()
    rows = raw.shape[0]
    gate_mask = sigm(mask[s : s + 1, :])
    sums = [jnp.zeros((1, gate_mask.shape[1]), F32)] * 4
    for b in range(rows // rb):
        part = pl.ds(b * rb, rb)
        u = saved[0, 0, part, :].astype(F32)
        c = saved[0, 2, part, :].astype(F32)
        dh = dh_in[part, :]
        t = dh * u
        dc = (t * (1.0 - c * c)).astype(BF)
        dreset = ndot(dc, weights[0, 1, 2])
        low = saved[0, 3, part, :]
        h = low.astype(F32)
        du = (t * (c - h) * (1.0 - u)).astype(BF)
        dbuf[2, part, :] = dc
        dbuf[0, part, :] = du
        dfeat = ndot(dc, weights[0, 0, 2]) + ndot(du, weights[0, 0, 0])
        state = ndot(du, weights[0, 1, 0])
        normed = (raw[part, :].astype(F32) - norm[0:1, :]) * norm[1:2, :] + norm[2:3, :]
        feat = (normed * gate_mask).astype(BF)
        r = saved[0, 1, part, :].astype(F32)
        rh = r * h
        dr = (dreset * rh * (1.0 - r)).astype(BF)
        dbuf[1, part, :] = dr
        lhs[0, :, part] = feat.T
        lhs[1, :, part] = low.T
        lhs[2, :, part] = rh.astype(BF).T
        dfeat = dfeat + ndot(dr, weights[0, 0, 1])
        dh_out[part, :] = (dh - t) + dreset * r + state + ndot(dr, weights[0, 1, 1])
        dn_out[part, :] = dfeat * gate_mask if first else dn_in[part, :] + dfeat * gate_mask
        for i, v in enumerate((du.astype(F32), dr.astype(F32), dc.astype(F32), dfeat * normed)):
            sums[i] = sums[i] + jnp.sum(v, 0, keepdims=True)
    slope = gate_mask * (1.0 - gate_mask)
    small[...] = jnp.concatenate(sums[:3] + [sums[3] * slope] + [jnp.zeros_like(slope)] * 4, axis=0)
    for copy in loads:
        copy.wait()


def backward_section(s, turn, raw, saved, norm, mask, weights, dh, dn, coming, rb=256):
    rows, feat = raw.shape
    first = dn is None
    ins = [("v", v) for v in (raw, saved, norm, mask, weights, dh)] + ([] if first else [("v", dn)])
    outs = [("v", (rows, feat), F32)] * 2 + [("v", (3, rows, feat), BF), ("v", (3, feat, rows), BF)]
    outs += [("v", (8, feat), F32)]
    if coming is not None:
        ins += [("h", v) for v in coming[:2]]
        outs += [("v", weights.shape, BF), ("v", saved.shape, BF)]
    return call(
        functools.partial(backward_kernel, s, rb, first, None if coming is None else coming[2]),
        turn,
        ins,
        outs,
        "backward_section",
        work=WORK,
        scratch=[pltpu.SemaphoreType.DMA((2,))],
        aliases={5: 0} if first else {5: 0, 6: 1},
        limit=9,
    )


def gradients_kernel(place, ins, outs):
    dbuf, lhs = ins
    half = outs[0].shape[-1]
    for out, core in zip(outs, (1 - place[1], place[1])):
        columns = pl.ds(pl.multiple_of(core * half, half), half)
        for m in range(6):
            which = 0 if m < 3 else (1 if m < 5 else 2)
            dot = mdot(lhs[which], dbuf[m % 3, :, columns]).astype(BF)
            out[m] = dot.reshape(out.shape[1:])


def gradients(turn, dbuf, lhs, half):
    feat = lhs.shape[1]
    shape = ("v", (6, 4, feat // 4, half), BF)
    return call(
        gradients_kernel, turn, [("v", dbuf), ("v", lhs)], [shape, shape], "gradients", limit=12, work=WORK
    )


class Whole:
    total = 2

    def start(self, place, pieces, weights, sems):
        copies = [pltpu.make_async_copy(pieces[a], weights.at[:, a], sems.at[a]) for a in range(2)]
        for copy in copies:
            copy.start()
        return copies


def spread(table_rows, vocab, offsets, columns):
    row = lax.broadcasted_iota(jnp.int32, (vocab, table_rows), 0)
    lane = lax.broadcasted_iota(jnp.int32, (vocab, table_rows), 1)
    return jnp.concatenate([(lane == row + offsets[c]).astype(BF) for c in range(columns)], axis=0)


def column_offsets(cardinality, columns):
    offsets, total = [], 0
    for c in range(columns):
        offsets.append(total)
        total = total + cardinality[c]
    return offsets


def onehot(cat, vocab):
    columns = cat.shape[0]
    width = columns * vocab
    lane = lax.broadcasted_iota(jnp.int32, (columns, width), 1)
    owner = lax.broadcasted_iota(jnp.int32, (columns, width), 0)
    repeat = (lane // vocab == owner).astype(BF)
    values = tdot(cat.astype(F32).astype(BF), repeat)
    wanted = (lax.broadcasted_iota(jnp.int32, (1, width), 1) % vocab).astype(F32)
    return (values == wanted).astype(BF)


def prepare_kernel(vocab, rb, place, ins, outs):
    numeric, cat, cardinality, table = ins
    raw, stats, counts = outs
    rows, num = numeric.shape
    columns, (emb, table_rows) = cat.shape[0], table.shape
    width = columns * emb
    chosen = spread(table_rows, vocab, column_offsets(cardinality, columns), columns)
    tile = (
        lax.broadcasted_iota(jnp.int32, (emb, width), 1) % emb
        == lax.broadcasted_iota(jnp.int32, (emb, width), 0)
    ).astype(BF)
    placed = mdot(chosen, tdot(table[...], tile).astype(BF))
    own = (
        lax.broadcasted_iota(jnp.int32, placed.shape, 1) // emb
        == lax.broadcasted_iota(jnp.int32, placed.shape, 0) // vocab
    )
    blocks = jnp.where(own, placed, 0.0).astype(BF)
    total = jnp.zeros((1, num + width), F32)
    counted = jnp.zeros((1, columns * vocab), F32)
    for b in range(rows // rb):
        part = pl.ds(b * rb, rb)
        hot = onehot(cat[:, part], vocab)
        looked = mdot(hot, blocks)
        raw[part, :num] = numeric[part, :]
        raw[part, num:] = looked.astype(BF)
        total = total + jnp.concatenate(
            [jnp.sum(numeric[part, :].astype(F32), 0, keepdims=True), jnp.sum(looked, 0, keepdims=True)], axis=1
        )
        counted = counted + mdot(jnp.ones((8, rb), BF), hot)[0:1, :]
    mean = total / rows
    squares = jnp.zeros_like(total)
    for b in range(rows // rb):
        away = raw[pl.ds(b * rb, rb), :].astype(F32) - mean
        squares = squares + jnp.sum(away * away, 0, keepdims=True)
    stats[0:1, :] = mean
    stats[1:2, :] = squares
    counts[...] = counted


def prepare(turn, numeric, cat, cardinality, table, vocab):
    rows, num = numeric.shape
    feat = num + cat.shape[0] * table.shape[0]
    return call(
        functools.partial(prepare_kernel, vocab, 256),
        turn,
        [("v", numeric), ("v", cat), ("s", cardinality), ("v", table)],
        [("v", (rows, feat), BF), ("v", (2, feat), F32), ("v", (1, cat.shape[0] * vocab), F32)],
        "prepare",
        work=WORK,
        limit=24,
    )


def merge_kernel(count, place, ins, outs):
    one, two = ins
    out = outs[0]
    apart = one[0:1, :] - two[0:1, :]
    out[0:1, :] = 0.5 * (one[0:1, :] + two[0:1, :])
    out[1:2, :] = one[1:2, :] + two[1:2, :] + apart * apart * (0.5 * count)


def norm_kernel(count, place, ins, outs):
    stats, gain, bias = ins
    out = outs[0]
    inverse = lax.rsqrt(stats[1:2, :] / count + EPSILON)
    out[0:1, :] = stats[0:1, :]
    out[1:2, :] = inverse * gain[...]
    out[2:3, :] = bias[...]
    out[3:4, :] = inverse
    out[4:5, :] = gain[...]
    out[5:8, :] = jnp.zeros((3, inverse.shape[1]), F32)


def head_kernel(rb, place, ins, outs, hidden, slopes):
    h, w1, b1, w2, b2, g = ins
    dh, logits, grad_w1, grad_w2, grad_b = outs
    rows = h.shape[0]
    width = w1.shape[1]
    classes = w2.shape[0]
    eye = lax.broadcasted_iota(jnp.int32, (classes, classes), 0) == lax.broadcasted_iota(
        jnp.int32, (classes, classes), 1
    )
    shift = jnp.sum(jnp.where(eye, b2[...], 0.0), 1, keepdims=True)
    two = jnp.zeros(w2.shape, F32)
    sums = jnp.zeros((1, width), F32)
    for b in range(rows // rb):
        part = pl.ds(b * rb, rb)
        head_in = h[part, :].astype(BF)
        hidden[part, :] = head_in
        x = mdot(head_in, w1[...]) + b1[...]
        phi = 0.5 * (1.0 + lax.erf(x * 0.7071067811865476))
        act = (x * phi).astype(BF)
        logits[:, part] = ndot(w2[...], act) + shift
        dact = tdot(g[:, part], w2[...])
        slope = phi + x * (jnp.exp(-0.5 * x * x) * 0.3989422804014327)
        dx = (dact * slope).astype(BF)
        slopes[part, :] = dx
        dh[part, :] = ndot(dx, w1[...])
        two = two + mdot(g[:, part], act)
        sums = sums + jnp.sum(dx.astype(F32), 0, keepdims=True)
    one = tdot(hidden[...], slopes[...]).astype(BF)
    depth = grad_w1.shape[1]
    for i in range(grad_w1.shape[0]):
        grad_w1[i] = one[i * depth : (i + 1) * depth]
    grad_w2[...] = two
    grad_b[...] = jnp.zeros_like(grad_b)
    grad_b[0:1, :] = sums
    grad_b[1:2, : g.shape[0]] = ndot(jnp.ones((8, rows), BF), g[...])[0:1, :]


def head(turn, h, w1, b1, w2, b2, g):
    rows, feat = h.shape
    classes, hidden = w2.shape
    return call(
        functools.partial(head_kernel, 256),
        turn,
        [("v", v) for v in (h, w1, b1.reshape(1, -1), w2, b2.reshape(1, -1), g)],
        [
            ("v", (rows, feat), F32),
            ("p", (classes, rows), F32),
            ("v", (4, feat // 4, hidden), BF),
            ("v", (classes, hidden), F32),
            ("v", (8, hidden), F32),
        ],
        "head",
        work=WORK,
        scratch=[pltpu.VMEM((rows, feat), BF), pltpu.VMEM((rows, hidden), BF)],
        aliases={0: 0},
        limit=16,
    )


def layout(sections, classes, emb, width, feat):
    at = {"sums": 0, "small": 8}
    at["bias"] = at["small"] + 8 * sections
    at["w2"] = at["bias"] + 1
    at["counts"] = at["w2"] + -(-classes // 2)
    at["table"] = -(-(at["counts"] + width // feat) // 8) * 8
    at["rows"] = at["table"] + emb * width // feat
    return at


def sums_kernel(vocab, rb, at, place, ins, outs):
    raw, cat, dh, dn, norm, counts, grad_w2, grad_b = ins[:8]
    small = ins[8:]
    pack = outs[0]
    rows, feat = raw.shape
    columns = cat.shape[0]
    width = columns * vocab
    emb = (pack.shape[0] - at["table"]) * feat // width
    num = feat - columns * emb
    plain = jnp.zeros((1, feat), F32)
    scaled = jnp.zeros((1, feat), F32)
    crossed = jnp.zeros((columns * emb, width), F32)
    for b in range(rows // rb):
        part = pl.ds(b * rb, rb)
        grad = dh[part, :] + dn[part, :]
        away = raw[part, :].astype(F32) - norm[0:1, :]
        plain = plain + jnp.sum(grad, 0, keepdims=True)
        scaled = scaled + jnp.sum(grad * away, 0, keepdims=True)
        hot = onehot(cat[:, part], vocab)
        pieces = grad[:, num:]
        high = pieces.astype(BF)
        rest = (pieces - high.astype(F32)).astype(BF)
        crossed = crossed + tdot(high, hot) + tdot(rest, hot)
    own = (
        lax.broadcasted_iota(jnp.int32, crossed.shape, 0) // emb
        == lax.broadcasted_iota(jnp.int32, crossed.shape, 1) // vocab
    )
    crossed = jnp.where(own, crossed, 0.0)
    table = crossed[:emb]
    for c in range(1, columns):
        table = table + crossed[c * emb : (c + 1) * emb]
    pack[...] = jnp.zeros_like(pack)
    pack[0:1, :] = plain
    pack[1:2, :] = scaled * norm[3:4, :]
    for k, v in enumerate(small):
        pack[at["small"] + 8 * k : at["small"] + 8 * k + 8, :] = v[...]
    half = feat // 2
    pack[at["bias"] : at["bias"] + 1, :half] = grad_b[0:1, :]
    pack[at["bias"] : at["bias"] + 1, half:] = grad_b[1:2, :]
    for i in range(grad_w2.shape[0]):
        row = at["w2"] + i // 2
        pack[row : row + 1, (i % 2) * half : (i % 2 + 1) * half] = grad_w2[i : i + 1, :]
    for i in range(width // feat):
        pack[at["counts"] + i : at["counts"] + i + 1, :] = counts[:, i * feat : (i + 1) * feat]
        pack[at["table"] + i * emb : at["table"] + (i + 1) * emb, :] = table[:, i * feat : (i + 1) * feat]


def exact_dot(left, right):
    high = left.astype(BF)
    left = left - high.astype(F32)
    middle = left.astype(BF)
    low = (left - middle.astype(F32)).astype(BF)
    return mdot(high, right) + mdot(middle, right) + mdot(low, right)


def finish_kernel(vocab, count, at, place, ins, outs):
    dh, dn, raw, norm, pack, table, cardinality = ins
    grad, grad_table, plain_out, scaled_out, grad_mask, grad_bias, grad_b1, grad_w2, grad_b2 = outs
    feat = raw.shape[1]
    num = grad.shape[1]
    emb, table_rows = table.shape
    columns = (feat - num) // emb
    width = columns * vocab
    mean, inverse, gain = norm[0:1, :], norm[3:4, :], norm[4:5, :]
    plain_out[...] = pack[0:1, :]
    scaled_out[...] = pack[1:2, :]
    plain = pack[0:1, :] / count
    scaled = pack[1:2, :] / count
    factor = gain * inverse
    for b in range(raw.shape[0] // 256):
        part = pl.ds(b * 256, 256)
        away = (raw[part, :num].astype(F32) - mean[:, :num]) * inverse[:, :num]
        both = dh[part, :num] + dn[part, :num]
        grad[part, :] = factor[:, :num] * (both - plain[:, :num] - away * scaled[:, :num])
    for k in range(grad_mask.shape[0]):
        rows = pack[at["small"] + 8 * k : at["small"] + 8 * k + 8, :]
        grad_bias[k] = rows[:3]
        grad_mask[k : k + 1, :] = rows[3:4]
    half = feat // 2
    grad_b1[...] = pack[at["bias"] : at["bias"] + 1, :half]
    grad_b2[...] = pack[at["bias"] : at["bias"] + 1, half : half + grad_b2.shape[1]]
    for i in range(grad_w2.shape[0]):
        row = at["w2"] + i // 2
        grad_w2[i : i + 1, :] = pack[row : row + 1, (i % 2) * half : (i % 2 + 1) * half]
    flat = columns * emb
    mine = (
        lax.broadcasted_iota(jnp.int32, (emb, flat), 1) % emb
        == lax.broadcasted_iota(jnp.int32, (emb, flat), 0)
    )
    expand = (
        lax.broadcasted_iota(jnp.int32, (flat, width), 0) // emb
        == lax.broadcasted_iota(jnp.int32, (flat, width), 1) // vocab
    ).astype(BF)
    vectors = [jnp.where(mine, v[:, num:], 0.0) for v in (mean, inverse, plain, scaled, factor)]
    wide = exact_dot(jnp.concatenate(vectors, axis=0), expand)
    mean_w, inverse_w, plain_w, scaled_w, factor_w = [wide[i * emb : (i + 1) * emb] for i in range(5)]
    chosen = spread(table_rows, vocab, column_offsets(cardinality, columns), columns)
    away = (ndot(table[...], chosen) - mean_w) * inverse_w
    steps = range(width // feat)
    counts = jnp.concatenate([pack[at["counts"] + i : at["counts"] + i + 1, :] for i in steps], axis=1)
    sums = jnp.concatenate([pack[at["table"] + i * emb : at["table"] + (i + 1) * emb, :] for i in steps], axis=1)
    grad_table[...] = exact_dot(factor_w * (sums - counts * (plain_w + away * scaled_w)), chosen)


class Parts:
    total = 28

    def __init__(self, first, n, ways):
        self.first, self.n, self.ways = first, n, ways

    def start(self, place, pieces, weights, sems):
        depth, width = pieces[0].shape[2:]
        tall = depth // 4
        z, c, d = place[0], place[1], place[2]
        copies = []

        def add(source, arrays, row, rows, core):
            column = (c if core == 0 else 1 - c) * width
            copies.append(
                pltpu.make_async_copy(
                    source,
                    weights.at[
                        :,
                        arrays,
                        :,
                        pl.ds(pl.multiple_of(row, rows), rows),
                        pl.ds(pl.multiple_of(column, width), width),
                    ],
                    sems.at[len(copies)],
                )
            )

        for core in range(2):
            for a in range(2):
                add(pieces[2 * core + a].at[pl.ds(self.first, self.n)], a, z * depth, depth, core)
            for i, way in enumerate((0, self.ways[0], self.ways[1], 3)):
                quarter = lax.bitwise_xor(d, way) if way else d
                for hop in range(3):
                    row = lax.rem(z + 3 - hop, 4) * depth + quarter * tall
                    add(pieces[4 + core].at[i, hop], slice(None), row, tall, core)
        for copy in copies:
            copy.start()
        return copies


SWAP = [(0, 1), (1, 0)]
ACROSS = {1: [(0, 1), (1, 0), (2, 3), (3, 2)], 2: [(0, 2), (2, 0), (1, 3), (3, 1)]}
NEAR = [(0, 1), (1, 0), (2, 3), (3, 2)]
FAR = [(0, 2), (1, 3), (2, 0), (3, 1)]


def other_core(v):
    return lax.ppermute(v, "wide", SWAP)


def along_dp(v, way):
    return lax.ppermute(v, "dp", ACROSS[way])


def along_narrow(v, hops):
    return lax.ppermute(v, "narrow", [(i, (i + hops) % 4) for i in range(4)])


def quarters_kernel(chunks, place, ins, outs, sems):
    tall = ins[0].shape[2] // 4
    rows = pl.ds(pl.multiple_of(place[2] * tall, tall), tall)
    copies = []
    for (s, n), out in zip(chunks, outs):
        for a in range(2):
            copies.append(pltpu.make_async_copy(ins[a].at[pl.ds(s, n), :, rows], out.at[:, a], sems.at[len(copies)]))
    for copy in copies:
        copy.start()
    for copy in copies:
        copy.wait()


def pack_kernel(place, ins, outs):
    for i, v in enumerate(ins):
        outs[0][i] = v[...]


def relay_kernel(place, ins, outs):
    for i, v in enumerate(ins[:3]):
        outs[0][i] = v[...]
    outs[1][...] = ins[1][...]


def close_kernel(place, ins, outs):
    for i in range(3):
        outs[0][i] = ins[0][i]
    outs[0][3] = ins[1][...]


STEPS = [("wide", SWAP), ("dp", ACROSS[1]), ("dp", ACROSS[2]), ("narrow", NEAR), ("narrow", FAR)]


def half_rows(place, a, kept, tall):
    side = lax.rem(place[2], 2) if a == 0 else lax.div(place[2], 2)
    return pl.ds(pl.multiple_of((side if kept else 1 - side) * tall, tall), tall)


def fold_kernel(place, ins, outs):
    tall = outs[0].shape[2]
    for a in range(2):
        keep, send = outs[2 * a], outs[2 * a + 1]
        pairs = [(ins[0].at[3 * a + j], ins[1].at[3 * a + j]) for j in range(3)]
        if a == 0 and len(ins) == 4:
            pairs.append((ins[2], ins[3]))
        for j, (mine, came) in enumerate(pairs):
            for out, kept in ((keep, True), (send, False)):
                rows = half_rows(place, a, kept, tall)
                for b in range(4):
                    out[j, b] = (mine[b, rows, :].astype(F32) + came[b, rows, :].astype(F32)).astype(BF)


def part_kernel(place, ins, outs):
    first = 0
    for a in range(2):
        keep, got = ins[2 * a], ins[2 * a + 1]
        for hop in range(4):
            block = lax.rem(place[0] + 3 - hop, 4)
            for j in range(keep.shape[0]):
                outs[hop][first + j] = (keep[j, block].astype(F32) + got[j, block].astype(F32)).astype(BF)
        first += keep.shape[0]


def stack_kernel(place, ins, outs):
    at = [0, 0]
    for v in ins:
        for j in range(v.shape[0]):
            a = 0 if j < v.shape[0] - 3 else 1
            outs[a][at[a]] = v[j]
            at[a] += 1


def add_kernel(place, ins, outs):
    for i, out in enumerate(outs):
        out[...] = (ins[2 * i][...].astype(F32) + ins[2 * i + 1][...].astype(F32)).astype(out.dtype)


def blocks_kernel(order, extra, place, ins, outs, buf, sems):
    tall = ins[0].shape[1]
    copies = []
    for i, k in enumerate(order):
        for a in range(2):
            mine, away = ins[2 * a], ins[2 * a + 1]
            for j in range(3):
                at = 3 * i + j + (extra if a == 0 and i else 0)
                buf[a, i, j, half_rows(place, a, True, tall), :] = mine[at].astype(F32)
                buf[a, i, j, half_rows(place, a, False, tall), :] = away[at].astype(F32)
            copies.append(pltpu.make_async_copy(buf.at[a, i], outs[a].at[k], sems.at[a, i]))
            copies[-1].start()
    if extra:
        outs[2][half_rows(place, 0, True, tall), :] = ins[0][3]
        outs[2][half_rows(place, 0, False, tall), :] = ins[1][3]
    for copy in copies:
        copy.wait()


def head_rows_kernel(place, ins, outs):
    depth = ins[0].shape[0]
    for hop, v in enumerate(ins):
        row = lax.rem(place[0] + 4 - hop, 4) * depth
        outs[0][pl.ds(pl.multiple_of(row, depth), depth), :] = v[...].astype(F32)


def blocks(turn, order, parts, sections, extra, before=None):
    ins = [("v", v) for v in parts]
    tall, width = parts[0].shape[1:]
    shape = (sections, 3, 2 * tall, width)
    outs = [("a", shape, F32)] * 2 + ([("v", (2 * tall, width), BF)] if extra else [])
    kernel = functools.partial(blocks_kernel, order, extra)
    if before is not None:
        inner = kernel
        kernel = lambda place, ins, outs, *rest: inner(place, ins[:4], outs, *rest)
        ins += [("a", v) for v in before]
    return call(
        kernel,
        turn,
        ins,
        outs,
        "blocks",
        scratch=[pltpu.VMEM((2, len(order)) + shape[1:], F32), pltpu.SemaphoreType.DMA((2, len(order)))],
        aliases={} if before is None else {4: 0, 5: 1},
        limit=10,
    )


CHUNKS = ((0, 1), (1, 2), (3, 2), (5, 1))
VOCAB = 64
AHEAD = (
    "K0 M M W10 R0 M W11 M C0 M N W12 K1 F0 R1 W20 W21 W22 K2 C1 K3 R2 F1 R3 C2 F2 C3 F3"
)
BACK = (
    "B0 G0 B1 F0 G1 B2 P0 F1 G2 H0 B3 P1 F2 H0 G3 H1 H0 B4 P2 F3 H1 G4 H2 H1 B5 P3 F4 H2 L G5 H3 H2 "
    "T F5 P4 T H3 H4 T P5 H3 S0 H4 H5 T A0 H4 H5 T X H5 S1 A1 Y"
)
GROUPS = ((0, 1, 2, 3), (4, 5))


def body(
    numeric,
    cat_index,
    cardinality,
    emb_table,
    input_norm_gain,
    input_norm_bias,
    mask_logit,
    w_feat,
    w_state,
    gate_bias,
    head_w1,
    head_b1,
    head_w2,
    head_b2,
    cotangent,
):
    axes = ("dp", "wide", "narrow")
    rows, num = numeric.shape
    sections = w_feat.shape[0]
    feat = w_feat.shape[2] * lax.axis_size("narrow")
    emb = emb_table.shape[1]
    columns = cat_index.shape[1]
    classes = head_w2.shape[1]
    count = float(rows * lax.axis_size(axes))
    fast = is_fast()
    half = feat // 2
    cat, table = cat_index.T, emb_table.T
    turn = jnp.zeros((8, 128), F32)

    waiting = []

    def run(kernel, ins, outs, name, **more):
        nonlocal turn
        *v, turn = call(kernel, turn, [("v", x) for x in ins], outs, name, awaited=tuple(waiting), **more)
        waiting.clear()
        return v

    if fast:
        arrays = (w_feat, w_state)
        tall = w_feat.shape[2] // 4
        *own, turn = call(
            functools.partial(quarters_kernel, CHUNKS),
            turn,
            [("h", w) for w in arrays],
            [("v", (n, 2, 3, tall, w_feat.shape[3]), BF) for _, n in CHUNKS],
            "quarters",
            scratch=[pltpu.SemaphoreType.DMA((2 * len(CHUNKS),))],
        )
        came = [[along_narrow(v, hops) for hops in (1, 2, 3)] for v in own]
        across = [other_core(w) for w in arrays]
    raw, stats, counts, turn = prepare(turn, numeric, cat, cardinality, table, VOCAB)

    ready = {}
    stored = []
    h = None
    norm = None
    merges = 0

    def do_pack(i):
        ways = (1, 2) if i % 2 == 0 else (2, 1)
        got = run(pack_kernel, came[i], [("v", (3,) + own[i].shape, BF)], "pack")[0]
        ready[i] = ways, got, along_dp(got, ways[0]), along_dp(got, ways[1])

    def do_relay(i):
        ways, got, one, two = ready[i]
        outs = [("v", (4,) + got.shape, BF), ("v", got.shape, BF)]
        parts, one = run(relay_kernel, [got, one, two], outs, "relay")
        ready[i] = ways, parts, along_dp(one, ways[1])

    def do_close(i):
        ways, parts, far = ready[i]
        parts = run(close_kernel, [parts, far], [("v", parts.shape, BF)], "close")[0]
        ready[i] = ways, parts, other_core(parts)

    def do_wait(which):
        waiting.append(came[which // 10][which % 10])

    def do_merge(_):
        nonlocal stats, merges
        axis, way = STEPS[merges]
        kernel = functools.partial(merge_kernel, float(rows * 2**merges))
        stats = run(kernel, [stats, lax.ppermute(stats, axis, way)], [("v", (2, feat), F32)], "merge")[0]
        merges += 1

    def do_norm(_):
        nonlocal norm
        ins = [stats, input_norm_gain.reshape(1, -1), input_norm_bias.reshape(1, -1)]
        norm = run(functools.partial(norm_kernel, count), ins, [("v", (8, feat), F32)], "norm")[0]

    def do_forward(i):
        nonlocal h, weights, saved, turn
        s, n = CHUNKS[i]
        if fast:
            ways, *parts = ready[i]
            copies = Parts(s, n, ways)
            pieces = [("h", w) for w in arrays] + [("h", w) for w in across] + [("a", v) for v in parts]
        else:
            copies, pieces = Whole(), [("h", w[s : s + n]) for w in whole]
        last = i + 1 == len(CHUNKS)
        h, weights, saved, turn = forward_sections(
            copies, s, n, last, turn, raw, h, norm, mask_logit, gate_bias, pieces
        )
        stored.extend((weights, saved, k) for k in range(n))

    weights = saved = None
    if not fast:
        means = lax.all_gather(stats, axes)
        mean = jnp.mean(means[:, 0], 0)
        away = means[:, 0] - mean
        stats = jnp.stack([mean, jnp.sum(means[:, 1], 0) + rows * jnp.sum(away * away, 0)])
        whole = [
            lax.all_gather(lax.all_gather(w, "narrow", axis=2, tiled=True), "wide", axis=3, tiled=True)
            for w in (w_feat, w_state)
        ]
    tasks = {"N": do_norm, "F": do_forward}
    if fast:
        tasks.update(K=do_pack, R=do_relay, C=do_close, M=do_merge, W=do_wait)
    for step in AHEAD.split():
        if step[0] in tasks:
            tasks[step[0]](int(step[1:] or 0))

    dh, logits, grad_w1, grad_w2, grad_b, turn = head(turn, h, head_w1, head_b1, head_w2.T, head_b2, cotangent.T)

    dn = None
    small = [None] * sections
    order = list(reversed(range(sections)))
    flight = {}
    halfway = lambda many: ("v", (many, 4, feat // 8, half), BF)
    flat = lambda many: ("v", (many, feat // 8, half), BF)
    at = layout(sections, classes, emb, columns * VOCAB, feat)
    result = {}

    def do_backward(t):
        nonlocal dh, dn, turn, weights, saved
        k = order[t]
        coming = stored[k - 1] if k else None
        dh, dn, dbuf, lhs, small[k], *rest, turn = backward_section(
            k, turn, raw, saved, norm, mask_logit, weights, dh, dn, coming
        )
        if rest:
            weights, saved = rest
        flight[t] = dbuf, lhs

    def do_gradients(t):
        nonlocal turn
        other, mine, turn = gradients(turn, *flight[t], half)
        flight[t] = [mine, other]
        if fast:
            flight[t] = [mine, other_core(other)]
            if t == 0:
                flight[t] += [grad_w1, other_core(grad_w1)]

    def do_fold(t):
        many = len(flight[t]) // 2 + 2
        v = run(fold_kernel, flight[t], [halfway(many), halfway(many), halfway(3), halfway(3)], "fold")
        flight[t] = [v[0], along_dp(v[1], 1), v[2], along_dp(v[3], 2)]

    def do_part(t):
        many = flight[t][0].shape[0] + 3
        flight[t] = run(part_kernel, flight[t], [flat(many)] * 4, "part")

    def do_hop(t):
        moving, mine, *rest = flight[t]
        moving = run(add_kernel, [along_narrow(moving, 1), mine], [flat(mine.shape[0])], "hop")[0]
        flight[t] = [moving] + rest

    def do_stack(g):
        ins = [flight[t][0] for t in GROUPS[g]]
        state = 3 * len(GROUPS[g])
        feats = sum(v.shape[0] for v in ins) - state
        v = run(stack_kernel, ins, [flat(feats), flat(state)], "stack")
        result[g] = [v[0], along_dp(v[0], 2), v[1], along_dp(v[1], 1)]

    def do_add(g):
        v = run(add_kernel, result[g], [flat(result[g][0].shape[0]), flat(result[g][2].shape[0])], "add")
        result[g] = [v[0], along_dp(v[0], 1), v[1], along_dp(v[1], 2)]

    def do_local(_):
        ins = (raw, cat, dh, dn, norm, counts, grad_w2, grad_b, *small)
        outs = [("v", (at["rows"], feat), F32)]
        result["pack"] = run(
            functools.partial(sums_kernel, VOCAB, 256, at), ins, outs, "local_sums", limit=16, work=WORK
        )[0]
        result["steps"] = 0

    def do_total(_):
        pack = result["pack"]
        axis, way = STEPS[result["steps"]]
        result["pack"] = run(add_kernel, [pack, lax.ppermute(pack, axis, way)], [("v", pack.shape, F32)], "total")[0]
        result["steps"] += 1

    def do_early(_):
        nonlocal turn
        *v, last, turn = blocks(turn, [order[t] for t in GROUPS[0]], result[0], sections, 1)
        result["blocks"] = v
        result["last"] = [last] + [along_narrow(last, hop) for hop in (1, 2, 3)]

    def do_late(_):
        nonlocal turn
        *v, turn = blocks(turn, [order[t] for t in GROUPS[1]], result[1], sections, 0, result["blocks"])
        result["blocks"] = v
        result["last"] = run(head_rows_kernel, result["last"], [("p", (feat, half), F32)], "head_rows")[0]

    tasks = {"B": do_backward, "G": do_gradients, "L": do_local}
    if fast:
        tasks.update(F=do_fold, P=do_part, H=do_hop, S=do_stack, A=do_add, X=do_early, Y=do_late, T=do_total)
    for step in BACK.split():
        if step[0] in tasks:
            tasks[step[0]](int(step[1:] or 0))
    pack = result["pack"]
    if fast:
        grad_feat, grad_state = result["blocks"]
        grad_w1 = result["last"]
    else:
        halves = ([None] * sections, [None] * sections)
        for t in range(sections):
            local = jnp.concatenate(flight[t], axis=3).reshape(6, feat, feat)
            for a in range(2):
                part = lax.psum_scatter(local[3 * a : 3 * a + 3], "wide", scatter_dimension=2, tiled=True)
                part = lax.psum_scatter(part, "narrow", scatter_dimension=1, tiled=True)
                halves[a][order[t]] = lax.psum(part, "dp").astype(F32)
        pack = lax.psum(pack, axes)
        grad_feat, grad_state = (jnp.stack(v) for v in halves)
        grad_w1 = lax.psum(grad_w1.reshape(feat, -1).astype(F32), axes)
    outs = call(
        functools.partial(finish_kernel, VOCAB, count, at),
        turn,
        [("v", v) for v in (dh, dn, raw, norm, pack, table)] + [("s", cardinality)],
        [
            ("p", (rows, num), F32),
            ("p", (emb, table.shape[1]), F32),
            ("p", (1, feat), F32),
            ("p", (1, feat), F32),
            ("p", mask_logit.shape, F32),
            ("p", gate_bias.shape, F32),
            ("p", (1, half), F32),
            ("p", (classes, half), F32),
            ("p", (1, classes), F32),
        ],
        "finish",
        limit=16,
    )
    grad_numeric, grad_table, plain, scaled, grad_mask, grad_bias, grad_b1, grad_w2, grad_b2, _ = outs
    return (
        logits.T,
        grad_numeric,
        grad_table.T,
        scaled.reshape(-1),
        plain.reshape(-1),
        grad_mask,
        grad_feat,
        grad_state,
        grad_bias,
        grad_w1,
        grad_b1.reshape(-1),
        grad_w2.T,
        grad_b2.reshape(-1),
    )


def solution(mesh):
    spread_rows = P(("dp", "wide", "narrow"), None)
    blocked = P(None, None, "narrow", "wide")
    in_specs = (spread_rows, spread_rows) + (P(),) * 5 + (blocked, blocked) + (P(),) * 5 + (spread_rows,)
    out_specs = (spread_rows, spread_rows) + (P(),) * 4 + (blocked, blocked) + (P(),) * 5
    return jax.shard_map(body, mesh=mesh, in_specs=in_specs, out_specs=out_specs, check_vma=False)
```

```python
import functools
import jax
import jax.numpy as jnp
from jax import lax
from jax.experimental import pallas as pl
from jax.experimental.pallas import tpu as pltpu
from jax.sharding import PartitionSpec as P

EPSILON = 1e-05
BF = jnp.bfloat16
F32 = jnp.float32
VMEM = pl.BlockSpec(memory_space=pltpu.VMEM)
SMEM = pl.BlockSpec(memory_space=pltpu.SMEM)
ANY = pl.BlockSpec(memory_space=pl.ANY)
MIB = 2**20
WORK = 3 * 10**10


def mdot(left, right):
    return lax.dot_general(left, right, (((1,), (0,)), ((), ())), preferred_element_type=F32)


def tdot(left, right):
    return lax.dot_general(left, right, (((0,), (0,)), ((), ())), preferred_element_type=F32)


def ndot(left, right):
    return lax.dot_general(left, right, (((1,), (1,)), ((), ())), preferred_element_type=F32)


def sigm(v):
    return 0.5 * jnp.tanh(0.5 * v) + 0.5


def call(kernel, turn, ins, outs, name, scratch=(), aliases=None, limit=4, work=0, awaited=()):
    specs = {"v": VMEM, "p": VMEM, "h": ANY, "a": ANY, "s": SMEM}
    memory = {"v": pltpu.VMEM, "h": pltpu.HBM}
    ins = [("v", turn)] + list(ins)
    used = len(ins)
    ins += [("a", x) for x in awaited]
    outs = [("v", turn.shape, turn.dtype)] + list(outs)
    given = [pltpu.with_memory_space_constraint(x, memory[kind]) if kind in memory else x for kind, x in ins]
    fast = is_fast()

    def shape(kind, dims, dtype):
        return memory[kind](dims, dtype) if kind in memory else jax.ShapeDtypeStruct(dims, dtype)

    def run(*refs):
        place = [lax.axis_index(a) if fast else 0 for a in ("narrow", "wide", "dp")]
        kernel(place, refs[1:used], refs[len(ins) + 1 : len(ins) + len(outs)], *refs[len(ins) + len(outs) :])

    turn, *results = pl.pallas_call(
        run,
        in_specs=[specs[kind] for kind, _ in ins],
        out_specs=[specs[o[0]] for o in outs],
        out_shape=[shape(*o) for o in outs],
        scratch_shapes=list(scratch),
        input_output_aliases={0: 0, **{i + 1: o + 1 for i, o in (aliases or {}).items()}},
        compiler_params=pltpu.CompilerParams(vmem_limit_bytes=limit * MIB),
        cost_estimate=pl.CostEstimate(flops=work, bytes_accessed=0, transcendentals=0),
        name=name,
    )(*given)
    return (*results, turn)


def is_fast():
    return tuple(lax.axis_size(a) for a in ("dp", "wide", "narrow")) == (4, 2, 4)


def forward_kernel(copies, s, n, first, rb, place, ins, outs, weights, saved, sems, outsem):
    raw, norm, mask, bias = ins[:4]
    pieces = ins[4:] if first else ins[5:]
    h_out, stored, kept = outs
    loads = copies.start(place, pieces, weights, sems)
    for copy in loads:
        copy.wait()
    stores = [pltpu.make_async_copy(weights, stored, outsem.at[0, 0])]
    stores[0].start()
    for b in range(raw.shape[0] // rb):
        part = pl.ds(b * rb, rb)
        normed = (raw[part, :].astype(F32) - norm[0:1, :]) * norm[1:2, :] + norm[2:3, :]
        h = normed if first else ins[4][part, :]
        for k in range(n):
            feat = (normed * sigm(mask[s + k : s + k + 1, :])).astype(BF)
            low = h.astype(BF)
            saved[k, 3, part, :] = low
            rpre = mdot(feat, weights[k, 0, 1]) + mdot(low, weights[k, 1, 1]) + bias[s + k, 1:2, :]
            r = sigm(rpre)
            upre = mdot(feat, weights[k, 0, 0]) + mdot(low, weights[k, 1, 0]) + bias[s + k, 0:1, :]
            u = sigm(upre)
            reset = (r * h).astype(BF)
            cpre = mdot(feat, weights[k, 0, 2]) + mdot(reset, weights[k, 1, 2]) + bias[s + k, 2:3, :]
            c = jnp.tanh(cpre)
            h = h + u * (c - h)
            saved[k, 0, part, :] = u.astype(BF)
            saved[k, 1, part, :] = r.astype(BF)
            saved[k, 2, part, :] = c.astype(BF)
            stores.append(pltpu.make_async_copy(saved.at[k, :, part], kept.at[k, :, part], outsem.at[1 + b, k]))
            stores[-1].start()
        h_out[part, :] = h
    for copy in stores:
        copy.wait()


def forward_sections(copies, s, n, turn, raw, h, norm, mask, bias, pieces, awaited, rb=512):
    rows, feat = raw.shape
    first = h is None
    ins = [("v", raw), ("v", norm), ("v", mask), ("v", bias)] + ([] if first else [("v", h)]) + pieces
    whole = (n, 2, 3, feat, feat)
    kept = (n, 4, rows, feat)
    outs = [("v", (rows, feat), F32), ("h", whole, BF), ("h", kept, BF)]
    scratch = [pltpu.VMEM(whole, BF), pltpu.VMEM(kept, BF)]
    scratch += [pltpu.SemaphoreType.DMA((copies.total,)), pltpu.SemaphoreType.DMA((1 + rows // rb, n))]
    return call(
        functools.partial(forward_kernel, copies, s, n, first, rb),
        turn,
        ins,
        outs,
        "forward_sections",
        work=WORK,
        scratch=scratch,
        aliases={} if first else {4: 0},
        limit=12 + 8 * n,
        awaited=awaited,
    )


def fetch(index, sources, targets, sems):
    copies = [
        pltpu.make_async_copy(source.at[pl.ds(index, 1), pl.ds(j, 1)], target.at[:, pl.ds(j, 1)], sems.at[i, j])
        for i, (source, target) in enumerate(zip(sources, targets))
        for j in range(source.shape[1])
    ]
    for copy in copies:
        copy.start()
    return copies


def backward_kernel(s, rb, first, coming, place, ins, outs, sems):
    raw, saved, norm, mask, weights, dh_in = ins[:6]
    dn_in = None if first else ins[6]
    dh_out, dn_out, dbuf, lhs, small = outs[:5]
    loads = [] if coming is None else fetch(coming, ins[-2:], outs[5:], sems)
    rows = raw.shape[0]
    gate_mask = sigm(mask[s : s + 1, :])
    sums = [jnp.zeros((1, gate_mask.shape[1]), F32)] * 4
    for b in range(rows // rb):
        part = pl.ds(b * rb, rb)
        u = saved[0, 0, part, :].astype(F32)
        c = saved[0, 2, part, :].astype(F32)
        dh = dh_in[part, :]
        t = dh * u
        dc = (t * (1.0 - c * c)).astype(BF)
        dreset = ndot(dc, weights[0, 1, 2])
        low = saved[0, 3, part, :]
        h = low.astype(F32)
        du = (t * (c - h) * (1.0 - u)).astype(BF)
        dbuf[2, part, :] = dc
        dbuf[0, part, :] = du
        dfeat = ndot(dc, weights[0, 0, 2]) + ndot(du, weights[0, 0, 0])
        state = ndot(du, weights[0, 1, 0])
        normed = (raw[part, :].astype(F32) - norm[0:1, :]) * norm[1:2, :] + norm[2:3, :]
        feat = (normed * gate_mask).astype(BF)
        r = saved[0, 1, part, :].astype(F32)
        rh = r * h
        dr = (dreset * rh * (1.0 - r)).astype(BF)
        dbuf[1, part, :] = dr
        lhs[0, :, part] = feat.T
        lhs[1, :, part] = low.T
        lhs[2, :, part] = rh.astype(BF).T
        dfeat = dfeat + ndot(dr, weights[0, 0, 1])
        dh_out[part, :] = (dh - t) + dreset * r + state + ndot(dr, weights[0, 1, 1])
        dn_out[part, :] = dfeat * gate_mask if first else dn_in[part, :] + dfeat * gate_mask
        for i, v in enumerate((du.astype(F32), dr.astype(F32), dc.astype(F32), dfeat * normed)):
            sums[i] = sums[i] + jnp.sum(v, 0, keepdims=True)
    slope = gate_mask * (1.0 - gate_mask)
    small[...] = jnp.concatenate(sums[:3] + [sums[3] * slope] + [jnp.zeros_like(slope)] * 4, axis=0)
    for copy in loads:
        copy.wait()


def backward_section(s, turn, raw, saved, norm, mask, weights, dh, dn, coming, rb=256):
    rows, feat = raw.shape
    first = dn is None
    ins = [("v", v) for v in (raw, saved, norm, mask, weights, dh)] + ([] if first else [("v", dn)])
    outs = [("v", (rows, feat), F32)] * 2 + [("v", (3, rows, feat), BF), ("v", (3, feat, rows), BF)]
    outs += [("v", (8, feat), F32)]
    if coming is not None:
        ins += [("h", v) for v in coming[:2]]
        outs += [("v", (1,) + weights.shape[1:], BF), ("v", (1,) + saved.shape[1:], BF)]
    return call(
        functools.partial(backward_kernel, s, rb, first, None if coming is None else coming[2]),
        turn,
        ins,
        outs,
        "backward_section",
        work=WORK,
        scratch=[pltpu.SemaphoreType.DMA((2, 4))],
        aliases={5: 0} if first else {5: 0, 6: 1},
        limit=9,
    )


def gradients_kernel(mine, place, ins, outs):
    dbuf, lhs = ins
    out = outs[0]
    half = out.shape[-1]
    core = place[1] if mine else 1 - place[1]
    columns = pl.ds(pl.multiple_of(core * half, half), half)
    for m in range(6):
        which = 0 if m < 3 else (1 if m < 5 else 2)
        out[m] = mdot(lhs[which], dbuf[m % 3, :, columns]).astype(BF).reshape(out.shape[1:])


class Whole:
    total = 2

    def start(self, place, pieces, weights, sems):
        copies = [pltpu.make_async_copy(pieces[a], weights.at[:, a], sems.at[a]) for a in range(2)]
        for copy in copies:
            copy.start()
        return copies


def spread(table_rows, vocab, offsets, columns):
    row = lax.broadcasted_iota(jnp.int32, (vocab, table_rows), 0)
    lane = lax.broadcasted_iota(jnp.int32, (vocab, table_rows), 1)
    return jnp.concatenate([(lane == row + offsets[c]).astype(BF) for c in range(columns)], axis=0)


def column_offsets(cardinality, columns):
    offsets, total = [], 0
    for c in range(columns):
        offsets.append(total)
        total = total + cardinality[c]
    return offsets


def onehot(cat, vocab):
    columns = cat.shape[0]
    width = columns * vocab
    lane = lax.broadcasted_iota(jnp.int32, (columns, width), 1)
    owner = lax.broadcasted_iota(jnp.int32, (columns, width), 0)
    repeat = (lane // vocab == owner).astype(BF)
    values = tdot(cat.astype(F32).astype(BF), repeat)
    wanted = (lax.broadcasted_iota(jnp.int32, (1, width), 1) % vocab).astype(F32)
    return (values == wanted).astype(BF)


def prepare_kernel(vocab, rb, place, ins, outs):
    numeric, cat, cardinality, table = ins
    raw, stats, counts = outs
    rows, num = numeric.shape
    columns, (emb, table_rows) = cat.shape[0], table.shape
    width = columns * emb
    chosen = spread(table_rows, vocab, column_offsets(cardinality, columns), columns)
    tile = (
        lax.broadcasted_iota(jnp.int32, (emb, width), 1) % emb
        == lax.broadcasted_iota(jnp.int32, (emb, width), 0)
    ).astype(BF)
    placed = mdot(chosen, tdot(table[...], tile).astype(BF))
    own = (
        lax.broadcasted_iota(jnp.int32, placed.shape, 1) // emb
        == lax.broadcasted_iota(jnp.int32, placed.shape, 0) // vocab
    )
    blocks = jnp.where(own, placed, 0.0).astype(BF)
    total = jnp.zeros((1, num + width), F32)
    counted = jnp.zeros((1, columns * vocab), F32)
    for b in range(rows // rb):
        part = pl.ds(b * rb, rb)
        hot = onehot(cat[:, part], vocab)
        looked = mdot(hot, blocks)
        raw[part, :num] = numeric[part, :]
        raw[part, num:] = looked.astype(BF)
        total = total + jnp.concatenate(
            [jnp.sum(numeric[part, :].astype(F32), 0, keepdims=True), jnp.sum(looked, 0, keepdims=True)], axis=1
        )
        counted = counted + mdot(jnp.ones((8, rb), BF), hot)[0:1, :]
    mean = total / rows
    squares = jnp.zeros_like(total)
    for b in range(rows // rb):
        away = raw[pl.ds(b * rb, rb), :].astype(F32) - mean
        squares = squares + jnp.sum(away * away, 0, keepdims=True)
    stats[0:1, :] = mean
    stats[1:2, :] = squares
    counts[...] = counted


def prepare(turn, numeric, cat, cardinality, table, vocab):
    rows, num = numeric.shape
    feat = num + cat.shape[0] * table.shape[0]
    return call(
        functools.partial(prepare_kernel, vocab, 256),
        turn,
        [("v", numeric), ("v", cat), ("s", cardinality), ("v", table)],
        [("v", (rows, feat), BF), ("v", (2, feat), F32), ("v", (1, cat.shape[0] * vocab), F32)],
        "prepare",
        work=WORK,
        limit=24,
    )


def merge_kernel(count, place, ins, outs):
    one, two = ins
    out = outs[0]
    apart = one[0:1, :] - two[0:1, :]
    out[0:1, :] = 0.5 * (one[0:1, :] + two[0:1, :])
    out[1:2, :] = one[1:2, :] + two[1:2, :] + apart * apart * (0.5 * count)


def norm_kernel(count, place, ins, outs):
    stats, gain, bias = ins
    out = outs[0]
    inverse = lax.rsqrt(stats[1:2, :] / count + EPSILON)
    out[0:1, :] = stats[0:1, :]
    out[1:2, :] = inverse * gain[...]
    out[2:3, :] = bias[...]
    out[3:4, :] = inverse
    out[4:5, :] = gain[...]
    out[5:8, :] = jnp.zeros((3, inverse.shape[1]), F32)


def head_kernel(rb, coming, place, ins, outs, hidden, slopes, sems):
    h, w1, b1, w2, b2, g = ins[:6]
    dh, logits, grad_w1, grad_w2, grad_b = outs[:5]
    loads = fetch(coming, ins[6:], outs[5:], sems)
    rows = h.shape[0]
    width = w1.shape[1]
    classes = w2.shape[0]
    eye = lax.broadcasted_iota(jnp.int32, (classes, classes), 0) == lax.broadcasted_iota(
        jnp.int32, (classes, classes), 1
    )
    shift = jnp.sum(jnp.where(eye, b2[...], 0.0), 1, keepdims=True)
    two = jnp.zeros(w2.shape, F32)
    sums = jnp.zeros((1, width), F32)
    for b in range(rows // rb):
        part = pl.ds(b * rb, rb)
        head_in = h[part, :].astype(BF)
        hidden[part, :] = head_in
        x = mdot(head_in, w1[...]) + b1[...]
        phi = 0.5 * (1.0 + lax.erf(x * 0.7071067811865476))
        act = (x * phi).astype(BF)
        logits[:, part] = ndot(w2[...], act) + shift
        dact = tdot(g[:, part], w2[...])
        slope = phi + x * (jnp.exp(-0.5 * x * x) * 0.3989422804014327)
        dx = (dact * slope).astype(BF)
        slopes[part, :] = dx
        dh[part, :] = ndot(dx, w1[...])
        two = two + mdot(g[:, part], act)
        sums = sums + jnp.sum(dx.astype(F32), 0, keepdims=True)
    one = tdot(hidden[...], slopes[...]).astype(BF)
    depth = grad_w1.shape[1]
    for i in range(grad_w1.shape[0]):
        grad_w1[i] = one[i * depth : (i + 1) * depth]
    grad_w2[...] = two
    grad_b[...] = jnp.zeros_like(grad_b)
    grad_b[0:1, :] = sums
    grad_b[1:2, : g.shape[0]] = ndot(jnp.ones((8, rows), BF), g[...])[0:1, :]
    for copy in loads:
        copy.wait()


def head(turn, h, w1, b1, w2, b2, g, coming):
    rows, feat = h.shape
    classes, hidden = w2.shape
    return call(
        functools.partial(head_kernel, 256, coming[2]),
        turn,
        [("v", v) for v in (h, w1, b1.reshape(1, -1), w2, b2.reshape(1, -1), g)] + [("h", v) for v in coming[:2]],
        [
            ("v", (rows, feat), F32),
            ("p", (classes, rows), F32),
            ("v", (4, feat // 4, hidden), BF),
            ("v", (classes, hidden), F32),
            ("v", (8, hidden), F32),
        ]
        + [("v", (1,) + v.shape[1:], BF) for v in coming[:2]],
        "head",
        work=WORK,
        scratch=[pltpu.VMEM((rows, feat), BF), pltpu.VMEM((rows, hidden), BF), pltpu.SemaphoreType.DMA((2, 4))],
        aliases={0: 0},
        limit=16,
    )


def layout(sections, classes, emb, width, feat):
    at = {"sums": 0, "small": 2}
    at["bias"] = at["small"] + 4 * sections
    at["w2"] = at["bias"] + 1
    at["counts"] = at["w2"] + -(-classes // 2)
    at["table"] = -(-(at["counts"] + width // feat) // 8) * 8
    at["rows"] = at["table"] + emb * width // feat
    return at


def sums_kernel(vocab, rb, at, place, ins, outs):
    raw, cat, dh, dn, norm, counts, grad_w2, grad_b = ins[:8]
    small = ins[8:]
    pack = outs[0]
    rows, feat = raw.shape
    columns = cat.shape[0]
    width = columns * vocab
    emb = (pack.shape[0] - at["table"]) * feat // width
    num = feat - columns * emb
    plain = jnp.zeros((1, feat), F32)
    scaled = jnp.zeros((1, feat), F32)
    crossed = jnp.zeros((columns * emb, width), F32)
    for b in range(rows // rb):
        part = pl.ds(b * rb, rb)
        grad = dh[part, :] + dn[part, :]
        away = raw[part, :].astype(F32) - norm[0:1, :]
        plain = plain + jnp.sum(grad, 0, keepdims=True)
        scaled = scaled + jnp.sum(grad * away, 0, keepdims=True)
        hot = onehot(cat[:, part], vocab)
        pieces = grad[:, num:]
        high = pieces.astype(BF)
        rest = (pieces - high.astype(F32)).astype(BF)
        crossed = crossed + tdot(high, hot) + tdot(rest, hot)
    own = (
        lax.broadcasted_iota(jnp.int32, crossed.shape, 0) // emb
        == lax.broadcasted_iota(jnp.int32, crossed.shape, 1) // vocab
    )
    crossed = jnp.where(own, crossed, 0.0)
    table = crossed[:emb]
    for c in range(1, columns):
        table = table + crossed[c * emb : (c + 1) * emb]
    pack[...] = jnp.zeros_like(pack)
    pack[0:1, :] = plain
    pack[1:2, :] = scaled * norm[3:4, :]
    for k, v in enumerate(small):
        pack[at["small"] + 4 * k : at["small"] + 4 * k + 4, :] = v[:4, :]
    half = feat // 2
    pack[at["bias"] : at["bias"] + 1, :half] = grad_b[0:1, :]
    pack[at["bias"] : at["bias"] + 1, half:] = grad_b[1:2, :]
    for i in range(grad_w2.shape[0]):
        row = at["w2"] + i // 2
        pack[row : row + 1, (i % 2) * half : (i % 2 + 1) * half] = grad_w2[i : i + 1, :]
    for i in range(width // feat):
        pack[at["counts"] + i : at["counts"] + i + 1, :] = counts[:, i * feat : (i + 1) * feat]
        pack[at["table"] + i * emb : at["table"] + (i + 1) * emb, :] = table[:, i * feat : (i + 1) * feat]


def exact_dot(left, right):
    high = left.astype(BF)
    left = left - high.astype(F32)
    middle = left.astype(BF)
    low = (left - middle.astype(F32)).astype(BF)
    return mdot(high, right) + mdot(middle, right) + mdot(low, right)


def finish_kernel(vocab, count, at, place, ins, outs):
    dh, dn, raw, norm, pack, table, cardinality = ins
    grad, grad_table, plain_out, scaled_out, grad_mask, grad_bias, grad_b1, grad_w2, grad_b2 = outs
    feat = raw.shape[1]
    num = grad.shape[1]
    emb, table_rows = table.shape
    columns = (feat - num) // emb
    width = columns * vocab
    mean, inverse, gain = norm[0:1, :], norm[3:4, :], norm[4:5, :]
    plain_out[...] = pack[0:1, :]
    scaled_out[...] = pack[1:2, :]
    plain = pack[0:1, :] / count
    scaled = pack[1:2, :] / count
    factor = gain * inverse
    for b in range(raw.shape[0] // 256):
        part = pl.ds(b * 256, 256)
        away = (raw[part, :num].astype(F32) - mean[:, :num]) * inverse[:, :num]
        both = dh[part, :num] + dn[part, :num]
        grad[part, :] = factor[:, :num] * (both - plain[:, :num] - away * scaled[:, :num])
    for k in range(grad_mask.shape[0]):
        rows = pack[at["small"] + 4 * k : at["small"] + 4 * k + 4, :]
        grad_bias[k] = rows[:3]
        grad_mask[k : k + 1, :] = rows[3:4]
    half = feat // 2
    grad_b1[...] = pack[at["bias"] : at["bias"] + 1, :half]
    grad_b2[...] = pack[at["bias"] : at["bias"] + 1, half : half + grad_b2.shape[1]]
    for i in range(grad_w2.shape[0]):
        row = at["w2"] + i // 2
        grad_w2[i : i + 1, :] = pack[row : row + 1, (i % 2) * half : (i % 2 + 1) * half]
    flat = columns * emb
    mine = (
        lax.broadcasted_iota(jnp.int32, (emb, flat), 1) % emb
        == lax.broadcasted_iota(jnp.int32, (emb, flat), 0)
    )
    expand = (
        lax.broadcasted_iota(jnp.int32, (flat, width), 0) // emb
        == lax.broadcasted_iota(jnp.int32, (flat, width), 1) // vocab
    ).astype(BF)
    vectors = [jnp.where(mine, v[:, num:], 0.0) for v in (mean, inverse, plain, scaled, factor)]
    wide = exact_dot(jnp.concatenate(vectors, axis=0), expand)
    mean_w, inverse_w, plain_w, scaled_w, factor_w = [wide[i * emb : (i + 1) * emb] for i in range(5)]
    chosen = spread(table_rows, vocab, column_offsets(cardinality, columns), columns)
    away = (ndot(table[...], chosen) - mean_w) * inverse_w
    steps = range(width // feat)
    counts = jnp.concatenate([pack[at["counts"] + i : at["counts"] + i + 1, :] for i in steps], axis=1)
    sums = jnp.concatenate([pack[at["table"] + i * emb : at["table"] + (i + 1) * emb, :] for i in steps], axis=1)
    grad_table[...] = exact_dot(factor_w * (sums - counts * (plain_w + away * scaled_w)), chosen)


class Parts:
    def __init__(self, s, n, slots):
        self.s, self.n, self.slots = s, n, slots
        self.total = 4 + 2 * len(slots)

    def start(self, place, pieces, weights, sems):
        depth, width = pieces[0].shape[2:]
        tall = depth // 4
        z, c, d = place[0], place[1], place[2]
        copies = []

        def add(source, arrays, row, rows, core):
            column = (c if core == 0 else 1 - c) * width
            copies.append(
                pltpu.make_async_copy(
                    source,
                    weights.at[
                        :,
                        arrays,
                        :,
                        pl.ds(pl.multiple_of(row, rows), rows),
                        pl.ds(pl.multiple_of(column, width), width),
                    ],
                    sems.at[len(copies)],
                )
            )

        for core in range(2):
            for a in range(2):
                add(pieces[2 * core + a].at[pl.ds(self.s, self.n)], a, z * depth, depth, core)
        for bundle, slot, hops, way in self.slots:
            quarter = lax.bitwise_xor(d, way) if way else d
            row = lax.rem(z + 4 - hops, 4) * depth + quarter * tall
            for core in range(2):
                add(pieces[4 + 2 * bundle + core].at[slot], slice(None), row, tall, core)
        for copy in copies:
            copy.start()
        return copies


SWAP = [(0, 1), (1, 0)]
ACROSS = {1: [(0, 1), (1, 0), (2, 3), (3, 2)], 2: [(0, 2), (2, 0), (1, 3), (3, 1)]}
NEAR = [(0, 1), (1, 0), (2, 3), (3, 2)]
FAR = [(0, 2), (1, 3), (2, 0), (3, 1)]


def other_core(v):
    return lax.ppermute(v, "wide", SWAP)


def along_dp(v, way):
    return lax.ppermute(v, "dp", ACROSS[way])


def along_narrow(v, hops):
    return lax.ppermute(v, "narrow", [(i, (i + hops) % 4) for i in range(4)])


def quarters_kernel(place, ins, outs, sems):
    tall = ins[0].shape[2] // 4
    rows = pl.ds(pl.multiple_of(place[2] * tall, tall), tall)
    copies = []
    for (s, n), out in zip(CHUNKS, outs):
        for a in range(2):
            copies.append(
                pltpu.make_async_copy(ins[a].at[pl.ds(s, n), :, rows], out.at[:, a], sems.at[len(copies)])
            )
    for copy in copies:
        copy.start()
    for copy in copies:
        copy.wait()


def bundle_kernel(kinds, place, ins, outs):
    ins, bundle, outs = list(ins), outs[0], list(outs[1:])
    slot = 0
    for kind in kinds:
        if kind == "K":
            block = ins.pop(0)[...]
            bundle[slot] = block
            outs.pop(0)[...] = block
            slot += 1
        elif kind == "X":
            for a in range(2):
                block = ins.pop(0)
                bundle[slot + a] = block[...]
                outs.pop(0)[...] = block[:, a]
            slot += 2
        else:
            for a in range(2):
                bundle[slot, :, a] = ins.pop(0)[...]
            slot += 1


STEPS = [("wide", SWAP), ("dp", ACROSS[1]), ("dp", ACROSS[2]), ("narrow", NEAR), ("narrow", FAR)]


def half_rows(place, a, kept, tall):
    side = lax.rem(place[2], 2) if a == 0 else lax.div(place[2], 2)
    return pl.ds(pl.multiple_of((side if kept else 1 - side) * tall, tall), tall)


def fold_kernel(place, ins, outs):
    tall = outs[0].shape[2]
    for a in range(2):
        keep, send = outs[2 * a], outs[2 * a + 1]
        pairs = [(ins[0].at[3 * a + j], ins[1].at[3 * a + j]) for j in range(3)]
        if a == 0 and len(ins) == 4:
            pairs.append((ins[2], ins[3]))
        for j, (mine, came) in enumerate(pairs):
            for out, kept in ((keep, True), (send, False)):
                rows = half_rows(place, a, kept, tall)
                for b in range(4):
                    out[j, b] = (mine[b, rows, :].astype(F32) + came[b, rows, :].astype(F32)).astype(BF)


def ring_kernel(active, new, place, ins, outs):
    ins, outs = list(ins), list(outs)
    came = ins.pop(0) if active else None
    on = outs.pop(0) if new or not all(last for _, last in active) else None
    source = target = 0
    for many, last in active:
        mine = ins.pop(0)
        out, first = (outs.pop(0), 0) if last else (on, target)
        for j in range(many):
            out[first + j] = (came[source + j].astype(F32) + mine[j].astype(F32)).astype(BF)
        source += many
        target += 0 if last else many
    for feats in new:
        stages = [(on, target)] + [(outs.pop(0), 0) for _ in range(3)]
        done = 0
        for many in (feats, 3):
            keep, got = ins.pop(0), ins.pop(0)
            for hop, (out, first) in enumerate(stages):
                block = lax.rem(place[0] + 3 - hop, 4)
                for j in range(many):
                    total = keep[j, block].astype(F32) + got[j, block].astype(F32)
                    out[first + done + j] = total.astype(BF)
            done += many
        target += done


def stack_kernel(place, ins, outs):
    at = [0, 0]
    for v in ins:
        for j in range(v.shape[0]):
            a = 0 if j < v.shape[0] - 3 else 1
            outs[a][at[a]] = v[j]
            at[a] += 1


def add_kernel(place, ins, outs):
    for i, out in enumerate(outs):
        out[...] = (ins[2 * i][...].astype(F32) + ins[2 * i + 1][...].astype(F32)).astype(out.dtype)


def blocks_kernel(order, extra, place, ins, outs, buf, sems):
    tall = ins[0].shape[1]
    copies = []
    for i, k in enumerate(order):
        for a in range(2):
            mine, away = ins[2 * a], ins[2 * a + 1]
            for j in range(3):
                at = 3 * i + j + (extra if a == 0 and i else 0)
                buf[a, i, j, half_rows(place, a, True, tall), :] = mine[at].astype(F32)
                buf[a, i, j, half_rows(place, a, False, tall), :] = away[at].astype(F32)
            copies.append(pltpu.make_async_copy(buf.at[a, i], outs[a].at[k], sems.at[a, i]))
            copies[-1].start()
    if extra:
        outs[2][half_rows(place, 0, True, tall), :] = ins[0][3]
        outs[2][half_rows(place, 0, False, tall), :] = ins[1][3]
    for copy in copies:
        copy.wait()


def head_rows_kernel(place, ins, outs):
    depth = ins[0].shape[0]
    for hop, v in enumerate(ins):
        row = lax.rem(place[0] + 4 - hop, 4) * depth
        outs[0][pl.ds(pl.multiple_of(row, depth), depth), :] = v[...].astype(F32)


def blocks(turn, order, parts, sections, extra, before=None):
    ins = [("v", v) for v in parts]
    tall, width = parts[0].shape[1:]
    shape = (sections, 3, 2 * tall, width)
    outs = [("a", shape, F32)] * 2 + ([("v", (2 * tall, width), BF)] if extra else [])
    kernel = functools.partial(blocks_kernel, order, extra)
    if before is not None:
        inner = kernel
        kernel = lambda place, ins, outs, *rest: inner(place, ins[:4], outs, *rest)
        ins += [("a", v) for v in before]
    return call(
        kernel,
        turn,
        ins,
        outs,
        "blocks",
        scratch=[pltpu.VMEM((2, len(order)) + shape[1:], F32), pltpu.SemaphoreType.DMA((2, len(order)))],
        aliases={} if before is None else {4: 0, 5: 1},
        limit=10,
    )


CHUNKS = ((0, 3), (3, 3))
VOCAB = 64
AHEAD = "M+K00 K10+X00+M K20+X10+D00+K01+M X20+D10+K11+M D20+K21+X01+M N F0 X11+X21+D01 D11+D21 F1"
BACK = (
    "B0 G0 g0 F0 B1 G1 g1 F1+R0 B2 G2 g2 F2+R1 B3 G3 g3 F3+R2 B4 G4 g4 F4+R3 B5 G5 L g5 F5+R4+T R5+T R+T S0 "
    "R+A0+T R+T S1 X0 Z Y A1 X1"
)
GROUPS = ((0, 1, 2, 3), (4, 5))


def body(
    numeric,
    cat_index,
    cardinality,
    emb_table,
    input_norm_gain,
    input_norm_bias,
    mask_logit,
    w_feat,
    w_state,
    gate_bias,
    head_w1,
    head_b1,
    head_w2,
    head_b2,
    cotangent,
):
    axes = ("dp", "wide", "narrow")
    rows, num = numeric.shape
    sections = w_feat.shape[0]
    feat = w_feat.shape[2] * lax.axis_size("narrow")
    emb = emb_table.shape[1]
    columns = cat_index.shape[1]
    classes = head_w2.shape[1]
    count = float(rows * lax.axis_size(axes))
    fast = is_fast()
    half = feat // 2
    cat, table = cat_index.T, emb_table.T
    turn = jnp.zeros((8, 128), F32)

    waiting = []

    def run(kernel, ins, outs, name, **more):
        nonlocal turn
        *v, turn = call(kernel, turn, [("v", x) for x in ins], outs, name, awaited=tuple(waiting), **more)
        waiting.clear()
        return v

    def together(jobs):
        asked = [next(job) for job in jobs]

        def kernel(place, ins, outs):
            for one, sources, targets in asked:
                one(place, ins[: len(sources)], outs[: len(targets)])
                ins, outs = ins[len(sources) :], outs[len(targets) :]

        results = run(kernel, [v for a in asked for v in a[1]], [v for a in asked for v in a[2]], "step")
        for job, (_, _, targets) in zip(jobs, asked):
            try:
                job.send(results[: len(targets)])
            except StopIteration:
                pass
            results = results[len(targets) :]
        run(lambda place, ins, outs: None, [], [], "pause", work=WORK)

    if fast:
        arrays = (w_feat, w_state)
        tall = w_feat.shape[2] // 4
        *quarters, turn = call(
            quarters_kernel,
            turn,
            [("h", w) for w in arrays],
            [("v", (n, 2, 3, tall, w_feat.shape[3]), BF) for _, n in CHUNKS],
            "quarters",
            scratch=[pltpu.SemaphoreType.DMA((2 * len(CHUNKS),))],
        )
        came = {(0, g): along_narrow(v, 1) for g, v in enumerate(quarters)}
        across = [other_core(w) for w in arrays]
    raw, stats, counts, turn = prepare(turn, numeric, cat, cardinality, table, VOCAB)

    crossed, far = {}, {}
    slots = [[] for _ in CHUNKS]
    bundles = [[] for _ in CHUNKS]
    stored = []
    h = None
    norm = None
    merges = 0

    def collect(g, steps):
        ins, where, more = [], [], []
        block = quarters[g].shape
        for kind, hop in steps:
            ins += [came[hop, g]] if kind == "K" else crossed[hop, g] if kind == "X" else far[hop, g]
            where += [(hop + 1, way) for way in {"K": (0,), "X": (1, 2), "D": (3,)}[kind]]
            more += {"K": [block], "X": [block[:1] + block[2:]] * 2, "D": []}[kind]
        outs = [("v", (len(where),) + block, BF)] + [("v", v, BF) for v in more]
        bundle, *more = yield functools.partial(bundle_kernel, [kind for kind, _ in steps]), ins, outs
        slots[g] += [(len(bundles[g]), i) + at for i, at in enumerate(where)]
        bundles[g].append((bundle, other_core(bundle)))
        for kind, hop in steps:
            if kind == "K":
                got = more.pop(0)
                crossed[hop, g] = [along_dp(got, way) for way in (1, 2)]
                if hop < 2:
                    came[hop + 1, g] = along_narrow(got, 1)
            elif kind == "X":
                far[hop, g] = [along_dp(more.pop(0), way) for way in (2, 1)]

    def do_merge():
        nonlocal stats, merges
        axis, way = STEPS[merges]
        kernel = functools.partial(merge_kernel, float(rows * 2**merges))
        merges += 1
        (stats,) = yield kernel, [stats, lax.ppermute(stats, axis, way)], [("v", (2, feat), F32)]

    def advance(step):
        parts = step.split("+")
        jobs = [do_merge()] if "M" in parts else []
        for g in range(len(CHUNKS)):
            steps = [(v[0], int(v[1])) for v in parts if v != "M" and int(v[2]) == g]
            jobs += [collect(g, steps)] if steps else []
        together(jobs)

    def do_norm(_):
        nonlocal norm
        ins = [stats, input_norm_gain.reshape(1, -1), input_norm_bias.reshape(1, -1)]
        norm = run(functools.partial(norm_kernel, count), ins, [("v", (8, feat), F32)], "norm")[0]

    def do_forward(i):
        nonlocal h, turn
        s, n = CHUNKS[i]
        if fast:
            copies = Parts(s, n, slots[i])
            pieces = [("h", w) for w in arrays] + [("h", w) for w in across]
            pieces += [("a", v) for pair in bundles[i] for v in pair]
        else:
            copies, pieces = Whole(), [("h", w[s : s + n]) for w in whole]
        h, *held, turn = forward_sections(
            copies, s, n, turn, raw, h, norm, mask_logit, gate_bias, pieces, tuple(waiting)
        )
        waiting.clear()
        stored.extend((held[0], held[1], k) for k in range(n))

    if not fast:
        means = lax.all_gather(stats, axes)
        mean = jnp.mean(means[:, 0], 0)
        away = means[:, 0] - mean
        stats = jnp.stack([mean, jnp.sum(means[:, 1], 0) + rows * jnp.sum(away * away, 0)])
        whole = [
            lax.all_gather(lax.all_gather(w, "narrow", axis=2, tiled=True), "wide", axis=3, tiled=True)
            for w in (w_feat, w_state)
        ]
    for step in AHEAD.split():
        if step == "N":
            do_norm(0)
        elif step[0] == "F":
            do_forward(int(step[1:]))
        elif fast:
            advance(step)

    dh, logits, grad_w1, grad_w2, grad_b, weights, saved, turn = head(
        turn, h, head_w1, head_b1, head_w2.T, head_b2, cotangent.T, stored[-1]
    )

    dn = None
    small = [None] * sections
    order = list(reversed(range(sections)))
    flight = {}
    halfway = lambda many: ("v", (many, 4, feat // 8, half), BF)
    flat = lambda many: ("v", (many, feat // 8, half), BF)
    at = layout(sections, classes, emb, columns * VOCAB, feat)
    result = {}

    def do_backward(t):
        nonlocal dh, dn, turn, weights, saved
        k = order[t]
        coming = stored[k - 1] if k else None
        dh, dn, dbuf, lhs, small[k], *rest, turn = backward_section(
            k, turn, raw, saved, norm, mask_logit, weights, dh, dn, coming
        )
        if rest:
            weights, saved = rest
        flight[t] = dbuf, lhs

    def columns(t, mine):
        kernel = functools.partial(gradients_kernel, mine)
        outs = [("v", (6, 4, feat // 4, half), BF)]
        return run(kernel, flight[t], outs, "gradients", limit=8, work=WORK)[0]

    def do_other(t):
        other = columns(t, False)
        if fast:
            other = other_core(other)
        flight[t] = flight[t], other

    def do_mine(t):
        flight[t], other = flight[t]
        flight[t] = [columns(t, True), other]
        if fast and t == 0:
            flight[t] += [grad_w1, other_core(grad_w1)]

    def do_fold(t):
        many = len(flight[t]) // 2 + 2
        v = yield fold_kernel, flight[t], [halfway(many), halfway(many), halfway(3), halfway(3)]
        flight[t] = [v[0], along_dp(v[1], 1), v[2], along_dp(v[3], 2)]

    ring = {"moving": None, "active": []}

    def do_ring(t):
        active = ring["active"]
        ins = [along_narrow(ring["moving"], 1)] if active else []
        ins += [parts[0] for _, parts in active]
        feats = [] if t is None else [flight[t][0].shape[0]]
        ins += [] if t is None else flight[t]
        going = sum(parts[0].shape[0] for _, parts in active if len(parts) > 1) + sum(v + 3 for v in feats)
        ended = [(k, parts[0].shape[0]) for k, parts in active if len(parts) == 1]
        outs = ([flat(going)] if going else []) + [flat(many) for _, many in ended]
        outs += [flat(v + 3) for v in feats for _ in range(3)]
        sizes = [(parts[0].shape[0], len(parts) == 1) for _, parts in active]
        v = yield functools.partial(ring_kernel, sizes, feats), ins, outs
        ring["moving"] = v.pop(0) if going else None
        flight.update((k, [v.pop(0)]) for k, _ in ended)
        ring["active"] = [(k, parts[1:]) for k, parts in active if len(parts) > 1]
        ring["active"] += [] if t is None else [(t, v)]

    def do_stack(g):
        ins = [flight[t][0] for t in GROUPS[g]]
        state = 3 * len(GROUPS[g])
        feats = sum(v.shape[0] for v in ins) - state
        v = yield stack_kernel, ins, [flat(feats), flat(state)]
        result[g] = [v[0], along_dp(v[0], 2), v[1], along_dp(v[1], 1)]

    def do_add(g):
        v = yield add_kernel, result[g], [flat(result[g][0].shape[0]), flat(result[g][2].shape[0])]
        result[g] = [v[0], along_dp(v[0], 1), v[1], along_dp(v[1], 2)]

    def do_local(_):
        ins = (raw, cat, dh, dn, norm, counts, grad_w2, grad_b, *small)
        outs = [("v", (at["rows"], feat), F32)]
        result["pack"] = run(
            functools.partial(sums_kernel, VOCAB, 256, at), ins, outs, "local_sums", limit=16, work=WORK
        )[0]
        result["steps"] = 0

    def do_total(_):
        pack = result["pack"]
        axis, way = STEPS[result["steps"]]
        result["steps"] += 1
        (result["pack"],) = yield add_kernel, [pack, lax.ppermute(pack, axis, way)], [("v", pack.shape, F32)]

    def do_blocks(g):
        nonlocal turn
        sectioned = [order[t] for t in GROUPS[g]]
        before = result.get("blocks")
        *v, turn = blocks(turn, sectioned, result[g], sections, 1 if g == 0 else 0, before)
        result["blocks"] = v[:2]
        if g == 0:
            result["last"] = [v[2]] + [along_narrow(v[2], hop) for hop in (1, 2, 3)]

    def do_head_rows(_):
        result["last"] = run(head_rows_kernel, result["last"], [("p", (feat, half), F32)], "head_rows")[0]

    def do_finish(_):
        nonlocal turn
        *result["finish"], turn = call(
            functools.partial(finish_kernel, VOCAB, count, at),
            turn,
            [("v", v) for v in (dh, dn, raw, norm, result["pack"], table)] + [("s", cardinality)],
            [
                ("p", (rows, num), F32),
                ("p", (emb, table.shape[1]), F32),
                ("p", (1, feat), F32),
                ("p", (1, feat), F32),
                ("p", mask_logit.shape, F32),
                ("p", gate_bias.shape, F32),
                ("p", (1, half), F32),
                ("p", (classes, half), F32),
                ("p", (1, classes), F32),
            ],
            "finish",
            limit=16,
            work=WORK,
        )

    tasks = {"B": do_backward, "G": do_other, "g": do_mine, "L": do_local}
    if fast:
        tasks.update(X=do_blocks, Y=do_head_rows, Z=do_finish)
    steps = dict(F=do_fold, R=do_ring, S=do_stack, A=do_add, T=do_total)
    for step in BACK.split():
        if step[0] in tasks:
            tasks[step[0]](int(step[1:] or 0))
        elif fast and step[0] in steps:
            together([steps[v[0]](int(v[1:]) if v[1:] else None) for v in step.split("+")])
    if fast:
        grad_feat, grad_state = result["blocks"]
        grad_w1 = result["last"]
    else:
        halves = ([None] * sections, [None] * sections)
        for t in range(sections):
            local = jnp.concatenate(flight[t], axis=3).reshape(6, feat, feat)
            for a in range(2):
                part = lax.psum_scatter(local[3 * a : 3 * a + 3], "wide", scatter_dimension=2, tiled=True)
                part = lax.psum_scatter(part, "narrow", scatter_dimension=1, tiled=True)
                halves[a][order[t]] = lax.psum(part, "dp").astype(F32)
        result["pack"] = lax.psum(result["pack"], axes)
        do_finish(0)
        grad_feat, grad_state = (jnp.stack(v) for v in halves)
        grad_w1 = lax.psum(grad_w1.reshape(feat, -1).astype(F32), axes)
    grad_numeric, grad_table, plain, scaled, grad_mask, grad_bias, grad_b1, grad_w2, grad_b2 = result["finish"]
    return (
        logits.T,
        grad_numeric,
        grad_table.T,
        scaled.reshape(-1),
        plain.reshape(-1),
        grad_mask,
        grad_feat,
        grad_state,
        grad_bias,
        grad_w1,
        grad_b1.reshape(-1),
        grad_w2.T,
        grad_b2.reshape(-1),
    )


def solution(mesh):
    spread_rows = P(("dp", "wide", "narrow"), None)
    blocked = P(None, None, "narrow", "wide")
    in_specs = (spread_rows, spread_rows) + (P(),) * 5 + (blocked, blocked) + (P(),) * 5 + (spread_rows,)
    out_specs = (spread_rows, spread_rows) + (P(),) * 4 + (blocked, blocked) + (P(),) * 5
    return jax.shard_map(body, mesh=mesh, in_specs=in_specs, out_specs=out_specs, check_vma=False)
```

```python
import functools
import jax
import jax.numpy as jnp
from jax import lax
from jax.experimental import pallas as pl
from jax.experimental.pallas import tpu as pltpu
from jax.sharding import PartitionSpec as P

EPSILON = 1e-05
BF = jnp.bfloat16
F32 = jnp.float32
VMEM = pl.BlockSpec(memory_space=pltpu.VMEM)
SMEM = pl.BlockSpec(memory_space=pltpu.SMEM)
ANY = pl.BlockSpec(memory_space=pl.ANY)
MIB = 2**20
WORK = 3 * 10**10


def mdot(left, right):
    return lax.dot_general(left, right, (((1,), (0,)), ((), ())), preferred_element_type=F32)


def tdot(left, right):
    return lax.dot_general(left, right, (((0,), (0,)), ((), ())), preferred_element_type=F32)


def ndot(left, right):
    return lax.dot_general(left, right, (((1,), (1,)), ((), ())), preferred_element_type=F32)


def sigm(v):
    return 0.5 * jnp.tanh(0.5 * v) + 0.5


def call(kernel, turn, ins, outs, name, scratch=(), aliases=None, limit=4, work=0, awaited=()):
    specs = {"v": VMEM, "p": VMEM, "h": ANY, "a": ANY, "s": SMEM}
    memory = {"v": pltpu.VMEM, "h": pltpu.HBM}
    ins = [("v", turn)] + list(ins)
    used = len(ins)
    ins += [("a", x) for x in awaited]
    outs = [("v", turn.shape, turn.dtype)] + list(outs)
    given = [pltpu.with_memory_space_constraint(x, memory[kind]) if kind in memory else x for kind, x in ins]
    fast = is_fast()

    def shape(kind, dims, dtype):
        return memory[kind](dims, dtype) if kind in memory else jax.ShapeDtypeStruct(dims, dtype)

    def run(*refs):
        place = [lax.axis_index(a) if fast else 0 for a in ("narrow", "wide", "dp")]
        kernel(place, refs[1:used], refs[len(ins) + 1 : len(ins) + len(outs)], *refs[len(ins) + len(outs) :])

    turn, *results = pl.pallas_call(
        run,
        in_specs=[specs[kind] for kind, _ in ins],
        out_specs=[specs[o[0]] for o in outs],
        out_shape=[shape(*o) for o in outs],
        scratch_shapes=list(scratch),
        input_output_aliases={0: 0, **{i + 1: o + 1 for i, o in (aliases or {}).items()}},
        compiler_params=pltpu.CompilerParams(vmem_limit_bytes=limit * MIB),
        cost_estimate=pl.CostEstimate(flops=work, bytes_accessed=0, transcendentals=0),
        name=name,
    )(*given)
    return (*results, turn)


def is_fast():
    return tuple(lax.axis_size(a) for a in ("dp", "wide", "narrow")) == (4, 2, 4)


def forward_kernel(copies, s, n, first, keep, rb, place, ins, outs, weights, results, sems, outsem):
    raw, norm, mask, bias = ins[:4]
    pieces = ins[4:] if first else ins[5:]
    h_out, stored, kept = outs[:3]
    saved = [results.at[k] for k in range(n)]
    for k in range(keep):
        saved[n - keep + k] = outs[3 + keep + k].at[0]
    loads = copies.start(place, pieces, weights, sems)
    for copy in loads:
        copy.wait()
    stores = [pltpu.make_async_copy(weights, stored, outsem.at[0, 0])]
    for k in range(keep):
        held = weights.at[pl.ds(n - keep + k, 1)]
        stores.append(pltpu.make_async_copy(held, outs[3 + k], outsem.at[0, 1 + k]))
    for copy in stores:
        copy.start()
    for b in range(raw.shape[0] // rb):
        part = pl.ds(b * rb, rb)
        normed = (raw[part, :].astype(F32) - norm[0:1, :]) * norm[1:2, :] + norm[2:3, :]
        h = normed if first else ins[4][part, :]
        for k in range(n):
            feat = (normed * sigm(mask[s + k : s + k + 1, :])).astype(BF)
            low = h.astype(BF)
            saved[k][3, part, :] = low
            rpre = mdot(feat, weights[k, 0, 1]) + mdot(low, weights[k, 1, 1]) + bias[s + k, 1:2, :]
            r = sigm(rpre)
            upre = mdot(feat, weights[k, 0, 0]) + mdot(low, weights[k, 1, 0]) + bias[s + k, 0:1, :]
            u = sigm(upre)
            reset = (r * h).astype(BF)
            cpre = mdot(feat, weights[k, 0, 2]) + mdot(reset, weights[k, 1, 2]) + bias[s + k, 2:3, :]
            c = jnp.tanh(cpre)
            h = h + u * (c - h)
            saved[k][0, part, :] = u.astype(BF)
            saved[k][1, part, :] = r.astype(BF)
            saved[k][2, part, :] = c.astype(BF)
            if k < n - keep:
                stores.append(pltpu.make_async_copy(saved[k].at[:, part], kept.at[k, :, part], outsem.at[1 + b, k]))
                stores[-1].start()
        h_out[part, :] = h
    for copy in stores:
        copy.wait()


def forward_sections(copies, s, n, keep, turn, raw, h, norm, mask, bias, pieces, awaited, rb=512):
    rows, feat = raw.shape
    first = h is None
    ins = [("v", raw), ("v", norm), ("v", mask), ("v", bias)] + ([] if first else [("v", h)]) + pieces
    whole = (n, 2, 3, feat, feat)
    kept = (n, 4, rows, feat)
    outs = [("v", (rows, feat), F32), ("h", whole, BF), ("h", kept, BF)]
    outs += [("v", (1,) + whole[1:], BF)] * keep + [("v", (1,) + kept[1:], BF)] * keep
    scratch = [pltpu.VMEM(whole, BF), pltpu.VMEM(kept, BF)]
    scratch += [pltpu.SemaphoreType.DMA((copies.total,)), pltpu.SemaphoreType.DMA((1 + rows // rb, n + 1))]
    return call(
        functools.partial(forward_kernel, copies, s, n, first, keep, rb),
        turn,
        ins,
        outs,
        "forward_sections",
        work=WORK,
        scratch=scratch,
        aliases={} if first else {4: 0},
        limit=12 + 8 * n,
        awaited=awaited,
    )


def fetch(index, sources, targets, sems):
    copies = [
        pltpu.make_async_copy(source.at[pl.ds(index, 1), pl.ds(j, 1)], target.at[:, pl.ds(j, 1)], sems.at[i, j])
        for i, (source, target) in enumerate(zip(sources, targets))
        for j in range(source.shape[1])
    ]
    for copy in copies:
        copy.start()
    return copies


def backward_kernel(s, rb, first, place, ins, outs):
    raw, saved, norm, mask, weights, dh_in = ins[:6]
    dn_in = None if first else ins[6]
    dh_out, dn_out, dbuf, lhs, small = outs
    rows = raw.shape[0]
    gate_mask = sigm(mask[s : s + 1, :])
    sums = [jnp.zeros((1, gate_mask.shape[1]), F32)] * 4
    for b in range(rows // rb):
        part = pl.ds(b * rb, rb)
        u = saved[0, 0, part, :].astype(F32)
        c = saved[0, 2, part, :].astype(F32)
        dh = dh_in[part, :]
        t = dh * u
        dc = (t * (1.0 - c * c)).astype(BF)
        dreset = ndot(dc, weights[0, 1, 2])
        low = saved[0, 3, part, :]
        h = low.astype(F32)
        du = (t * (c - h) * (1.0 - u)).astype(BF)
        dbuf[2, part, :] = dc
        dbuf[0, part, :] = du
        dfeat = ndot(dc, weights[0, 0, 2]) + ndot(du, weights[0, 0, 0])
        state = ndot(du, weights[0, 1, 0])
        normed = (raw[part, :].astype(F32) - norm[0:1, :]) * norm[1:2, :] + norm[2:3, :]
        feat = (normed * gate_mask).astype(BF)
        r = saved[0, 1, part, :].astype(F32)
        rh = r * h
        dr = (dreset * rh * (1.0 - r)).astype(BF)
        dbuf[1, part, :] = dr
        lhs[0, :, part] = feat.T
        lhs[1, :, part] = low.T
        lhs[2, :, part] = rh.astype(BF).T
        dfeat = dfeat + ndot(dr, weights[0, 0, 1])
        dh_out[part, :] = (dh - t) + dreset * r + state + ndot(dr, weights[0, 1, 1])
        dn_out[part, :] = dfeat * gate_mask if first else dn_in[part, :] + dfeat * gate_mask
        for i, v in enumerate((du.astype(F32), dr.astype(F32), dc.astype(F32), dfeat * normed)):
            sums[i] = sums[i] + jnp.sum(v, 0, keepdims=True)
    slope = gate_mask * (1.0 - gate_mask)
    small[...] = jnp.concatenate(sums[:3] + [sums[3] * slope] + [jnp.zeros_like(slope)] * 4, axis=0)


def backward_section(s, turn, raw, saved, norm, mask, weights, dh, dn, rb=256):
    rows, feat = raw.shape
    first = dn is None
    ins = [("v", v) for v in (raw, saved, norm, mask, weights, dh)] + ([] if first else [("v", dn)])
    outs = [("v", (rows, feat), F32)] * 2 + [("v", (3, rows, feat), BF), ("v", (3, feat, rows), BF)]
    outs += [("v", (8, feat), F32)]
    return call(
        functools.partial(backward_kernel, s, rb, first),
        turn,
        ins,
        outs,
        "backward_section",
        work=WORK,
        aliases={5: 0} if first else {5: 0, 6: 1},
        limit=9,
    )


def fetch_kernel(index, place, ins, outs, sems):
    for copy in fetch(index, ins, outs, sems):
        copy.wait()


def gradients_kernel(mine, place, ins, outs):
    dbuf, lhs = ins
    out = outs[0]
    half = out.shape[-1]
    core = place[1] if mine else 1 - place[1]
    columns = pl.ds(pl.multiple_of(core * half, half), half)
    for m in range(6):
        which = 0 if m < 3 else (1 if m < 5 else 2)
        out[m] = mdot(lhs[which], dbuf[m % 3, :, columns]).astype(BF).reshape(out.shape[1:])


class Whole:
    total = 2

    def start(self, place, pieces, weights, sems):
        copies = [pltpu.make_async_copy(pieces[a], weights.at[:, a], sems.at[a]) for a in range(2)]
        for copy in copies:
            copy.start()
        return copies


def spread(table_rows, vocab, offsets, columns):
    row = lax.broadcasted_iota(jnp.int32, (vocab, table_rows), 0)
    lane = lax.broadcasted_iota(jnp.int32, (vocab, table_rows), 1)
    return jnp.concatenate([(lane == row + offsets[c]).astype(BF) for c in range(columns)], axis=0)


def column_offsets(cardinality, columns):
    offsets, total = [], 0
    for c in range(columns):
        offsets.append(total)
        total = total + cardinality[c]
    return offsets


def onehot(cat, vocab):
    columns = cat.shape[0]
    width = columns * vocab
    lane = lax.broadcasted_iota(jnp.int32, (columns, width), 1)
    owner = lax.broadcasted_iota(jnp.int32, (columns, width), 0)
    repeat = (lane // vocab == owner).astype(BF)
    values = tdot(cat.astype(F32).astype(BF), repeat)
    wanted = (lax.broadcasted_iota(jnp.int32, (1, width), 1) % vocab).astype(F32)
    return (values == wanted).astype(BF)


def prepare_kernel(vocab, rb, place, ins, outs):
    numeric, cat, cardinality, table = ins
    raw, stats, counts = outs
    rows, num = numeric.shape
    columns, (emb, table_rows) = cat.shape[0], table.shape
    width = columns * emb
    chosen = spread(table_rows, vocab, column_offsets(cardinality, columns), columns)
    tile = (
        lax.broadcasted_iota(jnp.int32, (emb, width), 1) % emb
        == lax.broadcasted_iota(jnp.int32, (emb, width), 0)
    ).astype(BF)
    placed = mdot(chosen, tdot(table[...], tile).astype(BF))
    own = (
        lax.broadcasted_iota(jnp.int32, placed.shape, 1) // emb
        == lax.broadcasted_iota(jnp.int32, placed.shape, 0) // vocab
    )
    blocks = jnp.where(own, placed, 0.0).astype(BF)
    total = jnp.zeros((1, num + width), F32)
    counted = jnp.zeros((1, columns * vocab), F32)
    for b in range(rows // rb):
        part = pl.ds(b * rb, rb)
        hot = onehot(cat[:, part], vocab)
        looked = mdot(hot, blocks)
        raw[part, :num] = numeric[part, :]
        raw[part, num:] = looked.astype(BF)
        total = total + jnp.concatenate(
            [jnp.sum(numeric[part, :].astype(F32), 0, keepdims=True), jnp.sum(looked, 0, keepdims=True)], axis=1
        )
        counted = counted + mdot(jnp.ones((8, rb), BF), hot)[0:1, :]
    mean = total / rows
    squares = jnp.zeros_like(total)
    for b in range(rows // rb):
        away = raw[pl.ds(b * rb, rb), :].astype(F32) - mean
        squares = squares + jnp.sum(away * away, 0, keepdims=True)
    stats[0:1, :] = mean
    stats[1:2, :] = squares
    counts[...] = counted


def prepare(turn, numeric, cat, cardinality, table, vocab):
    rows, num = numeric.shape
    feat = num + cat.shape[0] * table.shape[0]
    return call(
        functools.partial(prepare_kernel, vocab, 256),
        turn,
        [("v", numeric), ("v", cat), ("s", cardinality), ("v", table)],
        [("v", (rows, feat), BF), ("v", (2, feat), F32), ("v", (1, cat.shape[0] * vocab), F32)],
        "prepare",
        work=WORK,
        limit=24,
    )


def merge_kernel(count, place, ins, outs):
    one, two = ins
    out = outs[0]
    apart = one[0:1, :] - two[0:1, :]
    out[0:1, :] = 0.5 * (one[0:1, :] + two[0:1, :])
    out[1:2, :] = one[1:2, :] + two[1:2, :] + apart * apart * (0.5 * count)


def norm_kernel(count, place, ins, outs):
    stats, gain, bias = ins
    out = outs[0]
    inverse = lax.rsqrt(stats[1:2, :] / count + EPSILON)
    out[0:1, :] = stats[0:1, :]
    out[1:2, :] = inverse * gain[...]
    out[2:3, :] = bias[...]
    out[3:4, :] = inverse
    out[4:5, :] = gain[...]
    out[5:8, :] = jnp.zeros((3, inverse.shape[1]), F32)


def head_kernel(rb, place, ins, outs, hidden, slopes):
    h, w1, b1, w2, b2, g = ins
    dh, logits, grad_w1, grad_w2, grad_b = outs
    rows = h.shape[0]
    width = w1.shape[1]
    classes = w2.shape[0]
    eye = lax.broadcasted_iota(jnp.int32, (classes, classes), 0) == lax.broadcasted_iota(
        jnp.int32, (classes, classes), 1
    )
    shift = jnp.sum(jnp.where(eye, b2[...], 0.0), 1, keepdims=True)
    two = jnp.zeros(w2.shape, F32)
    sums = jnp.zeros((1, width), F32)
    for b in range(rows // rb):
        part = pl.ds(b * rb, rb)
        head_in = h[part, :].astype(BF)
        hidden[part, :] = head_in
        x = mdot(head_in, w1[...]) + b1[...]
        phi = 0.5 * (1.0 + lax.erf(x * 0.7071067811865476))
        act = (x * phi).astype(BF)
        logits[:, part] = ndot(w2[...], act) + shift
        dact = tdot(g[:, part], w2[...])
        slope = phi + x * (jnp.exp(-0.5 * x * x) * 0.3989422804014327)
        dx = (dact * slope).astype(BF)
        slopes[part, :] = dx
        dh[part, :] = ndot(dx, w1[...])
        two = two + mdot(g[:, part], act)
        sums = sums + jnp.sum(dx.astype(F32), 0, keepdims=True)
    one = tdot(hidden[...], slopes[...]).astype(BF)
    depth = grad_w1.shape[1]
    for i in range(grad_w1.shape[0]):
        grad_w1[i] = one[i * depth : (i + 1) * depth]
    grad_w2[...] = two
    grad_b[...] = jnp.zeros_like(grad_b)
    grad_b[0:1, :] = sums
    grad_b[1:2, : g.shape[0]] = ndot(jnp.ones((8, rows), BF), g[...])[0:1, :]


def head(turn, h, w1, b1, w2, b2, g):
    rows, feat = h.shape
    classes, hidden = w2.shape
    return call(
        functools.partial(head_kernel, 256),
        turn,
        [("v", v) for v in (h, w1, b1.reshape(1, -1), w2, b2.reshape(1, -1), g)],
        [
            ("v", (rows, feat), F32),
            ("p", (classes, rows), F32),
            ("v", (4, feat // 4, hidden), BF),
            ("v", (classes, hidden), F32),
            ("v", (8, hidden), F32),
        ],
        "head",
        work=WORK,
        scratch=[pltpu.VMEM((rows, feat), BF), pltpu.VMEM((rows, hidden), BF)],
        aliases={0: 0},
        limit=16,
    )


def layout(sections, classes, emb, width, feat):
    at = {"sums": 0, "small": 2}
    at["bias"] = at["small"] + 4 * sections
    at["w2"] = at["bias"] + 1
    at["counts"] = at["w2"] + -(-classes // 2)
    at["table"] = -(-(at["counts"] + width // feat) // 8) * 8
    at["rows"] = at["table"] + emb * width // feat
    return at


def sums_kernel(vocab, rb, at, place, ins, outs):
    raw, cat, dh, dn, norm, counts, grad_w2, grad_b = ins[:8]
    small = ins[8:]
    pack = outs[0]
    rows, feat = raw.shape
    columns = cat.shape[0]
    width = columns * vocab
    emb = (pack.shape[0] - at["table"]) * feat // width
    num = feat - columns * emb
    plain = jnp.zeros((1, feat), F32)
    scaled = jnp.zeros((1, feat), F32)
    crossed = jnp.zeros((columns * emb, width), F32)
    for b in range(rows // rb):
        part = pl.ds(b * rb, rb)
        grad = dh[part, :] + dn[part, :]
        away = raw[part, :].astype(F32) - norm[0:1, :]
        plain = plain + jnp.sum(grad, 0, keepdims=True)
        scaled = scaled + jnp.sum(grad * away, 0, keepdims=True)
        hot = onehot(cat[:, part], vocab)
        pieces = grad[:, num:]
        high = pieces.astype(BF)
        rest = (pieces - high.astype(F32)).astype(BF)
        crossed = crossed + tdot(high, hot) + tdot(rest, hot)
    own = (
        lax.broadcasted_iota(jnp.int32, crossed.shape, 0) // emb
        == lax.broadcasted_iota(jnp.int32, crossed.shape, 1) // vocab
    )
    crossed = jnp.where(own, crossed, 0.0)
    table = crossed[:emb]
    for c in range(1, columns):
        table = table + crossed[c * emb : (c + 1) * emb]
    pack[...] = jnp.zeros_like(pack)
    pack[0:1, :] = plain
    pack[1:2, :] = scaled * norm[3:4, :]
    for k, v in enumerate(small):
        pack[at["small"] + 4 * k : at["small"] + 4 * k + 4, :] = v[:4, :]
    half = feat // 2
    pack[at["bias"] : at["bias"] + 1, :half] = grad_b[0:1, :]
    pack[at["bias"] : at["bias"] + 1, half:] = grad_b[1:2, :]
    for i in range(grad_w2.shape[0]):
        row = at["w2"] + i // 2
        pack[row : row + 1, (i % 2) * half : (i % 2 + 1) * half] = grad_w2[i : i + 1, :]
    for i in range(width // feat):
        pack[at["counts"] + i : at["counts"] + i + 1, :] = counts[:, i * feat : (i + 1) * feat]
        pack[at["table"] + i * emb : at["table"] + (i + 1) * emb, :] = table[:, i * feat : (i + 1) * feat]


def exact_dot(left, right):
    high = left.astype(BF)
    left = left - high.astype(F32)
    middle = left.astype(BF)
    low = (left - middle.astype(F32)).astype(BF)
    return mdot(high, right) + mdot(middle, right) + mdot(low, right)


def finish_kernel(vocab, count, at, place, ins, outs):
    dh, dn, raw, norm, pack, table, cardinality = ins
    grad, grad_table, plain_out, scaled_out, grad_mask, grad_bias, grad_b1, grad_w2, grad_b2 = outs
    feat = raw.shape[1]
    num = grad.shape[1]
    emb, table_rows = table.shape
    columns = (feat - num) // emb
    width = columns * vocab
    mean, inverse, gain = norm[0:1, :], norm[3:4, :], norm[4:5, :]
    plain_out[...] = pack[0:1, :]
    scaled_out[...] = pack[1:2, :]
    plain = pack[0:1, :] / count
    scaled = pack[1:2, :] / count
    factor = gain * inverse
    for b in range(raw.shape[0] // 256):
        part = pl.ds(b * 256, 256)
        away = (raw[part, :num].astype(F32) - mean[:, :num]) * inverse[:, :num]
        both = dh[part, :num] + dn[part, :num]
        grad[part, :] = factor[:, :num] * (both - plain[:, :num] - away * scaled[:, :num])
    for k in range(grad_mask.shape[0]):
        rows = pack[at["small"] + 4 * k : at["small"] + 4 * k + 4, :]
        grad_bias[k] = rows[:3]
        grad_mask[k : k + 1, :] = rows[3:4]
    half = feat // 2
    grad_b1[...] = pack[at["bias"] : at["bias"] + 1, :half]
    grad_b2[...] = pack[at["bias"] : at["bias"] + 1, half : half + grad_b2.shape[1]]
    for i in range(grad_w2.shape[0]):
        row = at["w2"] + i // 2
        grad_w2[i : i + 1, :] = pack[row : row + 1, (i % 2) * half : (i % 2 + 1) * half]
    flat = columns * emb
    mine = (
        lax.broadcasted_iota(jnp.int32, (emb, flat), 1) % emb
        == lax.broadcasted_iota(jnp.int32, (emb, flat), 0)
    )
    expand = (
        lax.broadcasted_iota(jnp.int32, (flat, width), 0) // emb
        == lax.broadcasted_iota(jnp.int32, (flat, width), 1) // vocab
    ).astype(BF)
    vectors = [jnp.where(mine, v[:, num:], 0.0) for v in (mean, inverse, plain, scaled, factor)]
    wide = exact_dot(jnp.concatenate(vectors, axis=0), expand)
    mean_w, inverse_w, plain_w, scaled_w, factor_w = [wide[i * emb : (i + 1) * emb] for i in range(5)]
    chosen = spread(table_rows, vocab, column_offsets(cardinality, columns), columns)
    away = (ndot(table[...], chosen) - mean_w) * inverse_w
    steps = range(width // feat)
    counts = jnp.concatenate([pack[at["counts"] + i : at["counts"] + i + 1, :] for i in steps], axis=1)
    sums = jnp.concatenate([pack[at["table"] + i * emb : at["table"] + (i + 1) * emb, :] for i in steps], axis=1)
    grad_table[...] = exact_dot(factor_w * (sums - counts * (plain_w + away * scaled_w)), chosen)


class Parts:
    def __init__(self, s, n, slots):
        self.s, self.n, self.slots = s, n, slots
        self.total = 4 + 2 * len(slots)

    def start(self, place, pieces, weights, sems):
        depth, width = pieces[0].shape[2:]
        tall = depth // 4
        z, c, d = place[0], place[1], place[2]
        copies = []

        def add(source, arrays, row, rows, core):
            column = (c if core == 0 else 1 - c) * width
            copies.append(
                pltpu.make_async_copy(
                    source,
                    weights.at[
                        :,
                        arrays,
                        :,
                        pl.ds(pl.multiple_of(row, rows), rows),
                        pl.ds(pl.multiple_of(column, width), width),
                    ],
                    sems.at[len(copies)],
                )
            )

        for core in range(2):
            for a in range(2):
                add(pieces[2 * core + a].at[pl.ds(self.s, self.n)], a, z * depth, depth, core)
        for bundle, slot, hops, way in self.slots:
            quarter = lax.bitwise_xor(d, way) if way else d
            row = lax.rem(z + 4 - hops, 4) * depth + quarter * tall
            for core in range(2):
                add(pieces[4 + 2 * bundle + core].at[slot], slice(None), row, tall, core)
        for copy in copies:
            copy.start()
        return copies


SWAP = [(0, 1), (1, 0)]
ACROSS = {1: [(0, 1), (1, 0), (2, 3), (3, 2)], 2: [(0, 2), (2, 0), (1, 3), (3, 1)]}
NEAR = [(0, 1), (1, 0), (2, 3), (3, 2)]
FAR = [(0, 2), (1, 3), (2, 0), (3, 1)]


def other_core(v):
    return lax.ppermute(v, "wide", SWAP)


def along_dp(v, way):
    return lax.ppermute(v, "dp", ACROSS[way])


def along_narrow(v, hops):
    return lax.ppermute(v, "narrow", [(i, (i + hops) % 4) for i in range(4)])


def quarters_kernel(place, ins, outs, sems):
    tall = ins[0].shape[2] // 4
    rows = pl.ds(pl.multiple_of(place[2] * tall, tall), tall)
    copies = []
    for (s, n), out in zip(CHUNKS, outs):
        for a in range(2):
            copies.append(
                pltpu.make_async_copy(ins[a].at[pl.ds(s, n), :, rows], out.at[:, a], sems.at[len(copies)])
            )
    for copy in copies:
        copy.start()
    for copy in copies:
        copy.wait()


def bundle_kernel(kinds, place, ins, outs):
    ins, bundle, outs = list(ins), outs[0], list(outs[1:])
    slot = 0
    for kind in kinds:
        if kind == "K":
            block = ins.pop(0)[...]
            bundle[slot] = block
            outs.pop(0)[...] = block
            slot += 1
        elif kind == "X":
            for a in range(2):
                block = ins.pop(0)
                bundle[slot + a] = block[...]
                outs.pop(0)[...] = block[:, a]
            slot += 2
        else:
            for a in range(2):
                bundle[slot, :, a] = ins.pop(0)[...]
            slot += 1


STEPS = [("wide", SWAP), ("dp", ACROSS[1]), ("dp", ACROSS[2]), ("narrow", NEAR), ("narrow", FAR)]


def half_rows(place, a, kept, tall):
    side = lax.rem(place[2], 2) if a == 0 else lax.div(place[2], 2)
    return pl.ds(pl.multiple_of((side if kept else 1 - side) * tall, tall), tall)


def fold_kernel(place, ins, outs):
    tall = outs[0].shape[2]
    for a in range(2):
        keep, send = outs[2 * a], outs[2 * a + 1]
        pairs = [(ins[0].at[3 * a + j], ins[1].at[3 * a + j]) for j in range(3)]
        if a == 0 and len(ins) == 4:
            pairs.append((ins[2], ins[3]))
        for j, (mine, came) in enumerate(pairs):
            for out, kept in ((keep, True), (send, False)):
                rows = half_rows(place, a, kept, tall)
                for b in range(4):
                    out[j, b] = (mine[b, rows, :].astype(F32) + came[b, rows, :].astype(F32)).astype(BF)


def ring_kernel(active, new, place, ins, outs):
    ins, outs = list(ins), list(outs)
    came = ins.pop(0) if active else None
    on = outs.pop(0) if new or not all(last for _, last in active) else None
    source = target = 0
    for many, last in active:
        mine = ins.pop(0)
        out, first = (outs.pop(0), 0) if last else (on, target)
        for j in range(many):
            out[first + j] = (came[source + j].astype(F32) + mine[j].astype(F32)).astype(BF)
        source += many
        target += 0 if last else many
    for feats in new:
        stages = [(on, target)] + [(outs.pop(0), 0) for _ in range(3)]
        done = 0
        for many in (feats, 3):
            keep, got = ins.pop(0), ins.pop(0)
            for hop, (out, first) in enumerate(stages):
                block = lax.rem(place[0] + 3 - hop, 4)
                for j in range(many):
                    total = keep[j, block].astype(F32) + got[j, block].astype(F32)
                    out[first + done + j] = total.astype(BF)
            done += many
        target += done


def stack_kernel(place, ins, outs):
    at = [0, 0]
    for v in ins:
        for j in range(v.shape[0]):
            a = 0 if j < v.shape[0] - 3 else 1
            outs[a][at[a]] = v[j]
            at[a] += 1


def add_kernel(place, ins, outs):
    for i, out in enumerate(outs):
        out[...] = (ins[2 * i][...].astype(F32) + ins[2 * i + 1][...].astype(F32)).astype(out.dtype)


def blocks_kernel(order, extra, place, ins, outs, buf, sems):
    tall = ins[0].shape[1]
    copies = []
    for i, k in enumerate(order):
        for a in range(2):
            mine, away = ins[2 * a], ins[2 * a + 1]
            for j in range(3):
                at = 3 * i + j + (extra if a == 0 and i else 0)
                buf[a, i, j, half_rows(place, a, True, tall), :] = mine[at].astype(F32)
                buf[a, i, j, half_rows(place, a, False, tall), :] = away[at].astype(F32)
            copies.append(pltpu.make_async_copy(buf.at[a, i], outs[a].at[k], sems.at[a, i]))
            copies[-1].start()
    if extra:
        outs[2][half_rows(place, 0, True, tall), :] = ins[0][3]
        outs[2][half_rows(place, 0, False, tall), :] = ins[1][3]
    for copy in copies:
        copy.wait()


def head_rows_kernel(place, ins, outs):
    depth = ins[0].shape[0]
    for hop, v in enumerate(ins):
        row = lax.rem(place[0] + 4 - hop, 4) * depth
        outs[0][pl.ds(pl.multiple_of(row, depth), depth), :] = v[...].astype(F32)


def blocks(turn, order, parts, sections, extra, before=None):
    ins = [("v", v) for v in parts]
    tall, width = parts[0].shape[1:]
    shape = (sections, 3, 2 * tall, width)
    outs = [("a", shape, F32)] * 2 + ([("v", (2 * tall, width), BF)] if extra else [])
    kernel = functools.partial(blocks_kernel, order, extra)
    if before is not None:
        inner = kernel
        kernel = lambda place, ins, outs, *rest: inner(place, ins[:4], outs, *rest)
        ins += [("a", v) for v in before]
    return call(
        kernel,
        turn,
        ins,
        outs,
        "blocks",
        scratch=[pltpu.VMEM((2, len(order)) + shape[1:], F32), pltpu.SemaphoreType.DMA((2, len(order)))],
        aliases={} if before is None else {4: 0, 5: 1},
        limit=10,
    )


CHUNKS = ((0, 3), (3, 3))
VOCAB = 64
KEPT = 1
AHEAD = "M+K00 K10+X00+M K20+X10+D00+K01+M X20+D10+K11+M D20+K21+X01+M N F0 X11+X21+D01 D11+D21 F1"
BACK = (
    "B0 G0 g0 p0 F0 B1 G1 g1 p1 F1+R0 B2 G2 g2 p2 F2+R1 B3 G3 g3 p3 F3+R2 B4 G4 g4 p4 F4+R3 B5 G5 g5 F5+R4 L "
    "R5+T R~ S0+T R+A0+T R~ S1+T X0 A1+T Z Y X1"
)
GROUPS = ((0, 1, 2, 3), (4, 5))


def body(
    numeric,
    cat_index,
    cardinality,
    emb_table,
    input_norm_gain,
    input_norm_bias,
    mask_logit,
    w_feat,
    w_state,
    gate_bias,
    head_w1,
    head_b1,
    head_w2,
    head_b2,
    cotangent,
):
    axes = ("dp", "wide", "narrow")
    rows, num = numeric.shape
    sections = w_feat.shape[0]
    feat = w_feat.shape[2] * lax.axis_size("narrow")
    emb = emb_table.shape[1]
    columns = cat_index.shape[1]
    classes = head_w2.shape[1]
    count = float(rows * lax.axis_size(axes))
    fast = is_fast()
    half = feat // 2
    cat, table = cat_index.T, emb_table.T
    turn = jnp.zeros((8, 128), F32)

    waiting = []

    def run(kernel, ins, outs, name, **more):
        nonlocal turn
        *v, turn = call(kernel, turn, [("v", x) for x in ins], outs, name, awaited=tuple(waiting), **more)
        waiting.clear()
        return v

    def together(jobs, pause=True):
        asked = [next(job) for job in jobs]

        def kernel(place, ins, outs):
            for one, sources, targets in asked:
                one(place, ins[: len(sources)], outs[: len(targets)])
                ins, outs = ins[len(sources) :], outs[len(targets) :]

        results = run(kernel, [v for a in asked for v in a[1]], [v for a in asked for v in a[2]], "step")
        for job, (_, _, targets) in zip(jobs, asked):
            try:
                job.send(results[: len(targets)])
            except StopIteration:
                pass
            results = results[len(targets) :]
        if pause:
            run(lambda place, ins, outs: None, [], [], "pause", work=WORK)

    if fast:
        arrays = (w_feat, w_state)
        tall = w_feat.shape[2] // 4
        *quarters, turn = call(
            quarters_kernel,
            turn,
            [("h", w) for w in arrays],
            [("v", (n, 2, 3, tall, w_feat.shape[3]), BF) for _, n in CHUNKS],
            "quarters",
            scratch=[pltpu.SemaphoreType.DMA((2 * len(CHUNKS),))],
        )
        came = {(0, g): along_narrow(v, 1) for g, v in enumerate(quarters)}
        across = [other_core(w) for w in arrays]
    raw, stats, counts, turn = prepare(turn, numeric, cat, cardinality, table, VOCAB)

    crossed, far = {}, {}
    slots = [[] for _ in CHUNKS]
    bundles = [[] for _ in CHUNKS]
    stored = []
    kept = []
    h = None
    norm = None
    merges = 0

    def collect(g, steps):
        ins, where, more = [], [], []
        block = quarters[g].shape
        for kind, hop in steps:
            ins += [came[hop, g]] if kind == "K" else crossed[hop, g] if kind == "X" else far[hop, g]
            where += [(hop + 1, way) for way in {"K": (0,), "X": (1, 2), "D": (3,)}[kind]]
            more += {"K": [block], "X": [block[:1] + block[2:]] * 2, "D": []}[kind]
        outs = [("v", (len(where),) + block, BF)] + [("v", v, BF) for v in more]
        bundle, *more = yield functools.partial(bundle_kernel, [kind for kind, _ in steps]), ins, outs
        slots[g] += [(len(bundles[g]), i) + at for i, at in enumerate(where)]
        bundles[g].append((bundle, other_core(bundle)))
        for kind, hop in steps:
            if kind == "K":
                got = more.pop(0)
                crossed[hop, g] = [along_dp(got, way) for way in (1, 2)]
                if hop < 2:
                    came[hop + 1, g] = along_narrow(got, 1)
            elif kind == "X":
                far[hop, g] = [along_dp(more.pop(0), way) for way in (2, 1)]

    def do_merge():
        nonlocal stats, merges
        axis, way = STEPS[merges]
        kernel = functools.partial(merge_kernel, float(rows * 2**merges))
        merges += 1
        (stats,) = yield kernel, [stats, lax.ppermute(stats, axis, way)], [("v", (2, feat), F32)]

    def advance(step):
        parts = step.split("+")
        jobs = [do_merge()] if "M" in parts else []
        for g in range(len(CHUNKS)):
            steps = [(v[0], int(v[1])) for v in parts if v != "M" and int(v[2]) == g]
            jobs += [collect(g, steps)] if steps else []
        together(jobs)

    def do_norm(_):
        nonlocal norm
        ins = [stats, input_norm_gain.reshape(1, -1), input_norm_bias.reshape(1, -1)]
        norm = run(functools.partial(norm_kernel, count), ins, [("v", (8, feat), F32)], "norm")[0]

    def do_forward(i):
        nonlocal h, turn, kept
        s, n = CHUNKS[i]
        if fast:
            copies = Parts(s, n, slots[i])
            pieces = [("h", w) for w in arrays] + [("h", w) for w in across]
            pieces += [("a", v) for pair in bundles[i] for v in pair]
        else:
            copies, pieces = Whole(), [("h", w[s : s + n]) for w in whole]
        h, *held, turn = forward_sections(
            copies, s, n, KEPT if i + 1 == len(CHUNKS) else 0, turn, raw, h, norm, mask_logit, gate_bias, pieces, tuple(waiting)
        )
        waiting.clear()
        stored.extend((held[0], held[1], k) for k in range(n))
        kept = list(zip(held[2 : 2 + KEPT], held[2 + KEPT :]))

    if not fast:
        means = lax.all_gather(stats, axes)
        mean = jnp.mean(means[:, 0], 0)
        away = means[:, 0] - mean
        stats = jnp.stack([mean, jnp.sum(means[:, 1], 0) + rows * jnp.sum(away * away, 0)])
        whole = [
            lax.all_gather(lax.all_gather(w, "narrow", axis=2, tiled=True), "wide", axis=3, tiled=True)
            for w in (w_feat, w_state)
        ]
    for step in AHEAD.split():
        if step == "N":
            do_norm(0)
        elif step[0] == "F":
            do_forward(int(step[1:]))
        elif fast:
            advance(step)

    dh, logits, grad_w1, grad_w2, grad_b, turn = head(turn, h, head_w1, head_b1, head_w2.T, head_b2, cotangent.T)

    dn = None
    weights, saved = kept.pop()
    small = [None] * sections
    order = list(reversed(range(sections)))
    flight = {}
    halfway = lambda many: ("v", (many, 4, feat // 8, half), BF)
    flat = lambda many: ("v", (many, feat // 8, half), BF)
    at = layout(sections, classes, emb, columns * VOCAB, feat)
    result = {}

    def do_backward(t):
        nonlocal dh, dn, turn
        k = order[t]
        dh, dn, dbuf, lhs, small[k], turn = backward_section(
            k, turn, raw, saved, norm, mask_logit, weights, dh, dn
        )
        flight[t] = dbuf, lhs

    def do_fetch(t):
        nonlocal weights, saved, turn
        if kept:
            weights, saved = kept.pop()
            return
        *coming, index = stored[order[t] - 1]
        weights, saved, turn = call(
            functools.partial(fetch_kernel, index),
            turn,
            [("h", v) for v in coming],
            [("v", (1,) + v.shape[1:], BF) for v in coming],
            "fetch",
            work=WORK,
            scratch=[pltpu.SemaphoreType.DMA((2, 4))],
        )

    def columns(t, mine):
        kernel = functools.partial(gradients_kernel, mine)
        outs = [("v", (6, 4, feat // 4, half), BF)]
        return run(kernel, flight[t], outs, "gradients", limit=8, work=WORK)[0]

    def do_other(t):
        other = columns(t, False)
        if fast:
            other = other_core(other)
        flight[t] = flight[t], other

    def do_mine(t):
        flight[t], other = flight[t]
        flight[t] = [columns(t, True), other]
        if fast and t == 0:
            flight[t] += [grad_w1, other_core(grad_w1)]

    def do_fold(t):
        many = len(flight[t]) // 2 + 2
        v = yield fold_kernel, flight[t], [halfway(many), halfway(many), halfway(3), halfway(3)]
        flight[t] = [v[0], along_dp(v[1], 1), v[2], along_dp(v[3], 2)]

    ring = {"moving": None, "active": []}

    def do_ring(t):
        active = ring["active"]
        ins = [along_narrow(ring["moving"], 1)] if active else []
        ins += [parts[0] for _, parts in active]
        feats = [] if t is None else [flight[t][0].shape[0]]
        ins += [] if t is None else flight[t]
        going = sum(parts[0].shape[0] for _, parts in active if len(parts) > 1) + sum(v + 3 for v in feats)
        ended = [(k, parts[0].shape[0]) for k, parts in active if len(parts) == 1]
        outs = ([flat(going)] if going else []) + [flat(many) for _, many in ended]
        outs += [flat(v + 3) for v in feats for _ in range(3)]
        sizes = [(parts[0].shape[0], len(parts) == 1) for _, parts in active]
        v = yield functools.partial(ring_kernel, sizes, feats), ins, outs
        ring["moving"] = v.pop(0) if going else None
        flight.update((k, [v.pop(0)]) for k, _ in ended)
        ring["active"] = [(k, parts[1:]) for k, parts in active if len(parts) > 1]
        ring["active"] += [] if t is None else [(t, v)]

    def do_stack(g):
        ins = [flight[t][0] for t in GROUPS[g]]
        state = 3 * len(GROUPS[g])
        feats = sum(v.shape[0] for v in ins) - state
        v = yield stack_kernel, ins, [flat(feats), flat(state)]
        result[g] = [v[0], along_dp(v[0], 2), v[1], along_dp(v[1], 1)]

    def do_add(g):
        v = yield add_kernel, result[g], [flat(result[g][0].shape[0]), flat(result[g][2].shape[0])]
        result[g] = [v[0], along_dp(v[0], 1), v[1], along_dp(v[1], 2)]

    def do_local(_):
        ins = (raw, cat, dh, dn, norm, counts, grad_w2, grad_b, *small)
        outs = [("v", (at["rows"], feat), F32)]
        result["pack"] = run(
            functools.partial(sums_kernel, VOCAB, 256, at), ins, outs, "local_sums", limit=16, work=WORK
        )[0]
        result["steps"] = 0

    def do_total(_):
        pack = result["pack"]
        axis, way = STEPS[result["steps"]]
        result["steps"] += 1
        (result["pack"],) = yield add_kernel, [pack, lax.ppermute(pack, axis, way)], [("v", pack.shape, F32)]

    def do_blocks(g):
        nonlocal turn
        sectioned = [order[t] for t in GROUPS[g]]
        before = result.get("blocks")
        *v, turn = blocks(turn, sectioned, result[g], sections, 1 if g == 0 else 0, before)
        result["blocks"] = v[:2]
        if g == 0:
            result["last"] = [v[2]] + [along_narrow(v[2], hop) for hop in (1, 2, 3)]

    def do_head_rows(_):
        result["last"] = run(head_rows_kernel, result["last"], [("p", (feat, half), F32)], "head_rows")[0]

    def do_finish(_):
        nonlocal turn
        *result["finish"], turn = call(
            functools.partial(finish_kernel, VOCAB, count, at),
            turn,
            [("v", v) for v in (dh, dn, raw, norm, result["pack"], table)] + [("s", cardinality)],
            [
                ("p", (rows, num), F32),
                ("p", (emb, table.shape[1]), F32),
                ("p", (1, feat), F32),
                ("p", (1, feat), F32),
                ("p", mask_logit.shape, F32),
                ("p", gate_bias.shape, F32),
                ("p", (1, half), F32),
                ("p", (classes, half), F32),
                ("p", (1, classes), F32),
            ],
            "finish",
            limit=16,
            work=WORK,
        )

    tasks = {"B": do_backward, "p": do_fetch, "G": do_other, "g": do_mine, "L": do_local}
    if fast:
        tasks.update(X=do_blocks, Y=do_head_rows, Z=do_finish)
    steps = dict(F=do_fold, R=do_ring, S=do_stack, A=do_add, T=do_total)
    for step in BACK.split():
        if step[0] in tasks:
            tasks[step[0]](int(step[1:] or 0))
        elif fast and step[0] in steps:
            jobs = [steps[v[0]](int(v[1:]) if v[1:] else None) for v in step.rstrip("~").split("+")]
            together(jobs, not step.endswith("~"))
    if fast:
        grad_feat, grad_state = result["blocks"]
        grad_w1 = result["last"]
    else:
        halves = ([None] * sections, [None] * sections)
        for t in range(sections):
            local = jnp.concatenate(flight[t], axis=3).reshape(6, feat, feat)
            for a in range(2):
                part = lax.psum_scatter(local[3 * a : 3 * a + 3], "wide", scatter_dimension=2, tiled=True)
                part = lax.psum_scatter(part, "narrow", scatter_dimension=1, tiled=True)
                halves[a][order[t]] = lax.psum(part, "dp").astype(F32)
        result["pack"] = lax.psum(result["pack"], axes)
        do_finish(0)
        grad_feat, grad_state = (jnp.stack(v) for v in halves)
        grad_w1 = lax.psum(grad_w1.reshape(feat, -1).astype(F32), axes)
    grad_numeric, grad_table, plain, scaled, grad_mask, grad_bias, grad_b1, grad_w2, grad_b2 = result["finish"]
    return (
        logits.T,
        grad_numeric,
        grad_table.T,
        scaled.reshape(-1),
        plain.reshape(-1),
        grad_mask,
        grad_feat,
        grad_state,
        grad_bias,
        grad_w1,
        grad_b1.reshape(-1),
        grad_w2.T,
        grad_b2.reshape(-1),
    )


def solution(mesh):
    spread_rows = P(("dp", "wide", "narrow"), None)
    blocked = P(None, None, "narrow", "wide")
    in_specs = (spread_rows, spread_rows) + (P(),) * 5 + (blocked, blocked) + (P(),) * 5 + (spread_rows,)
    out_specs = (spread_rows, spread_rows) + (P(),) * 4 + (blocked, blocked) + (P(),) * 5
    return jax.shard_map(body, mesh=mesh, in_specs=in_specs, out_specs=out_specs, check_vma=False)
```

```python
import functools
import jax
import jax.numpy as jnp
from jax import lax
from jax.experimental import pallas as pl
from jax.experimental.pallas import tpu as pltpu
from jax.sharding import PartitionSpec as P

EPSILON = 1e-05
BF = jnp.bfloat16
F32 = jnp.float32
VMEM = pl.BlockSpec(memory_space=pltpu.VMEM)
SMEM = pl.BlockSpec(memory_space=pltpu.SMEM)
ANY = pl.BlockSpec(memory_space=pl.ANY)
MIB = 2**20
WORK = 3 * 10**10


def mdot(left, right):
    return lax.dot_general(left, right, (((1,), (0,)), ((), ())), preferred_element_type=F32)


def tdot(left, right):
    return lax.dot_general(left, right, (((0,), (0,)), ((), ())), preferred_element_type=F32)


def ndot(left, right):
    return lax.dot_general(left, right, (((1,), (1,)), ((), ())), preferred_element_type=F32)


def sigm(v):
    return 0.5 * jnp.tanh(0.5 * v) + 0.5


def call(kernel, turn, ins, outs, name, scratch=(), aliases=None, limit=4, work=0, awaited=()):
    specs = {"v": VMEM, "p": VMEM, "h": ANY, "a": ANY, "s": SMEM}
    memory = {"v": pltpu.VMEM, "h": pltpu.HBM}
    ins = [("v", turn)] + list(ins)
    used = len(ins)
    ins += [("a", x) for x in awaited]
    outs = [("v", turn.shape, turn.dtype)] + list(outs)
    given = [pltpu.with_memory_space_constraint(x, memory[kind]) if kind in memory else x for kind, x in ins]
    fast = is_fast()

    def shape(kind, dims, dtype):
        return memory[kind](dims, dtype) if kind in memory else jax.ShapeDtypeStruct(dims, dtype)

    def run(*refs):
        place = [lax.axis_index(a) if fast else 0 for a in ("narrow", "wide", "dp")]
        kernel(place, refs[1:used], refs[len(ins) + 1 : len(ins) + len(outs)], *refs[len(ins) + len(outs) :])

    turn, *results = pl.pallas_call(
        run,
        in_specs=[specs[kind] for kind, _ in ins],
        out_specs=[specs[o[0]] for o in outs],
        out_shape=[shape(*o) for o in outs],
        scratch_shapes=list(scratch),
        input_output_aliases={0: 0, **{i + 1: o + 1 for i, o in (aliases or {}).items()}},
        compiler_params=pltpu.CompilerParams(vmem_limit_bytes=limit * MIB),
        cost_estimate=pl.CostEstimate(flops=work, bytes_accessed=0, transcendentals=0),
        name=name,
    )(*given)
    return (*results, turn)


def is_fast():
    return tuple(lax.axis_size(a) for a in ("dp", "wide", "narrow")) == (4, 2, 4)


def forward_kernel(copies, s, n, first, keep, rb, place, ins, outs, weights, results, sems, outsem):
    raw, norm, mask, bias = ins[:4]
    pieces = ins[4:] if first else ins[5:]
    h_out, stored, kept = outs[:3]
    saved = [results.at[k] for k in range(n)]
    for k in range(keep):
        saved[n - keep + k] = outs[3 + keep + k].at[0]
    loads = copies.start(place, pieces, weights, sems)
    for copy in loads:
        copy.wait()
    stores = [pltpu.make_async_copy(weights, stored, outsem.at[0, 0])]
    for k in range(keep):
        held = weights.at[pl.ds(n - keep + k, 1)]
        stores.append(pltpu.make_async_copy(held, outs[3 + k], outsem.at[0, 1 + k]))
    for copy in stores:
        copy.start()
    for b in range(raw.shape[0] // rb):
        part = pl.ds(b * rb, rb)
        normed = (raw[part, :].astype(F32) - norm[0:1, :]) * norm[1:2, :] + norm[2:3, :]
        h = normed if first else ins[4][part, :]
        for k in range(n):
            feat = (normed * sigm(mask[s + k : s + k + 1, :])).astype(BF)
            low = h.astype(BF)
            saved[k][3, part, :] = low
            rpre = mdot(feat, weights[k, 0, 1]) + mdot(low, weights[k, 1, 1]) + bias[s + k, 1:2, :]
            r = sigm(rpre)
            upre = mdot(feat, weights[k, 0, 0]) + mdot(low, weights[k, 1, 0]) + bias[s + k, 0:1, :]
            u = sigm(upre)
            reset = (r * h).astype(BF)
            cpre = mdot(feat, weights[k, 0, 2]) + mdot(reset, weights[k, 1, 2]) + bias[s + k, 2:3, :]
            c = jnp.tanh(cpre)
            h = h + u * (c - h)
            saved[k][0, part, :] = u.astype(BF)
            saved[k][1, part, :] = r.astype(BF)
            saved[k][2, part, :] = c.astype(BF)
            if k < n - keep:
                stores.append(pltpu.make_async_copy(saved[k].at[:, part], kept.at[k, :, part], outsem.at[1 + b, k]))
                stores[-1].start()
        h_out[part, :] = h
    for copy in stores:
        copy.wait()


def forward_sections(copies, s, n, keep, turn, raw, h, norm, mask, bias, pieces, awaited, rb=512):
    rows, feat = raw.shape
    first = h is None
    ins = [("v", raw), ("v", norm), ("v", mask), ("v", bias)] + ([] if first else [("v", h)]) + pieces
    whole = (n, 2, 3, feat, feat)
    kept = (n, 4, rows, feat)
    outs = [("v", (rows, feat), F32), ("h", whole, BF), ("h", kept, BF)]
    outs += [("v", (1,) + whole[1:], BF)] * keep + [("v", (1,) + kept[1:], BF)] * keep
    scratch = [pltpu.VMEM(whole, BF), pltpu.VMEM(kept, BF)]
    scratch += [pltpu.SemaphoreType.DMA((copies.total,)), pltpu.SemaphoreType.DMA((1 + rows // rb, n + 1))]
    return call(
        functools.partial(forward_kernel, copies, s, n, first, keep, rb),
        turn,
        ins,
        outs,
        "forward_sections",
        work=WORK,
        scratch=scratch,
        aliases={} if first else {4: 0},
        limit=12 + 8 * n,
        awaited=awaited,
    )


def fetch(index, sources, targets, sems):
    copies = [
        pltpu.make_async_copy(source.at[pl.ds(index, 1), pl.ds(j, 1)], target.at[:, pl.ds(j, 1)], sems.at[i, j])
        for i, (source, target) in enumerate(zip(sources, targets))
        for j in range(source.shape[1])
    ]
    for copy in copies:
        copy.start()
    return copies


def backward_kernel(s, rb, first, place, ins, outs):
    raw, saved, norm, mask, weights, dh_in = ins[:6]
    dn_in = None if first else ins[6]
    dh_out, dn_out, dbuf, lhs, small = outs
    rows = raw.shape[0]
    gate_mask = sigm(mask[s : s + 1, :])
    sums = [jnp.zeros((1, gate_mask.shape[1]), F32)] * 4
    for b in range(rows // rb):
        part = pl.ds(b * rb, rb)
        u = saved[0, 0, part, :].astype(F32)
        c = saved[0, 2, part, :].astype(F32)
        dh = dh_in[part, :]
        t = dh * u
        dc = (t * (1.0 - c * c)).astype(BF)
        dreset = ndot(dc, weights[0, 1, 2])
        low = saved[0, 3, part, :]
        h = low.astype(F32)
        du = (t * (c - h) * (1.0 - u)).astype(BF)
        dbuf[2, part, :] = dc
        dbuf[0, part, :] = du
        dfeat = ndot(dc, weights[0, 0, 2]) + ndot(du, weights[0, 0, 0])
        state = ndot(du, weights[0, 1, 0])
        normed = (raw[part, :].astype(F32) - norm[0:1, :]) * norm[1:2, :] + norm[2:3, :]
        feat = (normed * gate_mask).astype(BF)
        r = saved[0, 1, part, :].astype(F32)
        rh = r * h
        dr = (dreset * rh * (1.0 - r)).astype(BF)
        dbuf[1, part, :] = dr
        lhs[0, :, part] = feat.T
        lhs[1, :, part] = low.T
        lhs[2, :, part] = rh.astype(BF).T
        dfeat = dfeat + ndot(dr, weights[0, 0, 1])
        dh_out[part, :] = (dh - t) + dreset * r + state + ndot(dr, weights[0, 1, 1])
        dn_out[part, :] = dfeat * gate_mask if first else dn_in[part, :] + dfeat * gate_mask
        for i, v in enumerate((du.astype(F32), dr.astype(F32), dc.astype(F32), dfeat * normed)):
            sums[i] = sums[i] + jnp.sum(v, 0, keepdims=True)
    slope = gate_mask * (1.0 - gate_mask)
    small[...] = jnp.concatenate(sums[:3] + [sums[3] * slope] + [jnp.zeros_like(slope)] * 4, axis=0)


def backward_section(s, turn, raw, saved, norm, mask, weights, dh, dn, rb=256):
    rows, feat = raw.shape
    first = dn is None
    ins = [("v", v) for v in (raw, saved, norm, mask, weights, dh)] + ([] if first else [("v", dn)])
    outs = [("v", (rows, feat), F32)] * 2 + [("v", (3, rows, feat), BF), ("v", (3, feat, rows), BF)]
    outs += [("v", (8, feat), F32)]
    return call(
        functools.partial(backward_kernel, s, rb, first),
        turn,
        ins,
        outs,
        "backward_section",
        work=WORK,
        aliases={5: 0} if first else {5: 0, 6: 1},
        limit=9,
    )


def fetch_kernel(index, place, ins, outs, sems):
    for copy in fetch(index, ins, outs, sems):
        copy.wait()


def gradients_kernel(mine, place, ins, outs):
    dbuf, lhs = ins
    out = outs[0]
    half = out.shape[-1]
    core = place[1] if mine else 1 - place[1]
    columns = pl.ds(pl.multiple_of(core * half, half), half)
    for m in range(6):
        which = 0 if m < 3 else (1 if m < 5 else 2)
        out[m] = mdot(lhs[which], dbuf[m % 3, :, columns]).astype(BF).reshape(out.shape[1:])


class Whole:
    total = 2

    def start(self, place, pieces, weights, sems):
        copies = [pltpu.make_async_copy(pieces[a], weights.at[:, a], sems.at[a]) for a in range(2)]
        for copy in copies:
            copy.start()
        return copies


def spread(table_rows, vocab, offsets, columns):
    row = lax.broadcasted_iota(jnp.int32, (vocab, table_rows), 0)
    lane = lax.broadcasted_iota(jnp.int32, (vocab, table_rows), 1)
    return jnp.concatenate([(lane == row + offsets[c]).astype(BF) for c in range(columns)], axis=0)


def column_offsets(cardinality, columns):
    offsets, total = [], 0
    for c in range(columns):
        offsets.append(total)
        total = total + cardinality[c]
    return offsets


def onehot(cat, vocab):
    columns = cat.shape[0]
    width = columns * vocab
    lane = lax.broadcasted_iota(jnp.int32, (columns, width), 1)
    owner = lax.broadcasted_iota(jnp.int32, (columns, width), 0)
    repeat = (lane // vocab == owner).astype(BF)
    values = tdot(cat.astype(F32).astype(BF), repeat)
    wanted = (lax.broadcasted_iota(jnp.int32, (1, width), 1) % vocab).astype(F32)
    return (values == wanted).astype(BF)


def prepare_kernel(vocab, rb, place, ins, outs):
    numeric, cat, cardinality, table = ins
    raw, stats, counts = outs
    rows, num = numeric.shape
    columns, (emb, table_rows) = cat.shape[0], table.shape
    width = columns * emb
    chosen = spread(table_rows, vocab, column_offsets(cardinality, columns), columns)
    tile = (
        lax.broadcasted_iota(jnp.int32, (emb, width), 1) % emb
        == lax.broadcasted_iota(jnp.int32, (emb, width), 0)
    ).astype(BF)
    placed = mdot(chosen, tdot(table[...], tile).astype(BF))
    own = (
        lax.broadcasted_iota(jnp.int32, placed.shape, 1) // emb
        == lax.broadcasted_iota(jnp.int32, placed.shape, 0) // vocab
    )
    blocks = jnp.where(own, placed, 0.0).astype(BF)
    total = jnp.zeros((1, num + width), F32)
    counted = jnp.zeros((1, columns * vocab), F32)
    for b in range(rows // rb):
        part = pl.ds(b * rb, rb)
        hot = onehot(cat[:, part], vocab)
        looked = mdot(hot, blocks)
        raw[part, :num] = numeric[part, :]
        raw[part, num:] = looked.astype(BF)
        total = total + jnp.concatenate(
            [jnp.sum(numeric[part, :].astype(F32), 0, keepdims=True), jnp.sum(looked, 0, keepdims=True)], axis=1
        )
        counted = counted + mdot(jnp.ones((8, rb), BF), hot)[0:1, :]
    mean = total / rows
    squares = jnp.zeros_like(total)
    for b in range(rows // rb):
        away = raw[pl.ds(b * rb, rb), :].astype(F32) - mean
        squares = squares + jnp.sum(away * away, 0, keepdims=True)
    stats[0:1, :] = mean
    stats[1:2, :] = squares
    counts[...] = counted


def prepare(turn, numeric, cat, cardinality, table, vocab):
    rows, num = numeric.shape
    feat = num + cat.shape[0] * table.shape[0]
    return call(
        functools.partial(prepare_kernel, vocab, 256),
        turn,
        [("v", numeric), ("v", cat), ("s", cardinality), ("v", table)],
        [("v", (rows, feat), BF), ("v", (2, feat), F32), ("v", (1, cat.shape[0] * vocab), F32)],
        "prepare",
        work=WORK,
        limit=24,
    )


def merge_kernel(count, place, ins, outs):
    one, two = ins
    out = outs[0]
    apart = one[0:1, :] - two[0:1, :]
    out[0:1, :] = 0.5 * (one[0:1, :] + two[0:1, :])
    out[1:2, :] = one[1:2, :] + two[1:2, :] + apart * apart * (0.5 * count)


def norm_kernel(count, place, ins, outs):
    stats, gain, bias = ins
    out = outs[0]
    inverse = lax.rsqrt(stats[1:2, :] / count + EPSILON)
    out[0:1, :] = stats[0:1, :]
    out[1:2, :] = inverse * gain[...]
    out[2:3, :] = bias[...]
    out[3:4, :] = inverse
    out[4:5, :] = gain[...]
    out[5:8, :] = jnp.zeros((3, inverse.shape[1]), F32)


def head_kernel(rb, place, ins, outs, hidden, slopes):
    h, w1, b1, w2, b2, g = ins
    dh, logits, grad_w1, grad_w2, grad_b = outs
    rows = h.shape[0]
    width = w1.shape[1]
    classes = w2.shape[0]
    eye = lax.broadcasted_iota(jnp.int32, (classes, classes), 0) == lax.broadcasted_iota(
        jnp.int32, (classes, classes), 1
    )
    shift = jnp.sum(jnp.where(eye, b2[...], 0.0), 1, keepdims=True)
    two = jnp.zeros(w2.shape, F32)
    sums = jnp.zeros((1, width), F32)
    for b in range(rows // rb):
        part = pl.ds(b * rb, rb)
        head_in = h[part, :].astype(BF)
        hidden[part, :] = head_in
        x = mdot(head_in, w1[...]) + b1[...]
        phi = 0.5 * (1.0 + lax.erf(x * 0.7071067811865476))
        act = (x * phi).astype(BF)
        logits[:, part] = ndot(w2[...], act) + shift
        dact = tdot(g[:, part], w2[...])
        slope = phi + x * (jnp.exp(-0.5 * x * x) * 0.3989422804014327)
        dx = (dact * slope).astype(BF)
        slopes[part, :] = dx
        dh[part, :] = ndot(dx, w1[...])
        two = two + mdot(g[:, part], act)
        sums = sums + jnp.sum(dx.astype(F32), 0, keepdims=True)
    one = tdot(hidden[...], slopes[...]).astype(BF)
    depth = grad_w1.shape[1]
    for i in range(grad_w1.shape[0]):
        grad_w1[i] = one[i * depth : (i + 1) * depth]
    grad_w2[...] = two
    grad_b[...] = jnp.zeros_like(grad_b)
    grad_b[0:1, :] = sums
    grad_b[1:2, : g.shape[0]] = ndot(jnp.ones((8, rows), BF), g[...])[0:1, :]


def head(turn, h, w1, b1, w2, b2, g):
    rows, feat = h.shape
    classes, hidden = w2.shape
    return call(
        functools.partial(head_kernel, 256),
        turn,
        [("v", v) for v in (h, w1, b1.reshape(1, -1), w2, b2.reshape(1, -1), g)],
        [
            ("v", (rows, feat), F32),
            ("p", (classes, rows), F32),
            ("v", (4, feat // 4, hidden), BF),
            ("v", (classes, hidden), F32),
            ("v", (8, hidden), F32),
        ],
        "head",
        work=WORK,
        scratch=[pltpu.VMEM((rows, feat), BF), pltpu.VMEM((rows, hidden), BF)],
        aliases={0: 0},
        limit=16,
    )


def layout(sections, classes, emb, width, feat):
    at = {"sums": 0, "small": 2}
    at["bias"] = at["small"] + 4 * sections
    at["w2"] = at["bias"] + 1
    at["counts"] = at["w2"] + -(-classes // 2)
    at["table"] = -(-(at["counts"] + width // feat) // 8) * 8
    at["rows"] = at["table"] + emb * width // feat
    return at


def sums_kernel(vocab, rb, at, place, ins, outs):
    raw, cat, dh, dn, norm, counts, grad_w2, grad_b = ins[:8]
    small = ins[8:]
    pack = outs[0]
    rows, feat = raw.shape
    columns = cat.shape[0]
    width = columns * vocab
    emb = (pack.shape[0] - at["table"]) * feat // width
    num = feat - columns * emb
    plain = jnp.zeros((1, feat), F32)
    scaled = jnp.zeros((1, feat), F32)
    crossed = jnp.zeros((columns * emb, width), F32)
    for b in range(rows // rb):
        part = pl.ds(b * rb, rb)
        grad = dh[part, :] + dn[part, :]
        away = raw[part, :].astype(F32) - norm[0:1, :]
        plain = plain + jnp.sum(grad, 0, keepdims=True)
        scaled = scaled + jnp.sum(grad * away, 0, keepdims=True)
        hot = onehot(cat[:, part], vocab)
        pieces = grad[:, num:]
        high = pieces.astype(BF)
        rest = (pieces - high.astype(F32)).astype(BF)
        crossed = crossed + tdot(high, hot) + tdot(rest, hot)
    own = (
        lax.broadcasted_iota(jnp.int32, crossed.shape, 0) // emb
        == lax.broadcasted_iota(jnp.int32, crossed.shape, 1) // vocab
    )
    crossed = jnp.where(own, crossed, 0.0)
    table = crossed[:emb]
    for c in range(1, columns):
        table = table + crossed[c * emb : (c + 1) * emb]
    pack[...] = jnp.zeros_like(pack)
    pack[0:1, :] = plain
    pack[1:2, :] = scaled * norm[3:4, :]
    for k, v in enumerate(small):
        pack[at["small"] + 4 * k : at["small"] + 4 * k + 4, :] = v[:4, :]
    half = feat // 2
    pack[at["bias"] : at["bias"] + 1, :half] = grad_b[0:1, :]
    pack[at["bias"] : at["bias"] + 1, half:] = grad_b[1:2, :]
    for i in range(grad_w2.shape[0]):
        row = at["w2"] + i // 2
        pack[row : row + 1, (i % 2) * half : (i % 2 + 1) * half] = grad_w2[i : i + 1, :]
    for i in range(width // feat):
        pack[at["counts"] + i : at["counts"] + i + 1, :] = counts[:, i * feat : (i + 1) * feat]
        pack[at["table"] + i * emb : at["table"] + (i + 1) * emb, :] = table[:, i * feat : (i + 1) * feat]


def exact_dot(left, right):
    high = left.astype(BF)
    left = left - high.astype(F32)
    middle = left.astype(BF)
    low = (left - middle.astype(F32)).astype(BF)
    return mdot(high, right) + mdot(middle, right) + mdot(low, right)


def finish_kernel(vocab, count, at, place, ins, outs):
    dh, dn, raw, norm, pack, table, cardinality = ins
    grad, grad_table, plain_out, scaled_out, grad_mask, grad_bias, grad_b1, grad_w2, grad_b2 = outs
    feat = raw.shape[1]
    num = grad.shape[1]
    emb, table_rows = table.shape
    columns = (feat - num) // emb
    width = columns * vocab
    mean, inverse, gain = norm[0:1, :], norm[3:4, :], norm[4:5, :]
    plain_out[...] = pack[0:1, :]
    scaled_out[...] = pack[1:2, :]
    plain = pack[0:1, :] / count
    scaled = pack[1:2, :] / count
    factor = gain * inverse
    for b in range(raw.shape[0] // 256):
        part = pl.ds(b * 256, 256)
        away = (raw[part, :num].astype(F32) - mean[:, :num]) * inverse[:, :num]
        both = dh[part, :num] + dn[part, :num]
        grad[part, :] = factor[:, :num] * (both - plain[:, :num] - away * scaled[:, :num])
    for k in range(grad_mask.shape[0]):
        rows = pack[at["small"] + 4 * k : at["small"] + 4 * k + 4, :]
        grad_bias[k] = rows[:3]
        grad_mask[k : k + 1, :] = rows[3:4]
    half = feat // 2
    grad_b1[...] = pack[at["bias"] : at["bias"] + 1, :half]
    grad_b2[...] = pack[at["bias"] : at["bias"] + 1, half : half + grad_b2.shape[1]]
    for i in range(grad_w2.shape[0]):
        row = at["w2"] + i // 2
        grad_w2[i : i + 1, :] = pack[row : row + 1, (i % 2) * half : (i % 2 + 1) * half]
    flat = columns * emb
    mine = (
        lax.broadcasted_iota(jnp.int32, (emb, flat), 1) % emb
        == lax.broadcasted_iota(jnp.int32, (emb, flat), 0)
    )
    expand = (
        lax.broadcasted_iota(jnp.int32, (flat, width), 0) // emb
        == lax.broadcasted_iota(jnp.int32, (flat, width), 1) // vocab
    ).astype(BF)
    vectors = [jnp.where(mine, v[:, num:], 0.0) for v in (mean, inverse, plain, scaled, factor)]
    wide = exact_dot(jnp.concatenate(vectors, axis=0), expand)
    mean_w, inverse_w, plain_w, scaled_w, factor_w = [wide[i * emb : (i + 1) * emb] for i in range(5)]
    chosen = spread(table_rows, vocab, column_offsets(cardinality, columns), columns)
    away = (ndot(table[...], chosen) - mean_w) * inverse_w
    steps = range(width // feat)
    counts = jnp.concatenate([pack[at["counts"] + i : at["counts"] + i + 1, :] for i in steps], axis=1)
    sums = jnp.concatenate([pack[at["table"] + i * emb : at["table"] + (i + 1) * emb, :] for i in steps], axis=1)
    grad_table[...] = exact_dot(factor_w * (sums - counts * (plain_w + away * scaled_w)), chosen)


class Parts:
    def __init__(self, s, n, slots):
        self.s, self.n, self.slots = s, n, slots
        self.total = 4 + 2 * len(slots)

    def start(self, place, pieces, weights, sems):
        depth, width = pieces[0].shape[2:]
        tall = depth // 4
        z, c, d = place[0], place[1], place[2]
        copies = []

        def add(source, arrays, row, rows, core):
            column = (c if core == 0 else 1 - c) * width
            copies.append(
                pltpu.make_async_copy(
                    source,
                    weights.at[
                        :,
                        arrays,
                        :,
                        pl.ds(pl.multiple_of(row, rows), rows),
                        pl.ds(pl.multiple_of(column, width), width),
                    ],
                    sems.at[len(copies)],
                )
            )

        for core in range(2):
            for a in range(2):
                add(pieces[2 * core + a].at[pl.ds(self.s, self.n)], a, z * depth, depth, core)
        for bundle, slot, hops, way in self.slots:
            quarter = lax.bitwise_xor(d, way) if way else d
            row = lax.rem(z + 4 - hops, 4) * depth + quarter * tall
            for core in range(2):
                add(pieces[4 + 2 * bundle + core].at[slot], slice(None), row, tall, core)
        for copy in copies:
            copy.start()
        return copies


SWAP = [(0, 1), (1, 0)]
ACROSS = {1: [(0, 1), (1, 0), (2, 3), (3, 2)], 2: [(0, 2), (2, 0), (1, 3), (3, 1)]}
NEAR = [(0, 1), (1, 0), (2, 3), (3, 2)]
FAR = [(0, 2), (1, 3), (2, 0), (3, 1)]


def other_core(v):
    return lax.ppermute(v, "wide", SWAP)


def along_dp(v, way):
    return lax.ppermute(v, "dp", ACROSS[way])


def along_narrow(v, hops):
    return lax.ppermute(v, "narrow", [(i, (i + hops) % 4) for i in range(4)])


def quarters_kernel(place, ins, outs, sems):
    tall = ins[0].shape[2] // 4
    rows = pl.ds(pl.multiple_of(place[2] * tall, tall), tall)
    copies = []
    for (s, n), out in zip(CHUNKS, outs):
        for a in range(2):
            copies.append(
                pltpu.make_async_copy(ins[a].at[pl.ds(s, n), :, rows], out.at[:, a], sems.at[len(copies)])
            )
    for copy in copies:
        copy.start()
    for copy in copies:
        copy.wait()


def bundle_kernel(kinds, place, ins, outs):
    ins, bundle, outs = list(ins), outs[0], list(outs[1:])
    n = bundle.shape[1]
    slot = 0
    for kind, many in kinds:
        if kind in "Kk":
            block = ins.pop(0)[...]
            bundle[slot] = block
            out = outs.pop(0)
            out[...] = block
            slot += 1
            if many > 1:
                out = outs.pop(0)
                for i in range(many):
                    out[i * n : (i + 1) * n] = ins.pop(0)[...] if i + 1 < many else block
        elif kind == "X":
            for a in range(2):
                block = ins.pop(0)
                for i in range(many):
                    bundle[slot + i] = block[i * n : (i + 1) * n]
                outs.pop(0)[...] = block[:, a]
                slot += many
        else:
            for a in range(2):
                block = ins.pop(0)
                for i in range(many):
                    bundle[slot + i, :, a] = block[i * n : (i + 1) * n]
            slot += many


STEPS = [("wide", SWAP), ("dp", ACROSS[1]), ("dp", ACROSS[2]), ("narrow", NEAR), ("narrow", FAR)]


def half_rows(place, a, kept, tall):
    side = lax.rem(place[2], 2) if a == 0 else lax.div(place[2], 2)
    return pl.ds(pl.multiple_of((side if kept else 1 - side) * tall, tall), tall)


def fold_kernel(place, ins, outs):
    tall = outs[0].shape[2]
    for a in range(2):
        keep, send = outs[2 * a], outs[2 * a + 1]
        pairs = [(ins[0].at[3 * a + j], ins[1].at[3 * a + j]) for j in range(3)]
        if a == 0 and len(ins) == 4:
            pairs.append((ins[2], ins[3]))
        for j, (mine, came) in enumerate(pairs):
            for out, kept in ((keep, True), (send, False)):
                rows = half_rows(place, a, kept, tall)
                for b in range(4):
                    out[j, b] = (mine[b, rows, :].astype(F32) + came[b, rows, :].astype(F32)).astype(BF)


def ring_kernel(active, new, place, ins, outs):
    ins, outs = list(ins), list(outs)
    came = ins.pop(0) if active else None
    on = outs.pop(0) if new or not all(last for _, last in active) else None
    source = target = 0
    for many, last in active:
        mine = ins.pop(0)
        out, first = (outs.pop(0), 0) if last else (on, target)
        for j in range(many):
            out[first + j] = (came[source + j].astype(F32) + mine[j].astype(F32)).astype(BF)
        source += many
        target += 0 if last else many
    for feats in new:
        stages = [(on, target)] + [(outs.pop(0), 0) for _ in range(3)]
        done = 0
        for many in (feats, 3):
            keep, got = ins.pop(0), ins.pop(0)
            for hop, (out, first) in enumerate(stages):
                block = lax.rem(place[0] + 3 - hop, 4)
                for j in range(many):
                    total = keep[j, block].astype(F32) + got[j, block].astype(F32)
                    out[first + done + j] = total.astype(BF)
            done += many
        target += done


def stack_kernel(place, ins, outs):
    at = [0, 0]
    for v in ins:
        for j in range(v.shape[0]):
            a = 0 if j < v.shape[0] - 3 else 1
            outs[a][at[a]] = v[j]
            at[a] += 1


def add_kernel(place, ins, outs):
    for i, out in enumerate(outs):
        out[...] = (ins[2 * i][...].astype(F32) + ins[2 * i + 1][...].astype(F32)).astype(out.dtype)


def blocks_kernel(order, extra, place, ins, outs, buf, sems):
    tall = ins[0].shape[1]
    copies = []
    for i, k in enumerate(order):
        for a in range(2):
            mine, away = ins[2 * a], ins[2 * a + 1]
            for j in range(3):
                at = 3 * i + j + (extra if a == 0 and i else 0)
                buf[a, i, j, half_rows(place, a, True, tall), :] = mine[at].astype(F32)
                buf[a, i, j, half_rows(place, a, False, tall), :] = away[at].astype(F32)
            copies.append(pltpu.make_async_copy(buf.at[a, i], outs[a].at[k], sems.at[a, i]))
            copies[-1].start()
    if extra:
        outs[2][half_rows(place, 0, True, tall), :] = ins[0][3]
        outs[2][half_rows(place, 0, False, tall), :] = ins[1][3]
    for copy in copies:
        copy.wait()


def head_rows_kernel(place, ins, outs):
    depth = ins[0].shape[0]
    for hop, v in enumerate(ins):
        row = lax.rem(place[0] + 4 - hop, 4) * depth
        outs[0][pl.ds(pl.multiple_of(row, depth), depth), :] = v[...].astype(F32)


def blocks(turn, order, parts, sections, extra, before=None):
    ins = [("v", v) for v in parts]
    tall, width = parts[0].shape[1:]
    shape = (sections, 3, 2 * tall, width)
    outs = [("a", shape, F32)] * 2 + ([("v", (2 * tall, width), BF)] if extra else [])
    kernel = functools.partial(blocks_kernel, order, extra)
    if before is not None:
        inner = kernel
        kernel = lambda place, ins, outs, *rest: inner(place, ins[:4], outs, *rest)
        ins += [("a", v) for v in before]
    return call(
        kernel,
        turn,
        ins,
        outs,
        "blocks",
        scratch=[pltpu.VMEM((2, len(order)) + shape[1:], F32), pltpu.SemaphoreType.DMA((2, len(order)))],
        aliases={} if before is None else {4: 0, 5: 1},
        limit=10,
    )


CHUNKS = ((0, 3), (3, 3))
VOCAB = 64
KEPT = 1
AHEAD = "M~ M+K00 K10+X00+M K20+X10+D00+K01+M X20+D10+k11+M D20+K21+X01 N F0 X21+D01 D21 F1"
BACK = (
    "B0 G0 g0 p0 F0 B1 G1 g1 p1 F1+R0 B2 G2 g2 p2 F2+R1 B3 G3 g3 p3 F3+R2 B4 G4 g4 p4 F4+R3 B5 G5 g5 F5+R4 L "
    "R5+T R~ S0+T R+A0+T R~ S1+T X0 A1+T Z Y X1"
)
GROUPS = ((0, 1, 2, 3), (4, 5))


def body(
    numeric,
    cat_index,
    cardinality,
    emb_table,
    input_norm_gain,
    input_norm_bias,
    mask_logit,
    w_feat,
    w_state,
    gate_bias,
    head_w1,
    head_b1,
    head_w2,
    head_b2,
    cotangent,
):
    axes = ("dp", "wide", "narrow")
    rows, num = numeric.shape
    sections = w_feat.shape[0]
    feat = w_feat.shape[2] * lax.axis_size("narrow")
    emb = emb_table.shape[1]
    columns = cat_index.shape[1]
    classes = head_w2.shape[1]
    count = float(rows * lax.axis_size(axes))
    fast = is_fast()
    half = feat // 2
    cat, table = cat_index.T, emb_table.T
    turn = jnp.zeros((8, 128), F32)

    waiting = []

    def run(kernel, ins, outs, name, **more):
        nonlocal turn
        *v, turn = call(kernel, turn, [("v", x) for x in ins], outs, name, awaited=tuple(waiting), **more)
        waiting.clear()
        return v

    def together(jobs, pause=True):
        asked = [next(job) for job in jobs]

        def kernel(place, ins, outs):
            for one, sources, targets in asked:
                one(place, ins[: len(sources)], outs[: len(targets)])
                ins, outs = ins[len(sources) :], outs[len(targets) :]

        results = run(kernel, [v for a in asked for v in a[1]], [v for a in asked for v in a[2]], "step")
        for job, (_, _, targets) in zip(jobs, asked):
            try:
                job.send(results[: len(targets)])
            except StopIteration:
                pass
            results = results[len(targets) :]
        if pause:
            run(lambda place, ins, outs: None, [], [], "pause", work=WORK)

    if fast:
        arrays = (w_feat, w_state)
        tall = w_feat.shape[2] // 4
        *quarters, turn = call(
            quarters_kernel,
            turn,
            [("h", w) for w in arrays],
            [("v", (n, 2, 3, tall, w_feat.shape[3]), BF) for _, n in CHUNKS],
            "quarters",
            scratch=[pltpu.SemaphoreType.DMA((2 * len(CHUNKS),))],
        )
        came = {(0, g): along_narrow(v, 1) for g, v in enumerate(quarters)}
        across = [other_core(w) for w in arrays]
    raw, stats, counts, turn = prepare(turn, numeric, cat, cardinality, table, VOCAB)

    crossed, far, covered = {}, {}, {}
    held = [[] for _ in CHUNKS]
    slots = [[] for _ in CHUNKS]
    bundles = [[] for _ in CHUNKS]
    stored = []
    kept = []
    h = None
    norm = None
    merges = 0

    def collect(g, steps):
        ins, where, more, kinds = [], [], [], []
        block = quarters[g].shape
        n = block[0]
        for kind, hop in steps:
            if kind in "Kk":
                waits = held[g] if kind == "K" else []
                ins += [came[hop, g]] + [v for _, v in waits]
                covered[hop, g] = [other for other, _ in waits] + [hop]
                many = len(waits) + 1
                where.append((hop + 1, 0))
                more += [block] + ([(many * n,) + block[1:]] if many > 1 else [])
            else:
                ins += crossed[hop, g] if kind == "X" else far[hop, g]
                many = len(covered[hop, g])
                where += [(other + 1, way) for way in ((1, 2) if kind == "X" else (3,)) for other in covered[hop, g]]
                more += [(many * n,) + block[2:]] * 2 if kind == "X" else []
            kinds.append((kind, many))
        outs = [("v", (len(where),) + block, BF)] + [("v", v, BF) for v in more]
        bundle, *more = yield functools.partial(bundle_kernel, kinds), ins, outs
        slots[g] += [(len(bundles[g]), i) + at for i, at in enumerate(where)]
        bundles[g].append((bundle, other_core(bundle)))
        for (kind, hop), (_, many) in zip(steps, kinds):
            if kind in "Kk":
                got = more.pop(0)
                if hop < 2:
                    came[hop + 1, g] = along_narrow(got, 1)
                if kind == "k":
                    held[g] = [(hop, got)]
                else:
                    going = more.pop(0) if many > 1 else got
                    crossed[hop, g] = [along_dp(going, way) for way in (1, 2)]
            elif kind == "X":
                far[hop, g] = [along_dp(more.pop(0), way) for way in (2, 1)]

    def do_merge():
        nonlocal stats, merges
        axis, way = STEPS[merges]
        kernel = functools.partial(merge_kernel, float(rows * 2**merges))
        merges += 1
        (stats,) = yield kernel, [stats, lax.ppermute(stats, axis, way)], [("v", (2, feat), F32)]

    def advance(step):
        parts = step.rstrip("~").split("+")
        jobs = [do_merge()] if "M" in parts else []
        for g in range(len(CHUNKS)):
            steps = [(v[0], int(v[1])) for v in parts if v != "M" and int(v[2]) == g]
            jobs += [collect(g, steps)] if steps else []
        together(jobs, not step.endswith("~"))

    def do_norm(_):
        nonlocal norm
        ins = [stats, input_norm_gain.reshape(1, -1), input_norm_bias.reshape(1, -1)]
        norm = run(functools.partial(norm_kernel, count), ins, [("v", (8, feat), F32)], "norm")[0]

    def do_forward(i):
        nonlocal h, turn, kept
        s, n = CHUNKS[i]
        if fast:
            copies = Parts(s, n, slots[i])
            pieces = [("h", w) for w in arrays] + [("h", w) for w in across]
            pieces += [("a", v) for pair in bundles[i] for v in pair]
        else:
            copies, pieces = Whole(), [("h", w[s : s + n]) for w in whole]
        h, *held, turn = forward_sections(
            copies, s, n, KEPT if i + 1 == len(CHUNKS) else 0, turn, raw, h, norm, mask_logit, gate_bias, pieces, tuple(waiting)
        )
        waiting.clear()
        stored.extend((held[0], held[1], k) for k in range(n))
        kept = list(zip(held[2 : 2 + KEPT], held[2 + KEPT :]))

    if not fast:
        means = lax.all_gather(stats, axes)
        mean = jnp.mean(means[:, 0], 0)
        away = means[:, 0] - mean
        stats = jnp.stack([mean, jnp.sum(means[:, 1], 0) + rows * jnp.sum(away * away, 0)])
        whole = [
            lax.all_gather(lax.all_gather(w, "narrow", axis=2, tiled=True), "wide", axis=3, tiled=True)
            for w in (w_feat, w_state)
        ]
    for step in AHEAD.split():
        if step == "N":
            do_norm(0)
        elif step[0] == "F":
            do_forward(int(step[1:]))
        elif fast:
            advance(step)

    dh, logits, grad_w1, grad_w2, grad_b, turn = head(turn, h, head_w1, head_b1, head_w2.T, head_b2, cotangent.T)

    dn = None
    weights, saved = kept.pop()
    small = [None] * sections
    order = list(reversed(range(sections)))
    flight = {}
    halfway = lambda many: ("v", (many, 4, feat // 8, half), BF)
    flat = lambda many: ("v", (many, feat // 8, half), BF)
    at = layout(sections, classes, emb, columns * VOCAB, feat)
    result = {}

    def do_backward(t):
        nonlocal dh, dn, turn
        k = order[t]
        dh, dn, dbuf, lhs, small[k], turn = backward_section(
            k, turn, raw, saved, norm, mask_logit, weights, dh, dn
        )
        flight[t] = dbuf, lhs

    def do_fetch(t):
        nonlocal weights, saved, turn
        if kept:
            weights, saved = kept.pop()
            return
        *coming, index = stored[order[t] - 1]
        weights, saved, turn = call(
            functools.partial(fetch_kernel, index),
            turn,
            [("h", v) for v in coming],
            [("v", (1,) + v.shape[1:], BF) for v in coming],
            "fetch",
            work=WORK,
            scratch=[pltpu.SemaphoreType.DMA((2, 4))],
        )

    def columns(t, mine):
        kernel = functools.partial(gradients_kernel, mine)
        outs = [("v", (6, 4, feat // 4, half), BF)]
        return run(kernel, flight[t], outs, "gradients", limit=8, work=WORK)[0]

    def do_other(t):
        other = columns(t, False)
        if fast:
            other = other_core(other)
        flight[t] = flight[t], other

    def do_mine(t):
        flight[t], other = flight[t]
        flight[t] = [columns(t, True), other]
        if fast and t == 0:
            flight[t] += [grad_w1, other_core(grad_w1)]

    def do_fold(t):
        many = len(flight[t]) // 2 + 2
        v = yield fold_kernel, flight[t], [halfway(many), halfway(many), halfway(3), halfway(3)]
        flight[t] = [v[0], along_dp(v[1], 1), v[2], along_dp(v[3], 2)]

    ring = {"moving": None, "active": []}

    def do_ring(t):
        active = ring["active"]
        ins = [along_narrow(ring["moving"], 1)] if active else []
        ins += [parts[0] for _, parts in active]
        feats = [] if t is None else [flight[t][0].shape[0]]
        ins += [] if t is None else flight[t]
        going = sum(parts[0].shape[0] for _, parts in active if len(parts) > 1) + sum(v + 3 for v in feats)
        ended = [(k, parts[0].shape[0]) for k, parts in active if len(parts) == 1]
        outs = ([flat(going)] if going else []) + [flat(many) for _, many in ended]
        outs += [flat(v + 3) for v in feats for _ in range(3)]
        sizes = [(parts[0].shape[0], len(parts) == 1) for _, parts in active]
        v = yield functools.partial(ring_kernel, sizes, feats), ins, outs
        ring["moving"] = v.pop(0) if going else None
        flight.update((k, [v.pop(0)]) for k, _ in ended)
        ring["active"] = [(k, parts[1:]) for k, parts in active if len(parts) > 1]
        ring["active"] += [] if t is None else [(t, v)]

    def do_stack(g):
        ins = [flight[t][0] for t in GROUPS[g]]
        state = 3 * len(GROUPS[g])
        feats = sum(v.shape[0] for v in ins) - state
        v = yield stack_kernel, ins, [flat(feats), flat(state)]
        result[g] = [v[0], along_dp(v[0], 2), v[1], along_dp(v[1], 1)]

    def do_add(g):
        v = yield add_kernel, result[g], [flat(result[g][0].shape[0]), flat(result[g][2].shape[0])]
        result[g] = [v[0], along_dp(v[0], 1), v[1], along_dp(v[1], 2)]

    def do_local(_):
        ins = (raw, cat, dh, dn, norm, counts, grad_w2, grad_b, *small)
        outs = [("v", (at["rows"], feat), F32)]
        result["pack"] = run(
            functools.partial(sums_kernel, VOCAB, 256, at), ins, outs, "local_sums", limit=16, work=WORK
        )[0]
        result["steps"] = 0

    def do_total(_):
        pack = result["pack"]
        axis, way = STEPS[result["steps"]]
        result["steps"] += 1
        (result["pack"],) = yield add_kernel, [pack, lax.ppermute(pack, axis, way)], [("v", pack.shape, F32)]

    def do_blocks(g):
        nonlocal turn
        sectioned = [order[t] for t in GROUPS[g]]
        before = result.get("blocks")
        *v, turn = blocks(turn, sectioned, result[g], sections, 1 if g == 0 else 0, before)
        result["blocks"] = v[:2]
        if g == 0:
            result["last"] = [v[2]] + [along_narrow(v[2], hop) for hop in (1, 2, 3)]

    def do_head_rows(_):
        result["last"] = run(head_rows_kernel, result["last"], [("p", (feat, half), F32)], "head_rows")[0]

    def do_finish(_):
        nonlocal turn
        *result["finish"], turn = call(
            functools.partial(finish_kernel, VOCAB, count, at),
            turn,
            [("v", v) for v in (dh, dn, raw, norm, result["pack"], table)] + [("s", cardinality)],
            [
                ("p", (rows, num), F32),
                ("p", (emb, table.shape[1]), F32),
                ("p", (1, feat), F32),
                ("p", (1, feat), F32),
                ("p", mask_logit.shape, F32),
                ("p", gate_bias.shape, F32),
                ("p", (1, half), F32),
                ("p", (classes, half), F32),
                ("p", (1, classes), F32),
            ],
            "finish",
            limit=16,
            work=WORK,
        )

    tasks = {"B": do_backward, "p": do_fetch, "G": do_other, "g": do_mine, "L": do_local}
    if fast:
        tasks.update(X=do_blocks, Y=do_head_rows, Z=do_finish)
    steps = dict(F=do_fold, R=do_ring, S=do_stack, A=do_add, T=do_total)
    for step in BACK.split():
        if step[0] in tasks:
            tasks[step[0]](int(step[1:] or 0))
        elif fast and step[0] in steps:
            jobs = [steps[v[0]](int(v[1:]) if v[1:] else None) for v in step.rstrip("~").split("+")]
            together(jobs, not step.endswith("~"))
    if fast:
        grad_feat, grad_state = result["blocks"]
        grad_w1 = result["last"]
    else:
        halves = ([None] * sections, [None] * sections)
        for t in range(sections):
            local = jnp.concatenate(flight[t], axis=3).reshape(6, feat, feat)
            for a in range(2):
                part = lax.psum_scatter(local[3 * a : 3 * a + 3], "wide", scatter_dimension=2, tiled=True)
                part = lax.psum_scatter(part, "narrow", scatter_dimension=1, tiled=True)
                halves[a][order[t]] = lax.psum(part, "dp").astype(F32)
        result["pack"] = lax.psum(result["pack"], axes)
        do_finish(0)
        grad_feat, grad_state = (jnp.stack(v) for v in halves)
        grad_w1 = lax.psum(grad_w1.reshape(feat, -1).astype(F32), axes)
    grad_numeric, grad_table, plain, scaled, grad_mask, grad_bias, grad_b1, grad_w2, grad_b2 = result["finish"]
    return (
        logits.T,
        grad_numeric,
        grad_table.T,
        scaled.reshape(-1),
        plain.reshape(-1),
        grad_mask,
        grad_feat,
        grad_state,
        grad_bias,
        grad_w1,
        grad_b1.reshape(-1),
        grad_w2.T,
        grad_b2.reshape(-1),
    )


def solution(mesh):
    spread_rows = P(("dp", "wide", "narrow"), None)
    blocked = P(None, None, "narrow", "wide")
    in_specs = (spread_rows, spread_rows) + (P(),) * 5 + (blocked, blocked) + (P(),) * 5 + (spread_rows,)
    out_specs = (spread_rows, spread_rows) + (P(),) * 4 + (blocked, blocked) + (P(),) * 5
    return jax.shard_map(body, mesh=mesh, in_specs=in_specs, out_specs=out_specs, check_vma=False)
```

```python
import functools
import jax
import jax.numpy as jnp
from jax import lax
from jax.experimental import pallas as pl
from jax.experimental.pallas import tpu as pltpu
from jax.sharding import PartitionSpec as P

EPSILON = 1e-05
BF = jnp.bfloat16
F32 = jnp.float32
VMEM = pl.BlockSpec(memory_space=pltpu.VMEM)
SMEM = pl.BlockSpec(memory_space=pltpu.SMEM)
ANY = pl.BlockSpec(memory_space=pl.ANY)
MIB = 2**20
WORK = 3 * 10**10


def mdot(left, right):
    return lax.dot_general(left, right, (((1,), (0,)), ((), ())), preferred_element_type=F32)


def tdot(left, right):
    return lax.dot_general(left, right, (((0,), (0,)), ((), ())), preferred_element_type=F32)


def ndot(left, right):
    return lax.dot_general(left, right, (((1,), (1,)), ((), ())), preferred_element_type=F32)


def sigm(v):
    return 0.5 * jnp.tanh(0.5 * v) + 0.5


def call(kernel, turn, ins, outs, name, scratch=(), aliases=None, limit=4, work=0, awaited=()):
    specs = {"v": VMEM, "p": VMEM, "h": ANY, "a": ANY, "s": SMEM}
    memory = {"v": pltpu.VMEM, "h": pltpu.HBM}
    ins = [("v", turn)] + list(ins)
    used = len(ins)
    ins += [("a", x) for x in awaited]
    outs = [("v", turn.shape, turn.dtype)] + list(outs)
    given = [pltpu.with_memory_space_constraint(x, memory[kind]) if kind in memory else x for kind, x in ins]
    fast = is_fast()

    def shape(kind, dims, dtype):
        return memory[kind](dims, dtype) if kind in memory else jax.ShapeDtypeStruct(dims, dtype)

    def run(*refs):
        place = [lax.axis_index(a) if fast else 0 for a in ("narrow", "wide", "dp")]
        kernel(place, refs[1:used], refs[len(ins) + 1 : len(ins) + len(outs)], *refs[len(ins) + len(outs) :])

    turn, *results = pl.pallas_call(
        run,
        in_specs=[specs[kind] for kind, _ in ins],
        out_specs=[specs[o[0]] for o in outs],
        out_shape=[shape(*o) for o in outs],
        scratch_shapes=list(scratch),
        input_output_aliases={0: 0, **{i + 1: o + 1 for i, o in (aliases or {}).items()}},
        compiler_params=pltpu.CompilerParams(vmem_limit_bytes=limit * MIB),
        cost_estimate=pl.CostEstimate(flops=work, bytes_accessed=0, transcendentals=0),
        name=name,
    )(*given)
    return (*results, turn)


def is_fast():
    return tuple(lax.axis_size(a) for a in ("dp", "wide", "narrow")) == (4, 2, 4)


def forward_kernel(copies, s, n, first, keep, rb, place, ins, outs, weights, results, sems, outsem):
    raw, norm, mask, bias = ins[:4]
    pieces = ins[4:] if first else ins[5:]
    h_out, stored, kept = outs[:3]
    saved = [results.at[k] for k in range(n)]
    for k in range(keep):
        saved[n - keep + k] = outs[3 + keep + k].at[0]
    loads = copies.start(place, pieces, weights, sems)
    for copy in loads:
        copy.wait()
    stores = [pltpu.make_async_copy(weights, stored, outsem.at[0, 0])]
    for k in range(keep):
        held = weights.at[pl.ds(n - keep + k, 1)]
        stores.append(pltpu.make_async_copy(held, outs[3 + k], outsem.at[0, 1 + k]))
    for copy in stores:
        copy.start()
    for b in range(raw.shape[0] // rb):
        part = pl.ds(b * rb, rb)
        normed = (raw[part, :].astype(F32) - norm[0:1, :]) * norm[1:2, :] + norm[2:3, :]
        h = normed if first else ins[4][part, :]
        for k in range(n):
            feat = (normed * sigm(mask[s + k : s + k + 1, :])).astype(BF)
            low = h.astype(BF)
            saved[k][3, part, :] = low
            rpre = mdot(feat, weights[k, 0, 1]) + mdot(low, weights[k, 1, 1]) + bias[s + k, 1:2, :]
            r = sigm(rpre)
            upre = mdot(feat, weights[k, 0, 0]) + mdot(low, weights[k, 1, 0]) + bias[s + k, 0:1, :]
            u = sigm(upre)
            reset = (r * h).astype(BF)
            cpre = mdot(feat, weights[k, 0, 2]) + mdot(reset, weights[k, 1, 2]) + bias[s + k, 2:3, :]
            c = jnp.tanh(cpre)
            h = h + u * (c - h)
            saved[k][0, part, :] = u.astype(BF)
            saved[k][1, part, :] = r.astype(BF)
            saved[k][2, part, :] = c.astype(BF)
            if k < n - keep:
                stores.append(pltpu.make_async_copy(saved[k].at[:, part], kept.at[k, :, part], outsem.at[1 + b, k]))
                stores[-1].start()
        h_out[part, :] = h
    for copy in stores:
        copy.wait()


def forward_sections(copies, s, n, keep, turn, raw, h, norm, mask, bias, pieces, awaited, rb=512):
    rows, feat = raw.shape
    first = h is None
    ins = [("v", raw), ("v", norm), ("v", mask), ("v", bias)] + ([] if first else [("v", h)]) + pieces
    whole = (n, 2, 3, feat, feat)
    kept = (n, 4, rows, feat)
    outs = [("v", (rows, feat), F32), ("h", whole, BF), ("h", kept, BF)]
    outs += [("v", (1,) + whole[1:], BF)] * keep + [("v", (1,) + kept[1:], BF)] * keep
    scratch = [pltpu.VMEM(whole, BF), pltpu.VMEM(kept, BF)]
    scratch += [pltpu.SemaphoreType.DMA((copies.total,)), pltpu.SemaphoreType.DMA((1 + rows // rb, n + 1))]
    return call(
        functools.partial(forward_kernel, copies, s, n, first, keep, rb),
        turn,
        ins,
        outs,
        "forward_sections",
        work=WORK,
        scratch=scratch,
        aliases={} if first else {4: 0},
        limit=12 + 8 * n,
        awaited=awaited,
    )


def fetch(index, sources, targets, sems):
    copies = [
        pltpu.make_async_copy(source.at[pl.ds(index, 1), pl.ds(j, 1)], target.at[:, pl.ds(j, 1)], sems.at[i, j])
        for i, (source, target) in enumerate(zip(sources, targets))
        for j in range(source.shape[1])
    ]
    for copy in copies:
        copy.start()
    return copies


def backward_kernel(s, rb, first, place, ins, outs):
    raw, saved, norm, mask, weights, dh_in = ins[:6]
    dn_in = None if first else ins[6]
    dh_out, dn_out, dbuf, lhs, small = outs
    rows = raw.shape[0]
    gate_mask = sigm(mask[s : s + 1, :])
    sums = [jnp.zeros((1, gate_mask.shape[1]), F32)] * 4
    for b in range(rows // rb):
        part = pl.ds(b * rb, rb)
        u = saved[0, 0, part, :].astype(F32)
        c = saved[0, 2, part, :].astype(F32)
        dh = dh_in[part, :]
        t = dh * u
        dc = (t * (1.0 - c * c)).astype(BF)
        dreset = ndot(dc, weights[0, 1, 2])
        low = saved[0, 3, part, :]
        h = low.astype(F32)
        du = (t * (c - h) * (1.0 - u)).astype(BF)
        dbuf[2, part, :] = dc
        dbuf[0, part, :] = du
        dfeat = ndot(dc, weights[0, 0, 2]) + ndot(du, weights[0, 0, 0])
        state = ndot(du, weights[0, 1, 0])
        normed = (raw[part, :].astype(F32) - norm[0:1, :]) * norm[1:2, :] + norm[2:3, :]
        feat = (normed * gate_mask).astype(BF)
        r = saved[0, 1, part, :].astype(F32)
        rh = r * h
        dr = (dreset * rh * (1.0 - r)).astype(BF)
        dbuf[1, part, :] = dr
        lhs[0, :, part] = feat.T
        lhs[1, :, part] = low.T
        lhs[2, :, part] = rh.astype(BF).T
        dfeat = dfeat + ndot(dr, weights[0, 0, 1])
        dh_out[part, :] = (dh - t) + dreset * r + state + ndot(dr, weights[0, 1, 1])
        dn_out[part, :] = dfeat * gate_mask if first else dn_in[part, :] + dfeat * gate_mask
        for i, v in enumerate((du.astype(F32), dr.astype(F32), dc.astype(F32), dfeat * normed)):
            sums[i] = sums[i] + jnp.sum(v, 0, keepdims=True)
    slope = gate_mask * (1.0 - gate_mask)
    small[...] = jnp.concatenate(sums[:3] + [sums[3] * slope] + [jnp.zeros_like(slope)] * 4, axis=0)


def backward_section(s, turn, raw, saved, norm, mask, weights, dh, dn, rb=256):
    rows, feat = raw.shape
    first = dn is None
    ins = [("v", v) for v in (raw, saved, norm, mask, weights, dh)] + ([] if first else [("v", dn)])
    outs = [("v", (rows, feat), F32)] * 2 + [("v", (3, rows, feat), BF), ("v", (3, feat, rows), BF)]
    outs += [("v", (8, feat), F32)]
    return call(
        functools.partial(backward_kernel, s, rb, first),
        turn,
        ins,
        outs,
        "backward_section",
        work=WORK,
        aliases={5: 0} if first else {5: 0, 6: 1},
        limit=9,
    )


def fetch_kernel(index, place, ins, outs, sems):
    for copy in fetch(index, ins, outs, sems):
        copy.wait()


def gradients_kernel(mine, place, ins, outs):
    dbuf, lhs = ins
    out = outs[0]
    half = out.shape[-1]
    core = place[1] if mine else 1 - place[1]
    columns = pl.ds(pl.multiple_of(core * half, half), half)
    for m in range(6):
        which = 0 if m < 3 else (1 if m < 5 else 2)
        out[m] = mdot(lhs[which], dbuf[m % 3, :, columns]).astype(BF).reshape(out.shape[1:])


class Whole:
    total = 2

    def start(self, place, pieces, weights, sems):
        copies = [pltpu.make_async_copy(pieces[a], weights.at[:, a], sems.at[a]) for a in range(2)]
        for copy in copies:
            copy.start()
        return copies


def spread(table_rows, vocab, offsets, columns):
    row = lax.broadcasted_iota(jnp.int32, (vocab, table_rows), 0)
    lane = lax.broadcasted_iota(jnp.int32, (vocab, table_rows), 1)
    return jnp.concatenate([(lane == row + offsets[c]).astype(BF) for c in range(columns)], axis=0)


def column_offsets(cardinality, columns):
    offsets, total = [], 0
    for c in range(columns):
        offsets.append(total)
        total = total + cardinality[c]
    return offsets


def onehot(cat, vocab):
    columns = cat.shape[0]
    width = columns * vocab
    lane = lax.broadcasted_iota(jnp.int32, (columns, width), 1)
    owner = lax.broadcasted_iota(jnp.int32, (columns, width), 0)
    repeat = (lane // vocab == owner).astype(BF)
    values = tdot(cat.astype(F32).astype(BF), repeat)
    wanted = (lax.broadcasted_iota(jnp.int32, (1, width), 1) % vocab).astype(F32)
    return (values == wanted).astype(BF)


def prepare_kernel(vocab, rb, place, ins, outs):
    numeric, cat, cardinality, table = ins
    raw, stats, counts = outs
    rows, num = numeric.shape
    columns, (emb, table_rows) = cat.shape[0], table.shape
    width = columns * emb
    chosen = spread(table_rows, vocab, column_offsets(cardinality, columns), columns)
    tile = (
        lax.broadcasted_iota(jnp.int32, (emb, width), 1) % emb
        == lax.broadcasted_iota(jnp.int32, (emb, width), 0)
    ).astype(BF)
    placed = mdot(chosen, tdot(table[...], tile).astype(BF))
    own = (
        lax.broadcasted_iota(jnp.int32, placed.shape, 1) // emb
        == lax.broadcasted_iota(jnp.int32, placed.shape, 0) // vocab
    )
    blocks = jnp.where(own, placed, 0.0).astype(BF)
    total = jnp.zeros((1, num + width), F32)
    counted = jnp.zeros((1, columns * vocab), F32)
    for b in range(rows // rb):
        part = pl.ds(b * rb, rb)
        hot = onehot(cat[:, part], vocab)
        looked = mdot(hot, blocks)
        raw[part, :num] = numeric[part, :]
        raw[part, num:] = looked.astype(BF)
        total = total + jnp.concatenate(
            [jnp.sum(numeric[part, :].astype(F32), 0, keepdims=True), jnp.sum(looked, 0, keepdims=True)], axis=1
        )
        counted = counted + mdot(jnp.ones((8, rb), BF), hot)[0:1, :]
    mean = total / rows
    squares = jnp.zeros_like(total)
    for b in range(rows // rb):
        away = raw[pl.ds(b * rb, rb), :].astype(F32) - mean
        squares = squares + jnp.sum(away * away, 0, keepdims=True)
    stats[0:1, :] = mean
    stats[1:2, :] = squares
    counts[...] = counted


def prepare(turn, numeric, cat, cardinality, table, vocab):
    rows, num = numeric.shape
    feat = num + cat.shape[0] * table.shape[0]
    return call(
        functools.partial(prepare_kernel, vocab, 256),
        turn,
        [("v", numeric), ("v", cat), ("s", cardinality), ("v", table)],
        [("v", (rows, feat), BF), ("v", (2, feat), F32), ("v", (1, cat.shape[0] * vocab), F32)],
        "prepare",
        work=WORK,
        limit=24,
    )


def merge_kernel(count, place, ins, outs):
    one, two = ins
    out = outs[0]
    apart = one[0:1, :] - two[0:1, :]
    out[0:1, :] = 0.5 * (one[0:1, :] + two[0:1, :])
    out[1:2, :] = one[1:2, :] + two[1:2, :] + apart * apart * (0.5 * count)


def norm_kernel(count, place, ins, outs):
    stats, gain, bias = ins
    out = outs[0]
    inverse = lax.rsqrt(stats[1:2, :] / count + EPSILON)
    out[0:1, :] = stats[0:1, :]
    out[1:2, :] = inverse * gain[...]
    out[2:3, :] = bias[...]
    out[3:4, :] = inverse
    out[4:5, :] = gain[...]
    out[5:8, :] = jnp.zeros((3, inverse.shape[1]), F32)


def head_kernel(rb, place, ins, outs, hidden, slopes):
    h, w1, b1, w2, b2, g = ins
    dh, logits, grad_w1, grad_w2, grad_b = outs
    rows = h.shape[0]
    width = w1.shape[1]
    classes = w2.shape[0]
    eye = lax.broadcasted_iota(jnp.int32, (classes, classes), 0) == lax.broadcasted_iota(
        jnp.int32, (classes, classes), 1
    )
    shift = jnp.sum(jnp.where(eye, b2[...], 0.0), 1, keepdims=True)
    two = jnp.zeros(w2.shape, F32)
    sums = jnp.zeros((1, width), F32)
    for b in range(rows // rb):
        part = pl.ds(b * rb, rb)
        head_in = h[part, :].astype(BF)
        hidden[part, :] = head_in
        x = mdot(head_in, w1[...]) + b1[...]
        phi = 0.5 * (1.0 + lax.erf(x * 0.7071067811865476))
        act = (x * phi).astype(BF)
        logits[:, part] = ndot(w2[...], act) + shift
        dact = tdot(g[:, part], w2[...])
        slope = phi + x * (jnp.exp(-0.5 * x * x) * 0.3989422804014327)
        dx = (dact * slope).astype(BF)
        slopes[part, :] = dx
        dh[part, :] = ndot(dx, w1[...])
        two = two + mdot(g[:, part], act)
        sums = sums + jnp.sum(dx.astype(F32), 0, keepdims=True)
    one = tdot(hidden[...], slopes[...]).astype(BF)
    depth = grad_w1.shape[1]
    for i in range(grad_w1.shape[0]):
        grad_w1[i] = one[i * depth : (i + 1) * depth]
    grad_w2[...] = two
    grad_b[...] = jnp.zeros_like(grad_b)
    grad_b[0:1, :] = sums
    grad_b[1:2, : g.shape[0]] = ndot(jnp.ones((8, rows), BF), g[...])[0:1, :]


def head(turn, h, w1, b1, w2, b2, g):
    rows, feat = h.shape
    classes, hidden = w2.shape
    return call(
        functools.partial(head_kernel, 256),
        turn,
        [("v", v) for v in (h, w1, b1.reshape(1, -1), w2, b2.reshape(1, -1), g)],
        [
            ("v", (rows, feat), F32),
            ("p", (classes, rows), F32),
            ("v", (4, feat // 4, hidden), BF),
            ("v", (classes, hidden), F32),
            ("v", (8, hidden), F32),
        ],
        "head",
        work=WORK,
        scratch=[pltpu.VMEM((rows, feat), BF), pltpu.VMEM((rows, hidden), BF)],
        aliases={0: 0},
        limit=16,
    )


def layout(sections, classes, emb, width, feat):
    at = {"sums": 0, "small": 2}
    at["bias"] = at["small"] + 4 * sections
    at["w2"] = at["bias"] + 1
    at["counts"] = at["w2"] + -(-classes // 2)
    at["table"] = -(-(at["counts"] + width // feat) // 8) * 8
    at["rows"] = at["table"] + emb * width // feat
    return at


def sums_kernel(vocab, rb, at, place, ins, outs):
    raw, cat, dh, dn, norm, counts, grad_w2, grad_b = ins[:8]
    small = ins[8:]
    pack = outs[0]
    rows, feat = raw.shape
    columns = cat.shape[0]
    width = columns * vocab
    emb = (pack.shape[0] - at["table"]) * feat // width
    num = feat - columns * emb
    plain = jnp.zeros((1, feat), F32)
    scaled = jnp.zeros((1, feat), F32)
    crossed = jnp.zeros((columns * emb, width), F32)
    for b in range(rows // rb):
        part = pl.ds(b * rb, rb)
        grad = dh[part, :] + dn[part, :]
        away = raw[part, :].astype(F32) - norm[0:1, :]
        plain = plain + jnp.sum(grad, 0, keepdims=True)
        scaled = scaled + jnp.sum(grad * away, 0, keepdims=True)
        hot = onehot(cat[:, part], vocab)
        pieces = grad[:, num:]
        high = pieces.astype(BF)
        rest = (pieces - high.astype(F32)).astype(BF)
        crossed = crossed + tdot(high, hot) + tdot(rest, hot)
    own = (
        lax.broadcasted_iota(jnp.int32, crossed.shape, 0) // emb
        == lax.broadcasted_iota(jnp.int32, crossed.shape, 1) // vocab
    )
    crossed = jnp.where(own, crossed, 0.0)
    table = crossed[:emb]
    for c in range(1, columns):
        table = table + crossed[c * emb : (c + 1) * emb]
    pack[...] = jnp.zeros_like(pack)
    pack[0:1, :] = plain
    pack[1:2, :] = scaled * norm[3:4, :]
    for k, v in enumerate(small):
        pack[at["small"] + 4 * k : at["small"] + 4 * k + 4, :] = v[:4, :]
    half = feat // 2
    pack[at["bias"] : at["bias"] + 1, :half] = grad_b[0:1, :]
    pack[at["bias"] : at["bias"] + 1, half:] = grad_b[1:2, :]
    for i in range(grad_w2.shape[0]):
        row = at["w2"] + i // 2
        pack[row : row + 1, (i % 2) * half : (i % 2 + 1) * half] = grad_w2[i : i + 1, :]
    for i in range(width // feat):
        pack[at["counts"] + i : at["counts"] + i + 1, :] = counts[:, i * feat : (i + 1) * feat]
        pack[at["table"] + i * emb : at["table"] + (i + 1) * emb, :] = table[:, i * feat : (i + 1) * feat]


def exact_dot(left, right):
    high = left.astype(BF)
    left = left - high.astype(F32)
    middle = left.astype(BF)
    low = (left - middle.astype(F32)).astype(BF)
    return mdot(high, right) + mdot(middle, right) + mdot(low, right)


def finish_kernel(vocab, count, at, place, ins, outs):
    dh, dn, raw, norm, pack, table, cardinality = ins
    grad, grad_table, plain_out, scaled_out, grad_mask, grad_bias, grad_b1, grad_w2, grad_b2 = outs
    feat = raw.shape[1]
    num = grad.shape[1]
    emb, table_rows = table.shape
    columns = (feat - num) // emb
    width = columns * vocab
    mean, inverse, gain = norm[0:1, :], norm[3:4, :], norm[4:5, :]
    plain_out[...] = pack[0:1, :]
    scaled_out[...] = pack[1:2, :]
    plain = pack[0:1, :] / count
    scaled = pack[1:2, :] / count
    factor = gain * inverse
    for b in range(raw.shape[0] // 256):
        part = pl.ds(b * 256, 256)
        away = (raw[part, :num].astype(F32) - mean[:, :num]) * inverse[:, :num]
        both = dh[part, :num] + dn[part, :num]
        grad[part, :] = factor[:, :num] * (both - plain[:, :num] - away * scaled[:, :num])
    for k in range(grad_mask.shape[0]):
        rows = pack[at["small"] + 4 * k : at["small"] + 4 * k + 4, :]
        grad_bias[k] = rows[:3]
        grad_mask[k : k + 1, :] = rows[3:4]
    half = feat // 2
    grad_b1[...] = pack[at["bias"] : at["bias"] + 1, :half]
    grad_b2[...] = pack[at["bias"] : at["bias"] + 1, half : half + grad_b2.shape[1]]
    for i in range(grad_w2.shape[0]):
        row = at["w2"] + i // 2
        grad_w2[i : i + 1, :] = pack[row : row + 1, (i % 2) * half : (i % 2 + 1) * half]
    flat = columns * emb
    mine = (
        lax.broadcasted_iota(jnp.int32, (emb, flat), 1) % emb
        == lax.broadcasted_iota(jnp.int32, (emb, flat), 0)
    )
    expand = (
        lax.broadcasted_iota(jnp.int32, (flat, width), 0) // emb
        == lax.broadcasted_iota(jnp.int32, (flat, width), 1) // vocab
    ).astype(BF)
    vectors = [jnp.where(mine, v[:, num:], 0.0) for v in (mean, inverse, plain, scaled, factor)]
    wide = exact_dot(jnp.concatenate(vectors, axis=0), expand)
    mean_w, inverse_w, plain_w, scaled_w, factor_w = [wide[i * emb : (i + 1) * emb] for i in range(5)]
    chosen = spread(table_rows, vocab, column_offsets(cardinality, columns), columns)
    away = (ndot(table[...], chosen) - mean_w) * inverse_w
    steps = range(width // feat)
    counts = jnp.concatenate([pack[at["counts"] + i : at["counts"] + i + 1, :] for i in steps], axis=1)
    sums = jnp.concatenate([pack[at["table"] + i * emb : at["table"] + (i + 1) * emb, :] for i in steps], axis=1)
    grad_table[...] = exact_dot(factor_w * (sums - counts * (plain_w + away * scaled_w)), chosen)


class Parts:
    def __init__(self, s, n, slots):
        self.s, self.n, self.slots = s, n, slots
        self.total = 4 + 2 * len(slots)

    def start(self, place, pieces, weights, sems):
        depth, width = pieces[0].shape[2:]
        tall = depth // 4
        z, c, d = place[0], place[1], place[2]
        copies = []

        def add(source, arrays, row, rows, core):
            column = (c if core == 0 else 1 - c) * width
            copies.append(
                pltpu.make_async_copy(
                    source,
                    weights.at[
                        :,
                        arrays,
                        :,
                        pl.ds(pl.multiple_of(row, rows), rows),
                        pl.ds(pl.multiple_of(column, width), width),
                    ],
                    sems.at[len(copies)],
                )
            )

        for core in range(2):
            for a in range(2):
                add(pieces[2 * core + a].at[pl.ds(self.s, self.n)], a, z * depth, depth, core)
        for bundle, slot, hops, way in self.slots:
            quarter = lax.bitwise_xor(d, way) if way else d
            row = lax.rem(z + 4 - hops, 4) * depth + quarter * tall
            for core in range(2):
                add(pieces[4 + 2 * bundle + core].at[slot], slice(None), row, tall, core)
        for copy in copies:
            copy.start()
        return copies


SWAP = [(0, 1), (1, 0)]
ACROSS = {1: [(0, 1), (1, 0), (2, 3), (3, 2)], 2: [(0, 2), (2, 0), (1, 3), (3, 1)]}
NEAR = [(0, 1), (1, 0), (2, 3), (3, 2)]
FAR = [(0, 2), (1, 3), (2, 0), (3, 1)]


def other_core(v):
    return lax.ppermute(v, "wide", SWAP)


def along_dp(v, way):
    return lax.ppermute(v, "dp", ACROSS[way])


def along_narrow(v, hops):
    return lax.ppermute(v, "narrow", [(i, (i + hops) % 4) for i in range(4)])


def quarters_kernel(place, ins, outs, sems):
    tall = ins[0].shape[2] // 4
    rows = pl.ds(pl.multiple_of(place[2] * tall, tall), tall)
    copies = []
    for (s, n), out in zip(CHUNKS, outs):
        for a in range(2):
            copies.append(
                pltpu.make_async_copy(ins[a].at[pl.ds(s, n), :, rows], out.at[:, a], sems.at[len(copies)])
            )
    for copy in copies:
        copy.start()
    for copy in copies:
        copy.wait()


def bundle_kernel(kinds, place, ins, outs):
    ins, bundle, outs = list(ins), outs[0], list(outs[1:])
    n = bundle.shape[1]
    slot = 0
    for kind, many in kinds:
        if kind in "Kk":
            block = ins.pop(0)[...]
            bundle[slot] = block
            out = outs.pop(0)
            out[...] = block
            slot += 1
            if many > 1:
                out = outs.pop(0)
                for i in range(many):
                    out[i * n : (i + 1) * n] = ins.pop(0)[...] if i + 1 < many else block
        elif kind == "X":
            for a in range(2):
                block = ins.pop(0)
                for i in range(many):
                    bundle[slot + i] = block[i * n : (i + 1) * n]
                outs.pop(0)[...] = block[:, a]
                slot += many
        else:
            for a in range(2):
                block = ins.pop(0)
                for i in range(many):
                    bundle[slot + i, :, a] = block[i * n : (i + 1) * n]
            slot += many


STEPS = [("wide", SWAP), ("dp", ACROSS[1]), ("dp", ACROSS[2]), ("narrow", NEAR), ("narrow", FAR)]


def half_rows(place, a, kept, tall):
    side = lax.rem(place[2], 2) if a == 0 else lax.div(place[2], 2)
    return pl.ds(pl.multiple_of((side if kept else 1 - side) * tall, tall), tall)


def fold_kernel(place, ins, outs):
    tall = outs[0].shape[2]
    for a in range(2):
        keep, send = outs[2 * a], outs[2 * a + 1]
        pairs = [(ins[0].at[3 * a + j], ins[1].at[3 * a + j]) for j in range(3)]
        if a == 0 and len(ins) == 4:
            pairs.append((ins[2], ins[3]))
        for j, (mine, came) in enumerate(pairs):
            for out, kept in ((keep, True), (send, False)):
                rows = half_rows(place, a, kept, tall)
                for b in range(4):
                    out[j, b] = (mine[b, rows, :].astype(F32) + came[b, rows, :].astype(F32)).astype(BF)


def ring_kernel(active, new, place, ins, outs):
    ins, outs = list(ins), list(outs)
    came = ins.pop(0) if active else None
    on = outs.pop(0) if new or not all(last for _, last in active) else None
    source = target = 0
    for many, last in active:
        mine = ins.pop(0)
        out, first = (outs.pop(0), 0) if last else (on, target)
        for j in range(many):
            out[first + j] = (came[source + j].astype(F32) + mine[j].astype(F32)).astype(BF)
        source += many
        target += 0 if last else many
    for feats in new:
        stages = [(on, target)] + [(outs.pop(0), 0) for _ in range(3)]
        done = 0
        for many in (feats, 3):
            keep, got = ins.pop(0), ins.pop(0)
            for hop, (out, first) in enumerate(stages):
                block = lax.rem(place[0] + 3 - hop, 4)
                for j in range(many):
                    total = keep[j, block].astype(F32) + got[j, block].astype(F32)
                    out[first + done + j] = total.astype(BF)
            done += many
        target += done


def stack_kernel(place, ins, outs):
    at = [0, 0]
    for v in ins:
        for j in range(v.shape[0]):
            a = 0 if j < v.shape[0] - 3 else 1
            outs[a][at[a]] = v[j]
            at[a] += 1


def add_kernel(place, ins, outs):
    for i, out in enumerate(outs):
        out[...] = (ins[2 * i][...].astype(F32) + ins[2 * i + 1][...].astype(F32)).astype(out.dtype)


def blocks_kernel(order, extra, place, ins, outs, buf, sems):
    tall = ins[0].shape[1]
    copies = []
    for i, k in enumerate(order):
        for a in range(2):
            mine, away = ins[2 * a], ins[2 * a + 1]
            for j in range(3):
                at = 3 * i + j + (extra if a == 0 and i else 0)
                buf[a, i, j, half_rows(place, a, True, tall), :] = mine[at].astype(F32)
                buf[a, i, j, half_rows(place, a, False, tall), :] = away[at].astype(F32)
            copies.append(pltpu.make_async_copy(buf.at[a, i], outs[a].at[k], sems.at[a, i]))
            copies[-1].start()
    if extra:
        outs[2][half_rows(place, 0, True, tall), :] = ins[0][3]
        outs[2][half_rows(place, 0, False, tall), :] = ins[1][3]
    for copy in copies:
        copy.wait()


def head_rows_kernel(place, ins, outs):
    depth = ins[0].shape[0]
    for hop, v in enumerate(ins):
        row = lax.rem(place[0] + 4 - hop, 4) * depth
        outs[0][pl.ds(pl.multiple_of(row, depth), depth), :] = v[...].astype(F32)


def blocks(turn, order, parts, sections, extra, before=None):
    ins = [("v", v) for v in parts]
    tall, width = parts[0].shape[1:]
    shape = (sections, 3, 2 * tall, width)
    outs = [("a", shape, F32)] * 2 + ([("v", (2 * tall, width), BF)] if extra else [])
    kernel = functools.partial(blocks_kernel, order, extra)
    if before is not None:
        inner = kernel
        kernel = lambda place, ins, outs, *rest: inner(place, ins[:4], outs, *rest)
        ins += [("a", v) for v in before]
    return call(
        kernel,
        turn,
        ins,
        outs,
        "blocks",
        scratch=[pltpu.VMEM((2, len(order)) + shape[1:], F32), pltpu.SemaphoreType.DMA((2, len(order)))],
        aliases={} if before is None else {4: 0, 5: 1},
        limit=10,
    )


CHUNKS = ((0, 3), (3, 3))
VOCAB = 64
KEPT = 1
AHEAD = (
    "M~", "M+K00", "K10+X00+M", "K20+X10+D00+K01+M", "X20+D10+k11+M", "D20+K21+X01", "N", "F0", "X21+D01",
    "D21", "F1",
)
BACK = (
    "B0", "G0", "g0", "p0", "F0", "B1", "G1", "g1", "p1", "F1+R0", "B2", "G2", "g2", "p2", "F2+R1", "B3",
    "G3", "g3", "p3", "F3+R2", "B4", "G4", "g4", "p4", "F4+R3", "B5", "G5", "g5", "F5+R4", "L", "R5+T", "R~",
    "S0+T", "R+A0+T", "R~", "S1+T", "X0", "A1+T", "Z", "Y", "X1",
)
GROUPS = ((0, 1, 2, 3), (4, 5))


def body(
    numeric,
    cat_index,
    cardinality,
    emb_table,
    input_norm_gain,
    input_norm_bias,
    mask_logit,
    w_feat,
    w_state,
    gate_bias,
    head_w1,
    head_b1,
    head_w2,
    head_b2,
    cotangent,
):
    axes = ("dp", "wide", "narrow")
    rows, num = numeric.shape
    sections = w_feat.shape[0]
    feat = w_feat.shape[2] * lax.axis_size("narrow")
    emb = emb_table.shape[1]
    columns = cat_index.shape[1]
    classes = head_w2.shape[1]
    count = float(rows * lax.axis_size(axes))
    fast = is_fast()
    half = feat // 2
    cat, table = cat_index.T, emb_table.T
    turn = jnp.zeros((8, 128), F32)

    waiting = []

    def run(kernel, ins, outs, name, **more):
        nonlocal turn
        *v, turn = call(kernel, turn, [("v", x) for x in ins], outs, name, awaited=tuple(waiting), **more)
        waiting.clear()
        return v

    def together(jobs, pause=True):
        asked = [next(job) for job in jobs]

        def kernel(place, ins, outs):
            for one, sources, targets in asked:
                one(place, ins[: len(sources)], outs[: len(targets)])
                ins, outs = ins[len(sources) :], outs[len(targets) :]

        results = run(kernel, [v for a in asked for v in a[1]], [v for a in asked for v in a[2]], "step")
        for job, (_, _, targets) in zip(jobs, asked):
            try:
                job.send(results[: len(targets)])
            except StopIteration:
                pass
            results = results[len(targets) :]
        if pause:
            run(lambda place, ins, outs: None, [], [], "pause", work=WORK)

    if fast:
        arrays = (w_feat, w_state)
        tall = w_feat.shape[2] // 4
        *quarters, turn = call(
            quarters_kernel,
            turn,
            [("h", w) for w in arrays],
            [("v", (n, 2, 3, tall, w_feat.shape[3]), BF) for _, n in CHUNKS],
            "quarters",
            scratch=[pltpu.SemaphoreType.DMA((2 * len(CHUNKS),))],
        )
        came = {(0, g): along_narrow(v, 1) for g, v in enumerate(quarters)}
        across = [other_core(w) for w in arrays]
    raw, stats, counts, turn = prepare(turn, numeric, cat, cardinality, table, VOCAB)

    crossed, far, covered = {}, {}, {}
    held = [[] for _ in CHUNKS]
    slots = [[] for _ in CHUNKS]
    bundles = [[] for _ in CHUNKS]
    stored = []
    kept = []
    h = None
    norm = None
    merges = 0

    def collect(g, steps):
        ins, where, more, kinds = [], [], [], []
        block = quarters[g].shape
        n = block[0]
        for kind, hop in steps:
            if kind in "Kk":
                waits = held[g] if kind == "K" else []
                ins += [came[hop, g]] + [v for _, v in waits]
                covered[hop, g] = [other for other, _ in waits] + [hop]
                many = len(waits) + 1
                where.append((hop + 1, 0))
                more += [block] + ([(many * n,) + block[1:]] if many > 1 else [])
            else:
                ins += crossed[hop, g] if kind == "X" else far[hop, g]
                many = len(covered[hop, g])
                where += [(other + 1, way) for way in ((1, 2) if kind == "X" else (3,)) for other in covered[hop, g]]
                more += [(many * n,) + block[2:]] * 2 if kind == "X" else []
            kinds.append((kind, many))
        outs = [("v", (len(where),) + block, BF)] + [("v", v, BF) for v in more]
        bundle, *more = yield functools.partial(bundle_kernel, kinds), ins, outs
        slots[g] += [(len(bundles[g]), i) + at for i, at in enumerate(where)]
        bundles[g].append((bundle, other_core(bundle)))
        for (kind, hop), (_, many) in zip(steps, kinds):
            if kind in "Kk":
                got = more.pop(0)
                if hop < 2:
                    came[hop + 1, g] = along_narrow(got, 1)
                if kind == "k":
                    held[g] = [(hop, got)]
                else:
                    going = more.pop(0) if many > 1 else got
                    crossed[hop, g] = [along_dp(going, way) for way in (1, 2)]
            elif kind == "X":
                far[hop, g] = [along_dp(more.pop(0), way) for way in (2, 1)]

    def do_merge():
        nonlocal stats, merges
        axis, way = STEPS[merges]
        kernel = functools.partial(merge_kernel, float(rows * 2**merges))
        merges += 1
        (stats,) = yield kernel, [stats, lax.ppermute(stats, axis, way)], [("v", (2, feat), F32)]

    def advance(step):
        parts = step.rstrip("~").split("+")
        jobs = [do_merge()] if "M" in parts else []
        for g in range(len(CHUNKS)):
            steps = [(v[0], int(v[1])) for v in parts if v != "M" and int(v[2]) == g]
            jobs += [collect(g, steps)] if steps else []
        together(jobs, not step.endswith("~"))

    def do_norm(_):
        nonlocal norm
        ins = [stats, input_norm_gain.reshape(1, -1), input_norm_bias.reshape(1, -1)]
        norm = run(functools.partial(norm_kernel, count), ins, [("v", (8, feat), F32)], "norm")[0]

    def do_forward(i):
        nonlocal h, turn, kept
        s, n = CHUNKS[i]
        if fast:
            copies = Parts(s, n, slots[i])
            pieces = [("h", w) for w in arrays] + [("h", w) for w in across]
            pieces += [("a", v) for pair in bundles[i] for v in pair]
        else:
            copies, pieces = Whole(), [("h", w[s : s + n]) for w in whole]
        h, *held, turn = forward_sections(
            copies, s, n, KEPT if i + 1 == len(CHUNKS) else 0, turn, raw, h, norm, mask_logit, gate_bias, pieces, tuple(waiting)
        )
        waiting.clear()
        stored.extend((held[0], held[1], k) for k in range(n))
        kept = list(zip(held[2 : 2 + KEPT], held[2 + KEPT :]))

    if not fast:
        means = lax.all_gather(stats, axes)
        mean = jnp.mean(means[:, 0], 0)
        away = means[:, 0] - mean
        stats = jnp.stack([mean, jnp.sum(means[:, 1], 0) + rows * jnp.sum(away * away, 0)])
        whole = [
            lax.all_gather(lax.all_gather(w, "narrow", axis=2, tiled=True), "wide", axis=3, tiled=True)
            for w in (w_feat, w_state)
        ]
    for step in AHEAD:
        if step == "N":
            do_norm(0)
        elif step[0] == "F":
            do_forward(int(step[1:]))
        elif fast:
            advance(step)

    dh, logits, grad_w1, grad_w2, grad_b, turn = head(turn, h, head_w1, head_b1, head_w2.T, head_b2, cotangent.T)

    dn = None
    weights, saved = kept.pop()
    small = [None] * sections
    order = list(reversed(range(sections)))
    flight = {}
    halfway = lambda many: ("v", (many, 4, feat // 8, half), BF)
    flat = lambda many: ("v", (many, feat // 8, half), BF)
    at = layout(sections, classes, emb, columns * VOCAB, feat)
    result = {}

    def do_backward(t):
        nonlocal dh, dn, turn
        k = order[t]
        dh, dn, dbuf, lhs, small[k], turn = backward_section(
            k, turn, raw, saved, norm, mask_logit, weights, dh, dn
        )
        flight[t] = dbuf, lhs

    def do_fetch(t):
        nonlocal weights, saved, turn
        if kept:
            weights, saved = kept.pop()
            return
        *coming, index = stored[order[t] - 1]
        weights, saved, turn = call(
            functools.partial(fetch_kernel, index),
            turn,
            [("h", v) for v in coming],
            [("v", (1,) + v.shape[1:], BF) for v in coming],
            "fetch",
            work=WORK,
            scratch=[pltpu.SemaphoreType.DMA((2, 4))],
        )

    def columns(t, mine):
        kernel = functools.partial(gradients_kernel, mine)
        outs = [("v", (6, 4, feat // 4, half), BF)]
        return run(kernel, flight[t], outs, "gradients", limit=8, work=WORK)[0]

    def do_other(t):
        other = columns(t, False)
        if fast:
            other = other_core(other)
        flight[t] = flight[t], other

    def do_mine(t):
        flight[t], other = flight[t]
        flight[t] = [columns(t, True), other]
        if fast and t == 0:
            flight[t] += [grad_w1, other_core(grad_w1)]

    def do_fold(t):
        many = len(flight[t]) // 2 + 2
        v = yield fold_kernel, flight[t], [halfway(many), halfway(many), halfway(3), halfway(3)]
        flight[t] = [v[0], along_dp(v[1], 1), v[2], along_dp(v[3], 2)]

    ring = {"moving": None, "active": []}

    def do_ring(t):
        active = ring["active"]
        ins = [along_narrow(ring["moving"], 1)] if active else []
        ins += [parts[0] for _, parts in active]
        feats = [] if t is None else [flight[t][0].shape[0]]
        ins += [] if t is None else flight[t]
        going = sum(parts[0].shape[0] for _, parts in active if len(parts) > 1) + sum(v + 3 for v in feats)
        ended = [(k, parts[0].shape[0]) for k, parts in active if len(parts) == 1]
        outs = ([flat(going)] if going else []) + [flat(many) for _, many in ended]
        outs += [flat(v + 3) for v in feats for _ in range(3)]
        sizes = [(parts[0].shape[0], len(parts) == 1) for _, parts in active]
        v = yield functools.partial(ring_kernel, sizes, feats), ins, outs
        ring["moving"] = v.pop(0) if going else None
        flight.update((k, [v.pop(0)]) for k, _ in ended)
        ring["active"] = [(k, parts[1:]) for k, parts in active if len(parts) > 1]
        ring["active"] += [] if t is None else [(t, v)]

    def do_stack(g):
        ins = [flight[t][0] for t in GROUPS[g]]
        state = 3 * len(GROUPS[g])
        feats = sum(v.shape[0] for v in ins) - state
        v = yield stack_kernel, ins, [flat(feats), flat(state)]
        result[g] = [v[0], along_dp(v[0], 2), v[1], along_dp(v[1], 1)]

    def do_add(g):
        v = yield add_kernel, result[g], [flat(result[g][0].shape[0]), flat(result[g][2].shape[0])]
        result[g] = [v[0], along_dp(v[0], 1), v[1], along_dp(v[1], 2)]

    def do_local(_):
        ins = (raw, cat, dh, dn, norm, counts, grad_w2, grad_b, *small)
        outs = [("v", (at["rows"], feat), F32)]
        result["pack"] = run(
            functools.partial(sums_kernel, VOCAB, 256, at), ins, outs, "local_sums", limit=16, work=WORK
        )[0]
        result["steps"] = 0

    def do_total(_):
        pack = result["pack"]
        axis, way = STEPS[result["steps"]]
        result["steps"] += 1
        (result["pack"],) = yield add_kernel, [pack, lax.ppermute(pack, axis, way)], [("v", pack.shape, F32)]

    def do_blocks(g):
        nonlocal turn
        sectioned = [order[t] for t in GROUPS[g]]
        before = result.get("blocks")
        *v, turn = blocks(turn, sectioned, result[g], sections, 1 if g == 0 else 0, before)
        result["blocks"] = v[:2]
        if g == 0:
            result["last"] = [v[2]] + [along_narrow(v[2], hop) for hop in (1, 2, 3)]

    def do_head_rows(_):
        result["last"] = run(head_rows_kernel, result["last"], [("p", (feat, half), F32)], "head_rows")[0]

    def do_finish(_):
        nonlocal turn
        *result["finish"], turn = call(
            functools.partial(finish_kernel, VOCAB, count, at),
            turn,
            [("v", v) for v in (dh, dn, raw, norm, result["pack"], table)] + [("s", cardinality)],
            [
                ("p", (rows, num), F32),
                ("p", (emb, table.shape[1]), F32),
                ("p", (1, feat), F32),
                ("p", (1, feat), F32),
                ("p", mask_logit.shape, F32),
                ("p", gate_bias.shape, F32),
                ("p", (1, half), F32),
                ("p", (classes, half), F32),
                ("p", (1, classes), F32),
            ],
            "finish",
            limit=16,
            work=WORK,
        )

    tasks = {"B": do_backward, "p": do_fetch, "G": do_other, "g": do_mine, "L": do_local}
    if fast:
        tasks.update(X=do_blocks, Y=do_head_rows, Z=do_finish)
    steps = dict(F=do_fold, R=do_ring, S=do_stack, A=do_add, T=do_total)
    for step in BACK:
        if step[0] in tasks:
            tasks[step[0]](int(step[1:] or 0))
        elif fast and step[0] in steps:
            jobs = [steps[v[0]](int(v[1:]) if v[1:] else None) for v in step.rstrip("~").split("+")]
            together(jobs, not step.endswith("~"))
    if fast:
        grad_feat, grad_state = result["blocks"]
        grad_w1 = result["last"]
    else:
        halves = ([None] * sections, [None] * sections)
        for t in range(sections):
            local = jnp.concatenate(flight[t], axis=3).reshape(6, feat, feat)
            for a in range(2):
                part = lax.psum_scatter(local[3 * a : 3 * a + 3], "wide", scatter_dimension=2, tiled=True)
                part = lax.psum_scatter(part, "narrow", scatter_dimension=1, tiled=True)
                halves[a][order[t]] = lax.psum(part, "dp").astype(F32)
        result["pack"] = lax.psum(result["pack"], axes)
        do_finish(0)
        grad_feat, grad_state = (jnp.stack(v) for v in halves)
        grad_w1 = lax.psum(grad_w1.reshape(feat, -1).astype(F32), axes)
    grad_numeric, grad_table, plain, scaled, grad_mask, grad_bias, grad_b1, grad_w2, grad_b2 = result["finish"]
    return (
        logits.T,
        grad_numeric,
        grad_table.T,
        scaled.reshape(-1),
        plain.reshape(-1),
        grad_mask,
        grad_feat,
        grad_state,
        grad_bias,
        grad_w1,
        grad_b1.reshape(-1),
        grad_w2.T,
        grad_b2.reshape(-1),
    )


def solution(mesh):
    spread_rows = P(("dp", "wide", "narrow"), None)
    blocked = P(None, None, "narrow", "wide")
    in_specs = (spread_rows, spread_rows) + (P(),) * 5 + (blocked, blocked) + (P(),) * 5 + (spread_rows,)
    out_specs = (spread_rows, spread_rows) + (P(),) * 4 + (blocked, blocked) + (P(),) * 5
    return jax.shard_map(body, mesh=mesh, in_specs=in_specs, out_specs=out_specs, check_vma=False)
```
